128 devices in a mesh: rep: 8 (over x_hi, z), shard: 16 (over y, x_lo, core).
Axes of the slice: x: 4 (x_hi: 2, x_lo: 2; x = x_hi * 2 + x_lo), y: 4, z: 4, core: 2. Of those that a mesh axis runs over, the one named last changes fastest.
Arguments:
- tokens: bfloat16 [16384, 1536], P(('rep', 'shard')), may hold values from -6 to 6
- cotangent: bfloat16 [16384, 1536], P(('rep', 'shard')), may hold values from -6 to 6
- seq_lengths: int32 [8, 32], P('rep'), may hold values from 16 to 112, as said below
- seq_order: int32 [8, 32], P('rep'), may hold values from 0 to 31, as said below
- routes: int32 [16384, 4], P(('rep', 'shard')), may hold values from 0 to 7, all different within a row; in each aligned block of 128 rows (0 to 127, 128 to 255, ...) at most 80 rows name the same one
- gate_weights: float32 [16384, 4], P(('rep', 'shard')), may hold values from 0.1 to 0.5
- attn_gain: bfloat16 [1536], P('shard'), may hold values from 0.5 to 1.5
- w_query: bfloat16 [1536, 1536], P('shard'), may hold values from -0.15625 to 0.15625
- key_value_weight: bfloat16 [1536, 512], P('shard'), may hold values from -0.15625 to 0.15625
- w_out: bfloat16 [1536, 1536], P('shard'), may hold values from -1.25 to 1.25
- ffn_gain: bfloat16 [1536], P('shard'), may hold values from 0.5 to 1.5
- w_gateup: bfloat16 [8, 1536, 1536], P(None, 'shard'), may hold values from -0.15625 to 0.15625
- w_down: bfloat16 [8, 768, 1536], P(None, 'shard'), may hold values from -0.21875 to 0.21875
Outputs:
- output: bfloat16 [16384, 1536], P(('rep', 'shard'))
- grad_tokens: bfloat16 [16384, 1536], P(('rep', 'shard'))
- grad_attn_gain: float32 [1536], P('shard')
- grad_query: float32 [1536, 1536], P('shard')
- grad_keyval: float32 [1536, 512], P('shard')
- grad_out: float32 [1536, 1536], P('shard')
- grad_ffn_gain: float32 [1536], P('shard')
- grad_gateup: float32 [8, 1536, 1536], P(None, 'shard')
- grad_down: float32 [8, 768, 1536], P(None, 'shard')
The draws below stay inside these ranges and needn't reach their ends.
Inputs may be any that keep to these rules, and one draw needn't show every extreme that they name: `seq_lengths`: each group's sequences come in pairs that seq_order places on one device, and each pair's lengths sum to 128. `seq_order`: each row is a permutation; entries 2j and 2j + 1 of row g name the two sequences of device j of group g. `routes`: each row names 4 different experts; among the rows of one device no expert is named more than 80 times.
All inputs are finite; a program needn't handle non-finite values.
Results may differ from the reference program's by a relative error of at most 0.024.
Values may be sent and summed in bfloat16 or wider, within the bound.
No kernel may reach another device: no remote copies, remote signals or barrier semaphores. Data moves between devices by JAX's collectives and lax.ppermute only.
A program may use at most 192 MiB of HBM per device.

```python
import math
import jax
import jax.numpy as jnp
import numpy as np
from jax import lax

MODEL_WIDTH = 1536
QUERY_HEADS = 12
KEY_VALUE_HEADS = 2
HEAD_SIZE = 128
FF = 768
TOP = 4
EXPERTS = 8
DEVICE_TOKENS = 128
CAP = 80
MIN_LEN = 16
TOKENS = 16384
N_REP = 8
N_SHARD = 16


def deal_sequences(key):
    key = jax.random.fold_in(key, 11)
    first = jax.random.randint(key, (N_REP, N_SHARD), MIN_LEN, DEVICE_TOKENS - MIN_LEN + 1)
    first = first.at[:, 0].set(MIN_LEN)
    slot_length = jnp.stack([first, DEVICE_TOKENS - first], axis=2).reshape(N_REP, 2 * N_SHARD)
    order_keys = jax.random.split(jax.random.fold_in(key, 5), N_REP)
    placed = jax.vmap(jax.random.permutation, in_axes=(0, None))(order_keys, 2 * N_SHARD).astype(jnp.int32)
    group_ids = jnp.arange(N_REP, dtype=jnp.int32)[:, None]
    lengths = jnp.zeros((N_REP, 2 * N_SHARD), jnp.int32).at[group_ids, placed].set(slot_length.astype(jnp.int32))
    return (lengths.astype(jnp.int32), placed)


def draw_seq_lengths(key, part):
    lengths, placed = deal_sequences(key)
    return lengths


def draw_seq_order(key, part):
    lengths, placed = deal_sequences(key)
    return placed


def levels(stream_key, extent, cuts, low, high):
    def one(axis_at, blocks):
        heights = jax.random.uniform(jax.random.fold_in(jax.random.fold_in(stream_key, 6), axis_at), (blocks,), jnp.float32, low / len(cuts), high / len(cuts))
        return jnp.repeat(jnp.exp(heights), extent[axis_at] // blocks).reshape((-1,) + (1,) * (len(extent) - axis_at - 1))

    factor_of = one(*cuts[0])
    for cut in cuts[1:]:
        factor_of = factor_of * one(*cut)
    return factor_of


def routed_block(own_key, own, number, rows, amount, top, limit, slope):
    ranking = jax.random.permutation(own_key, amount)
    heavy_load, ordinary = shares(amount, rows * top, limit, slope, True), shares(amount, rows * top, limit, slope, False)
    places = jnp.arange(amount)

    def named(sizes, offset_by):
        used = int((sizes > 0).sum())
        fixed = max(1, used // 4)
        passed = fixed + (places - fixed + offset_by * (used - fixed)) % max(1, amount - fixed)
        return jnp.zeros((amount,), jnp.int32).at[ranking[jnp.where(places < fixed, places, passed)]].set(jnp.asarray(sizes, jnp.int32))

    sizes = jnp.where(number % 4 == 0, named(heavy_load, number // 4), named(ordinary, number - number // 4 - 1))
    mixed = jax.random.permutation(jax.random.fold_in(own, 3), amount)
    giver, sink = mixed[0:amount // 2 * 2:2], mixed[1:amount // 2 * 2:2]
    room = jnp.minimum(sizes[giver] - 1, limit - sizes[sink]) // 2
    room = jnp.where((giver == ranking[0]) | (sink == ranking[0]) | (sizes[sink] == 0), 0, jnp.maximum(room, 0))
    passed = jax.random.randint(jax.random.fold_in(own, 4), (amount // 2,), 0, 1 << 20) % (room + 1)
    sizes = sizes.at[giver].add(-passed).at[sink].add(passed)
    members = jnp.searchsorted(jnp.cumsum(sizes), jnp.arange(rows * top), side="right").astype(jnp.int32)
    table = members.reshape(top, rows).T
    table = table[jax.random.permutation(jax.random.fold_in(own, 1), rows)]
    offset_by = jax.random.randint(jax.random.fold_in(own, 2), (rows, 1), 0, top)
    return jnp.take_along_axis(table, (jnp.arange(top)[None, :] + offset_by) % top, axis=1)


def shares(number_of, total, bound, slope, full):
    weights = [(1 << 20) // math.isqrt(standing ** slope) + 1 for standing in range(1, number_of + 1)]
    largest = bound if full else min(bound, max(-(-total // number_of), total * weights[0] // sum(weights)))
    least = 1 if total - largest >= number_of - 1 else 0
    counts, spare = [largest] + [least] * (number_of - 1), total - largest - least * (number_of - 1)
    while spare > 0:
        candidates = [i for i in range(1, number_of) if counts[i] < largest] or [i for i in range(1, number_of) if counts[i] < bound]
        pool, left = sum([weights[i] for i in candidates]), spare
        for i in candidates:
            more = min(bound - counts[i], max(1, left * weights[i] // pool), spare)
            counts[i] = counts[i] + more
            spare = spare - more
    return np.array(counts)


def bell_draw(stream_key, extent, spread, bound, shards=(), kind=jnp.bfloat16):
    loudness = levels(stream_key, extent, shards, -0.22, 0.18) if shards else 1.0
    drawn = jax.random.normal(stream_key, extent, jnp.float32) * spread * loudness
    return jnp.minimum(jnp.maximum(drawn, -bound), bound).astype(kind)


def setup_inputs(seed: int = 0) -> dict:
    seeds = jax.random.split(jax.random.key(seed), 14)
    tokens = bell_draw(seeds[0], (TOKENS, MODEL_WIDTH), 1.0, 6.0, ((0, 128),))
    cotangent = bell_draw(seeds[1], (TOKENS, MODEL_WIDTH), 1.0, 6.0, ((0, 128),))
    seq_lengths = draw_seq_lengths(jax.random.fold_in(seeds[13], 71), 0)
    seq_order = draw_seq_order(jax.random.fold_in(seeds[13], 71), 0)
    routes_keys = jax.random.split(jax.random.fold_in(seeds[4], 1), TOKENS // DEVICE_TOKENS)
    routes_turns = jax.random.permutation(jax.random.fold_in(seeds[4], 3), TOKENS // DEVICE_TOKENS)
    routes = jax.vmap(lambda own, number: routed_block(jax.random.fold_in(seeds[4], 2), own, number, DEVICE_TOKENS, EXPERTS, TOP, CAP, 1))(routes_keys, routes_turns).reshape((TOKENS, TOP))
    gate_weights = jnp.clip(jnp.exp(math.log(0.5) - 1.609438 * jax.random.uniform(seeds[5], (TOKENS, TOP), jnp.float32) ** levels(seeds[5], (TOKENS, TOP), ((0, 128),), -0.2, 0.2)), 0.1, 0.5)
    attn_gain = jnp.clip(1.0 + 0.1 * jax.random.normal(seeds[6], (MODEL_WIDTH,), jnp.float32), 0.5, 1.5).astype(jnp.bfloat16)
    w_query = bell_draw(seeds[7], (MODEL_WIDTH, QUERY_HEADS * HEAD_SIZE), MODEL_WIDTH ** -0.5, 0.15625, ((0, 16),))
    key_value_weight = bell_draw(seeds[8], (MODEL_WIDTH, 2 * KEY_VALUE_HEADS * HEAD_SIZE), MODEL_WIDTH ** -0.5, 0.15625, ((0, 16),))
    w_out = bell_draw(seeds[9], (QUERY_HEADS * HEAD_SIZE, MODEL_WIDTH), (QUERY_HEADS * HEAD_SIZE // 64) ** -0.5, 1.25, ((0, 16),))
    ffn_gain = jnp.clip(1.0 + 0.1 * jax.random.normal(seeds[10], (MODEL_WIDTH,), jnp.float32), 0.5, 1.5).astype(jnp.bfloat16)
    w_gateup = bell_draw(seeds[11], (EXPERTS, MODEL_WIDTH, 2 * FF), MODEL_WIDTH ** -0.5, 0.15625, ((1, 16),))
    w_down = bell_draw(seeds[12], (EXPERTS, FF, MODEL_WIDTH), FF ** -0.5, 0.21875, ((1, 16),))
    return {"tokens": tokens, "cotangent": cotangent, "seq_lengths": seq_lengths, "seq_order": seq_order, "routes": routes, "gate_weights": gate_weights, "attn_gain": attn_gain, "w_query": w_query, "key_value_weight": key_value_weight, "w_out": w_out, "ffn_gain": ffn_gain, "w_gateup": w_gateup, "w_down": w_down}


epsilon = 1e-06
rope_base = 10000.0

@jax.custom_vjp
def lower_bound(v):
    return lax.optimization_barrier(v.astype(jnp.bfloat16)).astype(jnp.float32)

@jax.custom_vjp
def low_back(v):
    return v

def low_keep(v):
    return (lower_bound(v), None)

def low_pass(kept, grad):
    return (grad,)

def back_keep(v):
    return (v, None)

def back_low(kept, grad):
    return (lower_bound(grad),)
lower_bound.defvjp(low_keep, low_pass)
low_back.defvjp(back_keep, back_low)

def precise_dot(left, right):
    return jnp.dot(left, right, precision=lax.Precision.HIGHEST)

def sequence_layout(lengths, placed, device_slots, rows_each):
    starts = (jnp.cumsum(lengths) - lengths).astype(jnp.int32)
    first_index = placed[2 * device_slots]
    second_index = placed[2 * device_slots + 1]
    first_length = lengths[first_index]
    offsets = jnp.arange(rows_each, dtype=jnp.int32)[None, :]
    in_first = offsets < first_length[:, None]
    sequence = jnp.where(in_first, first_index[:, None], second_index[:, None])
    token_position = jnp.where(in_first, offsets, offsets - first_length[:, None])
    source = starts[sequence] + token_position
    segment = jnp.where(in_first, 0, 1)
    return (source.astype(jnp.int32), token_position.astype(jnp.int32), segment.astype(jnp.int32))

def slot_table(routes, gate_weights, experts, capacity):
    block_list = routes.shape[0]
    rows_each = routes.shape[1]
    expert_ids = jnp.arange(experts, dtype=jnp.int32)
    chosen = routes[..., None] == expert_ids
    member = jnp.any(chosen, axis=2).astype(jnp.int32)
    weight = lax.optimization_barrier(jnp.sum(jnp.where(chosen, gate_weights[..., None], 0.0), axis=2))
    place = jnp.cumsum(member, axis=1) - 1
    target = jnp.transpose(jnp.where(member > 0, place, capacity), (0, 2, 1)).astype(jnp.int32)
    block_ids = jnp.arange(block_list, dtype=jnp.int32)[:, None, None]
    token_ids = jnp.broadcast_to(jnp.arange(rows_each, dtype=jnp.int32)[None, None, :], target.shape)
    table = jnp.zeros((block_list, experts, capacity + 1), jnp.int32)
    table = table.at[block_ids, expert_ids[None, :, None], target].set(token_ids)[:, :, :capacity]
    count = lax.optimization_barrier(jnp.sum(member, axis=1))
    filled = jnp.arange(capacity, dtype=jnp.int32)[None, None, :] < count[:, :, None]
    table = jnp.where(filled, table, 0).astype(jnp.int32)
    slot_weight = jnp.take_along_axis(jnp.transpose(weight, (0, 2, 1)), table, axis=2)
    slot_weight = jnp.where(filled, slot_weight, 0.0)
    return (table, slot_weight)

def rotary_embed(values, token_position, direction):
    half_width = values.shape[-1] // 2
    frequency = rope_base ** (-jnp.arange(half_width, dtype=jnp.float32) / half_width)
    angle = token_position.astype(jnp.float32)[:, None] * frequency[None, :]
    cosine = jnp.cos(angle)[:, None, :]
    sine_turn = direction * jnp.sin(angle)[:, None, :]
    first = values[..., :half_width]
    second = values[..., half_width:]
    return jnp.concatenate([first * cosine - second * sine_turn, second * cosine + first * sine_turn], axis=-1)

def rms_norm(values, gain_row):
    return values * lax.rsqrt(lax.optimization_barrier(jnp.mean(values * values, axis=-1, keepdims=True)) + epsilon) * gain_row

def attend_heads(block):
    query_matrix, key_matrix, value_matrix, segment = block
    count_of_rows = query_matrix.shape[0]
    grouped_heads = query_matrix.reshape(count_of_rows, KEY_VALUE_HEADS, QUERY_HEADS // KEY_VALUE_HEADS, HEAD_SIZE)
    raw_scores = low_back(jnp.einsum('sgrd,tgd->grst', grouped_heads, key_matrix, precision=lax.Precision.HIGHEST))
    row_index = jnp.arange(count_of_rows)
    allowed = (row_index[None, :] <= row_index[:, None]) & (segment[None, :] == segment[:, None])
    scores = jnp.where(allowed, raw_scores * HEAD_SIZE ** (-0.5), -1000000000.0)
    highest = lax.optimization_barrier(jnp.max(scores, axis=-1, keepdims=True))
    exp_scores = jnp.exp(scores - highest)
    prob_low = lower_bound(exp_scores / lax.optimization_barrier(jnp.sum(exp_scores, axis=-1, keepdims=True)))
    mixed = jnp.einsum('grst,tgd->sgrd', prob_low, value_matrix, precision=lax.Precision.HIGHEST)
    return lower_bound(low_back(mixed)).reshape(count_of_rows, QUERY_HEADS * HEAD_SIZE)

def reference(tokens, cotangent, seq_lengths, seq_order, routes, gate_weights, attn_gain, w_query, key_value_weight, w_out, ffn_gain, w_gateup, w_down):
    block_list = N_REP * N_SHARD
    group_rows = DEVICE_TOKENS * N_SHARD
    overall_row_count = block_list * DEVICE_TOKENS
    device_slots = jnp.arange(N_SHARD, dtype=jnp.int32)
    sources = []
    positions = []
    segments = []
    for group_id in range(N_REP):
        source, token_position, segment = sequence_layout(seq_lengths[group_id], seq_order[group_id], device_slots, DEVICE_TOKENS)
        sources.append(source.reshape(-1) + group_id * group_rows)
        positions.append(token_position.reshape(-1))
        segments.append(segment.reshape(-1))
    source_all = jnp.concatenate(sources).astype(jnp.int32)
    gathered_positions = jnp.concatenate(positions).astype(jnp.int32)
    gathered_segments = jnp.concatenate(segments).astype(jnp.int32)
    inverse_all = jnp.zeros((overall_row_count,), jnp.int32).at[source_all].set(jnp.arange(overall_row_count, dtype=jnp.int32))
    table, slot_weight = slot_table(routes.reshape(block_list, DEVICE_TOKENS, TOP), gate_weights.reshape(block_list, DEVICE_TOKENS, TOP), EXPERTS, CAP)
    table = table + (jnp.arange(block_list, dtype=jnp.int32) * DEVICE_TOKENS)[:, None, None]
    slot_rows = jnp.transpose(table, (1, 0, 2)).reshape(EXPERTS, block_list * CAP).astype(jnp.int32)
    slot_scale = jnp.transpose(slot_weight, (1, 0, 2)).reshape(EXPERTS, block_list * CAP)
    key_value_width = KEY_VALUE_HEADS * HEAD_SIZE

    def forward(wide_tokens, gain_attn, query_w, keyval_w, output_w, gain_ffn, gateup_w, down_w):
        dealt_rows = low_back(wide_tokens[source_all])
        normed = lower_bound(rms_norm(dealt_rows, gain_attn))
        query_pre = low_back(precise_dot(normed, query_w))
        key_value_projected = low_back(precise_dot(normed, keyval_w))
        query_matrix = lower_bound(rotary_embed(query_pre.reshape(overall_row_count, QUERY_HEADS, HEAD_SIZE), gathered_positions, 1.0))
        key_matrix = lower_bound(rotary_embed(key_value_projected[:, :key_value_width].reshape(overall_row_count, KEY_VALUE_HEADS, HEAD_SIZE), gathered_positions, 1.0))
        value_matrix = lower_bound(key_value_projected[:, key_value_width:].reshape(overall_row_count, KEY_VALUE_HEADS, HEAD_SIZE))
        attention_output = lax.map(jax.checkpoint(attend_heads), (query_matrix.reshape(block_list, DEVICE_TOKENS, QUERY_HEADS, HEAD_SIZE), key_matrix.reshape(block_list, DEVICE_TOKENS, KEY_VALUE_HEADS, HEAD_SIZE), value_matrix.reshape(block_list, DEVICE_TOKENS, KEY_VALUE_HEADS, HEAD_SIZE), gathered_segments.reshape(block_list, DEVICE_TOKENS)))
        attention_output = attention_output.reshape(overall_row_count, QUERY_HEADS * HEAD_SIZE)
        branch = lower_bound(precise_dot(attention_output, output_w))
        residual = wide_tokens + low_back(branch[inverse_all])
        normed_ffn = lower_bound(rms_norm(residual, gain_ffn))

        def expert_step(carried, inputs):
            gateup_one, down_one, pick_rows, pick_weight = inputs
            picked = normed_ffn[pick_rows]
            pre_act = low_back(precise_dot(picked, gateup_one))
            acted = lower_bound(jax.nn.silu(pre_act[:, :FF]) * pre_act[:, FF:])
            result = low_back(precise_dot(acted, down_one))
            return (carried, result * pick_weight[:, None])
        carried, weighted_out = lax.scan(jax.checkpoint(expert_step), jnp.zeros((), jnp.float32), (gateup_w, down_w, slot_rows, slot_scale))
        mixture = jnp.zeros_like(residual).at[slot_rows.reshape(-1)].add(weighted_out.reshape(-1, MODEL_WIDTH))
        return residual + mixture
    wide_args = (tokens.astype(jnp.float32), attn_gain.astype(jnp.float32), w_query.astype(jnp.float32), key_value_weight.astype(jnp.float32), w_out.astype(jnp.float32), ffn_gain.astype(jnp.float32), w_gateup.astype(jnp.float32), w_down.astype(jnp.float32))
    result, pullback = jax.vjp(forward, *wide_args)
    grads = pullback(cotangent.astype(jnp.float32))
    return (result.astype(jnp.bfloat16), grads[0].astype(jnp.bfloat16), grads[1], grads[2], grads[3], grads[4], grads[5], grads[6], grads[7])
```

```python
import jax
import jax.numpy as jnp
from jax import lax
from jax.sharding import Mesh, PartitionSpec as P

QUERY_HEADS = 12
KEY_VALUE_HEADS = 2
GROUP = QUERY_HEADS // KEY_VALUE_HEADS
HEAD_SIZE = 128
CAP = 80

EPSILON = 1e-06
ROPE_BASE = 10000.0
SHARD = ("y", "x", "c")
CHIPS = ("y", "x")
SWAP = [(0, 1), (1, 0)]

bf16 = jnp.bfloat16
f32 = jnp.float32


def exchange(parts, axes):
    return lax.all_to_all(parts, axes, 0, 0, tiled=True)


def matmul(left, right):
    return jnp.dot(left, right, preferred_element_type=f32)


def dot_general(left, right, dims):
    return lax.dot_general(left, right, (dims, ((), ())), preferred_element_type=f32)


def in_core_order(core, mine, other):
    return jnp.where(core == 0, jnp.stack([mine, other], 1), jnp.stack([other, mine], 1))


def rotary_tables(position):
    half = HEAD_SIZE // 2
    frequency = ROPE_BASE ** (-jnp.arange(half, dtype=f32) / half)
    angle = position.astype(f32)[:, None] * frequency[None, :]
    return jnp.cos(angle)[:, None, :], jnp.sin(angle)[:, None, :]


def rotate(values, cosine, sine):
    half = values.shape[-1] // 2
    first, second = values[..., :half], values[..., half:]
    return jnp.concatenate(
        [first * cosine - second * sine, second * cosine + first * sine], axis=-1
    )


def norm_back(values, factor, gain_row, upstream):
    grad_normed = upstream * gain_row
    grad_gain = jnp.sum(upstream * values * factor, axis=0)
    cubed = factor * factor * factor
    grad_input = factor * grad_normed - values * cubed * jnp.mean(
        grad_normed * values, axis=-1, keepdims=True
    )
    return grad_input, grad_gain


def cut(rows, ways):
    *lead, a, b = rows.shape
    wide = ways // 2
    n = len(lead)
    cut_up = rows.reshape(*lead, 2, a // 2, wide, b // wide)
    order = (n, n + 2, *range(n), n + 1, n + 3)
    return cut_up.transpose(order).reshape(ways, *lead, a // 2, b // wide)


def uncut(pieces, ways):
    _, *lead, a, b = pieces.shape
    wide = ways // 2
    n = len(lead)
    whole = pieces.reshape(2, wide, *lead, a, b)
    order = (*range(2, 2 + n), 0, 2 + n, 1, 3 + n)
    return whole.transpose(order).reshape(*lead, 2 * a, wide * b)


def spread(part, ways, axes):
    return exchange(jnp.broadcast_to(part[None], (ways, *part.shape)), axes)


def per_device(
    tokens,
    cotangent,
    seq_lengths,
    seq_order,
    routes,
    gate_weights,
    attn_gain,
    w_query,
    key_value_weight,
    w_out,
    ffn_gain,
    w_gateup,
    w_down,
):
    reps = lax.axis_size("rep")
    shards = lax.axis_size("y") * lax.axis_size("x") * lax.axis_size("c")
    core = lax.axis_index("c")
    shard = (lax.axis_index("y") * lax.axis_size("x") + lax.axis_index("x")) * 2 + core
    rows, width = tokens.shape
    experts = w_gateup.shape[0]
    ff = w_gateup.shape[2] // 2
    kv_width = KEY_VALUE_HEADS * HEAD_SIZE
    scale = HEAD_SIZE ** (-0.5)

    gains = spread(jnp.stack([attn_gain, ffn_gain]), shards, SHARD)
    gains = gains.transpose(1, 0, 2).reshape(2, width).astype(f32)
    gain_attn, gain_ffn = gains[0], gains[1]
    qkv_full = lax.all_gather(
        jnp.concatenate([w_query, key_value_weight], 1), SHARD, axis=0, tiled=True
    )
    out_full = lax.all_gather(w_out, SHARD, axis=0, tiled=True)
    gateup_mine = exchange(w_gateup, CHIPS)
    down_mine = exchange(w_down, CHIPS)
    gateup_full = in_core_order(core, gateup_mine, lax.ppermute(gateup_mine, "c", SWAP))
    gateup_full = gateup_full.reshape(width, 2 * ff)
    down_full = in_core_order(core, down_mine, lax.ppermute(down_mine, "c", SWAP))
    down_full = down_full.reshape(ff, width)

    chosen = routes[:, :, None] == jnp.arange(experts, dtype=jnp.int32)
    member = jnp.any(chosen, axis=1)
    weight = jnp.sum(jnp.where(chosen, gate_weights[:, :, None], 0.0), axis=1)
    place = jnp.cumsum(member.astype(jnp.int32), axis=0) - 1
    slot = jnp.where(member, place, -1).T
    picks = slot[:, None, :] == jnp.arange(CAP, dtype=jnp.int32)[None, :, None]
    pick = picks.astype(bf16).reshape(experts * CAP, rows)
    slot_weight = jnp.sum(jnp.where(picks, weight.T[:, None, :], 0.0), axis=2)
    upstream = cotangent.astype(f32)
    grad_out_sent = matmul(pick, cotangent) * slot_weight.reshape(-1, 1)
    grad_out = exchange(grad_out_sent.astype(bf16), CHIPS)

    lengths = seq_lengths[0]
    starts = jnp.cumsum(lengths) - lengths
    row_at = shard * rows + jnp.arange(rows, dtype=jnp.int32)
    first_at = jnp.max(jnp.where(starts[None, :] <= row_at[:, None], starts[None, :], 0), axis=1)
    cosine, sine = rotary_tables(row_at - first_at)
    key_at = (shard - 1) * rows + jnp.arange(2 * rows, dtype=jnp.int32)
    allowed = (key_at[None, :] <= row_at[:, None]) & (key_at[None, :] >= first_at[:, None])

    wide = tokens.astype(f32)
    attn_factor = lax.rsqrt(jnp.mean(wide * wide, axis=-1, keepdims=True) + EPSILON)
    normed = (wide * attn_factor * gain_attn).astype(bf16)
    normed_all = lax.all_gather(normed, SHARD, axis=0, tiled=True)
    qkv = matmul(normed, qkv_full)
    turned = rotate(
        qkv[:, : width + kv_width].reshape(rows, QUERY_HEADS + KEY_VALUE_HEADS, HEAD_SIZE),
        cosine,
        sine,
    ).astype(bf16)
    queries = turned[:, :QUERY_HEADS].reshape(rows, KEY_VALUE_HEADS, GROUP, HEAD_SIZE)
    keyval = jnp.concatenate(
        [turned[:, QUERY_HEADS:].reshape(rows, kv_width), qkv[:, width + kv_width :].astype(bf16)],
        axis=1,
    )
    ring = [(i, (i + 1) % shards) for i in range(shards)]
    back_ring = [((i + 1) % shards, i) for i in range(shards)]
    keyval = jnp.concatenate([lax.ppermute(keyval, SHARD, ring), keyval], axis=0)
    keys = keyval[:, :kv_width].reshape(2 * rows, KEY_VALUE_HEADS, HEAD_SIZE)
    values = keyval[:, kv_width:].reshape(2 * rows, KEY_VALUE_HEADS, HEAD_SIZE)
    raw = jnp.einsum("sgrd,tgd->grst", queries, keys, preferred_element_type=f32)
    scores = jnp.where(allowed, raw * scale, -1000000000.0)
    exp_scores = jnp.exp(scores - jnp.max(scores, axis=-1, keepdims=True))
    probs = exp_scores / jnp.sum(exp_scores, axis=-1, keepdims=True)
    prob_low = probs.astype(bf16)
    mixed = jnp.einsum("grst,tgd->sgrd", prob_low, values, preferred_element_type=f32)
    attended = mixed.reshape(rows, width).astype(bf16)
    branch = matmul(attended, out_full).astype(bf16)
    residual = wide + branch.astype(f32)
    ffn_factor = lax.rsqrt(jnp.mean(residual * residual, axis=-1, keepdims=True) + EPSILON)
    normed_ffn = (residual * ffn_factor * gain_ffn).astype(bf16)
    attended_cols = exchange(attended.T, SHARD).reshape(shards, width // shards, rows)

    picked = exchange(matmul(pick, normed_ffn).astype(bf16), CHIPS)
    pre = matmul(picked, gateup_full)
    gate, up = pre[:, :ff], pre[:, ff:]
    sigmoid = jax.nn.sigmoid(gate)
    silu = gate * sigmoid
    acted = (silu * up).astype(bf16)
    expert_out = exchange(matmul(acted, down_full).astype(bf16), CHIPS)
    grad_act = dot_general(grad_out, down_full, ((1,), (1,)))
    grad_gate = grad_act * up * sigmoid * (1.0 + gate * (1.0 - sigmoid))
    grad_pre = jnp.concatenate([grad_gate, grad_act * silu], axis=1).astype(bf16)
    grad_picked = dot_general(grad_pre, gateup_full, ((1,), (1,)))
    grad_picked = exchange(grad_picked.astype(bf16), CHIPS)
    grad_down = dot_general(acted, grad_out, ((0,), (0,)))
    grad_gateup = dot_general(picked, grad_pre, ((0,), (0,)))

    def owned(grad):
        halves = grad.reshape(experts, 2, -1, width)
        here = jnp.where(core == 0, halves[:, 0], halves[:, 1])
        there = jnp.where(core == 0, halves[:, 1], halves[:, 0])
        return here + lax.ppermute(there.astype(bf16), "c", SWAP).astype(f32)

    both = jnp.concatenate([owned(grad_gateup), owned(grad_down)], axis=1).astype(bf16)
    over_rep = exchange(cut(both, reps), "rep").astype(f32).sum(axis=0).astype(bf16)
    expert_grads = uncut(spread(exchange(over_rep, CHIPS), reps, "rep"), reps).astype(f32)
    shard_gateup = expert_grads[:, : width // shards]
    shard_down = expert_grads[:, width // shards :]

    back = pick.astype(f32) * slot_weight.reshape(-1, 1)
    back_high = back.astype(bf16)
    back_low = (back - back_high.astype(f32)).astype(bf16)
    mixture = dot_general(back_high, expert_out, ((0,), (0,)))
    mixture = mixture + dot_general(back_low, expert_out, ((0,), (0,)))
    output = (residual + mixture).astype(bf16)
    grad_ffn_in = dot_general(pick, grad_picked, ((0,), (0,)))
    grad_from_norm, grad_gain_ffn = norm_back(residual, ffn_factor, gain_ffn, grad_ffn_in)
    grad_residual = upstream + grad_from_norm
    grad_branch = grad_residual.astype(bf16)
    grad_branch_all = lax.all_gather(grad_branch, SHARD, axis=0, tiled=True)

    grad_attended = dot_general(grad_branch, out_full, ((1,), (1,))).astype(bf16)
    grad_attended = grad_attended.reshape(rows, KEY_VALUE_HEADS, GROUP, HEAD_SIZE)
    grad_probs = jnp.einsum("sgrd,tgd->grst", grad_attended, values, preferred_element_type=f32)
    grad_values = jnp.einsum("grst,sgrd->tgd", prob_low, grad_attended, preferred_element_type=f32)
    inner = jnp.sum(probs * grad_probs, axis=-1, keepdims=True)
    grad_raw = (probs * (grad_probs - inner) * scale).astype(bf16)
    grad_queries = jnp.einsum("grst,tgd->sgrd", grad_raw, keys, preferred_element_type=f32)
    grad_keys = jnp.einsum("grst,sgrd->tgd", grad_raw, queries, preferred_element_type=f32)
    grad_keyval = jnp.concatenate(
        [grad_keys.reshape(2 * rows, kv_width), grad_values.reshape(2 * rows, kv_width)], axis=1
    )
    from_next = lax.ppermute(grad_keyval[:rows].astype(bf16), SHARD, back_ring)
    grad_keyval = grad_keyval[rows:] + from_next.astype(f32)
    grad_turned = jnp.concatenate(
        [grad_queries.reshape(rows, width), grad_keyval[:, :kv_width]], axis=1
    )
    grad_turned = grad_turned.reshape(rows, QUERY_HEADS + KEY_VALUE_HEADS, HEAD_SIZE)
    grad_qkv = jnp.concatenate(
        [
            rotate(grad_turned, cosine, -sine).reshape(rows, width + kv_width),
            grad_keyval[:, kv_width:],
        ],
        axis=1,
    ).astype(bf16)
    grad_normed = dot_general(grad_qkv, qkv_full, ((1,), (1,)))
    grad_in, grad_gain_attn = norm_back(wide, attn_factor, gain_attn, grad_normed)
    grad_tokens = (grad_residual + grad_in).astype(bf16)

    columns = grad_qkv.shape[1] // shards
    grad_qkv_cols = exchange(grad_qkv.reshape(rows, shards, columns).transpose(1, 0, 2), SHARD)
    qkv_block = dot_general(
        normed_all, grad_qkv_cols.reshape(shards * rows, columns), ((0,), (0,))
    )
    qkv_rows = exchange(qkv_block.astype(bf16), SHARD).reshape(shards, width // shards, columns)
    qkv_rows = qkv_rows.transpose(1, 0, 2).reshape(width // shards, shards * columns)
    out_rows = jnp.einsum(
        "jat,jtn->an",
        attended_cols,
        grad_branch_all.reshape(shards, rows, width),
        preferred_element_type=f32,
    ).astype(bf16)
    attn_rows = jnp.concatenate([qkv_rows, out_rows], axis=1)
    attn_rep = exchange(cut(attn_rows, reps), "rep").astype(f32).sum(axis=0).astype(bf16)
    attn_grads = uncut(spread(attn_rep, reps, "rep"), reps).astype(f32)

    grad_gains = jnp.stack([grad_gain_attn, grad_gain_ffn]).reshape(2, shards, -1)
    grad_gains = exchange(grad_gains.transpose(1, 0, 2).astype(bf16), SHARD)
    grad_gains = grad_gains.astype(f32).sum(axis=0)
    grad_gains = spread(grad_gains.astype(bf16), reps, "rep").astype(f32).sum(axis=0)
    return (
        output,
        grad_tokens,
        grad_gains[0],
        attn_grads[:, :width],
        attn_grads[:, width : width + 2 * kv_width],
        attn_grads[:, width + 2 * kv_width :],
        grad_gains[1],
        shard_gateup,
        shard_down,
    )


def solution(mesh):
    reps, shards = mesh.devices.shape
    fine = Mesh(mesh.devices.reshape(reps, shards // 4, 2, 2), ("rep", "y", "x", "c"))
    split = ("rep", "y", "x", "c")
    placed = (
        P(split, None),
        P(split, None),
        P("rep", None),
        P("rep", None),
        P(split, None),
        P(split, None),
        P(SHARD),
        P(SHARD, None),
        P(SHARD, None),
        P(SHARD, None),
        P(SHARD),
        P(None, SHARD, None),
        P(None, SHARD, None),
    )
    return jax.shard_map(
        per_device,
        mesh=fine,
        in_specs=placed,
        out_specs=(
            P(split, None),
            P(split, None),
            P(SHARD),
            P(SHARD, None),
            P(SHARD, None),
            P(SHARD, None),
            P(SHARD),
            P(None, SHARD, None),
            P(None, SHARD, None),
        ),
        check_vma=False,
    )
```

```python
import jax
import jax.numpy as jnp
from jax import lax
from jax.experimental import pallas as pl
from jax.experimental.pallas import tpu as pltpu
from jax.sharding import Mesh, PartitionSpec as P

QUERY_HEADS = 12
KEY_VALUE_HEADS = 2
GROUP = QUERY_HEADS // KEY_VALUE_HEADS
HEAD_SIZE = 128
CAP = 80

EPSILON = 1e-06
ROPE_BASE = 10000.0
SHARD = ("y", "x", "c")
CHIPS = ("y", "x")
REP = ("h", "z")
ALL = REP + SHARD
SWAP = [(0, 1), (1, 0)]

bf16 = jnp.bfloat16
f32 = jnp.float32


def exchange(parts, axes):
    return lax.all_to_all(parts, axes, 0, 0, tiled=True)


def matmul(left, right):
    return jnp.dot(left, right, preferred_element_type=f32)


def dot_general(left, right, dims):
    return lax.dot_general(left, right, (dims, ((), ())), preferred_element_type=f32)


def in_core_order(core, mine, other):
    return jnp.where(core == 0, jnp.stack([mine, other], 1), jnp.stack([other, mine], 1))


def rotary_tables(position):
    half = HEAD_SIZE // 2
    frequency = ROPE_BASE ** (-jnp.arange(half, dtype=f32) / half)
    angle = position.astype(f32)[:, None] * frequency[None, :]
    return jnp.cos(angle)[:, None, :], jnp.sin(angle)[:, None, :]


def rotate(values, cosine, sine):
    half = values.shape[-1] // 2
    first, second = values[..., :half], values[..., half:]
    return jnp.concatenate(
        [first * cosine - second * sine, second * cosine + first * sine], axis=-1
    )


def norm_back(values, factor, gain_row, upstream):
    grad_normed = upstream * gain_row
    grad_gain = jnp.sum(upstream * values * factor, axis=0)
    cubed = factor * factor * factor
    grad_input = factor * grad_normed - values * cubed * jnp.mean(
        grad_normed * values, axis=-1, keepdims=True
    )
    return grad_input, grad_gain


def after(value, *earlier):
    return lax.optimization_barrier((value, *earlier))[0]


def pieces_of(rows, wide):
    *lead, a, b = rows.shape
    n = len(lead)
    cut_up = rows.reshape(*lead, 2, a // 2, wide, b // wide)
    return cut_up.transpose(n, n + 2, *range(n), n + 1, n + 3)


def sum_over_rep(pieces):
    wide = pieces.shape[1]
    z = lax.axis_index("z")
    total = lax.dynamic_index_in_dim(pieces, z, 1, keepdims=False).astype(f32)
    for k in range(1, wide):
        sent = lax.dynamic_index_in_dim(pieces, z ^ k, 1, keepdims=False)
        total = total + lax.ppermute(sent, "z", [(i, i ^ k) for i in range(wide)]).astype(f32)
    h = lax.axis_index("h")
    mine = lax.dynamic_index_in_dim(total, h, 0, keepdims=False)
    sent = lax.dynamic_index_in_dim(total, 1 - h, 0, keepdims=False).astype(bf16)
    return (mine + lax.ppermute(sent, "h", SWAP).astype(f32)).astype(bf16)


def gather_over_rep(piece):
    other = lax.ppermute(piece, "h", SWAP)
    low = lax.axis_index("h") == 0
    both = jnp.stack([jnp.where(low, piece, other), jnp.where(low, other, piece)])
    wide = lax.axis_size("z")
    moved = [
        lax.ppermute(both, "z", [(i, i ^ k) for i in range(wide)]) for k in range(1, wide)
    ]
    return [both, *moved]


def expert_outputs(moved, rows_up, rows_down):
    wide = len(moved)
    _, experts, half, part = moved[0].shape
    width = wide * part
    z = lax.axis_index("z").astype(jnp.int32).reshape(1)

    def kernel(z_ref, *refs):
        up_ref, down_ref = refs[wide], refs[wide + 1]
        for k in range(wide):
            at = pl.multiple_of((z_ref[0] ^ k) * part, 128)
            first = refs[k][0, 0].astype(f32)
            second = refs[k][1, 0].astype(f32)
            split = rows_up - half
            up_ref[0, :half, pl.ds(at, part)] = first
            up_ref[0, half:, pl.ds(at, part)] = second[:split]
            down_ref[0, :, pl.ds(at, part)] = second[split:]

    return pl.pallas_call(
        kernel,
        grid_spec=pltpu.PrefetchScalarGridSpec(
            num_scalar_prefetch=1,
            grid=(experts,),
            in_specs=[pl.BlockSpec((2, 1, half, part), lambda e, z_ref: (0, e, 0, 0))] * wide,
            out_specs=[
                pl.BlockSpec((1, rows_up, width), lambda e, z_ref: (e, 0, 0)),
                pl.BlockSpec((1, rows_down, width), lambda e, z_ref: (e, 0, 0)),
            ],
        ),
        out_shape=[
            jax.ShapeDtypeStruct((experts, rows_up, width), f32),
            jax.ShapeDtypeStruct((experts, rows_down, width), f32),
        ],
    )(z, *moved)


def attention_outputs(pieces, widths):
    count, half, part = pieces.shape
    wide = count // 2

    def kernel(piece_ref, *out_refs):
        for h in range(2):
            for z in range(wide):
                left, right, base = z * part, (z + 1) * part, 0
                for ref, size in zip(out_refs, widths):
                    low, high = max(left, base), min(right, base + size)
                    if low < high:
                        ref[h * half : (h + 1) * half, low - base : high - base] = piece_ref[
                            h * wide + z, :, low - left : high - left
                        ].astype(f32)
                    base += size

    return pl.pallas_call(
        kernel,
        out_shape=[jax.ShapeDtypeStruct((2 * half, size), f32) for size in widths],
    )(pieces)


def spread(part, ways, axes):
    return exchange(jnp.broadcast_to(part[None], (ways, *part.shape)), axes)


def per_device(
    tokens,
    cotangent,
    seq_lengths,
    seq_order,
    routes,
    gate_weights,
    attn_gain,
    w_query,
    key_value_weight,
    w_out,
    ffn_gain,
    w_gateup,
    w_down,
):
    wide_z = lax.axis_size("z")
    reps = 2 * wide_z
    shards = lax.axis_size("y") * lax.axis_size("x") * lax.axis_size("c")
    core = lax.axis_index("c")
    shard = (lax.axis_index("y") * lax.axis_size("x") + lax.axis_index("x")) * 2 + core
    rows, width = tokens.shape
    experts = w_gateup.shape[0]
    ff = w_gateup.shape[2] // 2
    kv_width = KEY_VALUE_HEADS * HEAD_SIZE
    scale = HEAD_SIZE ** (-0.5)

    qkv_full = lax.all_gather(
        jnp.concatenate([w_query, key_value_weight], 1), SHARD, axis=0, tiled=True
    )
    out_full = lax.all_gather(w_out, SHARD, axis=0, tiled=True)
    part = width // wide_z
    rows_up, rows_down = w_gateup.shape[1], w_down.shape[1]
    column = lax.axis_index("z") * part
    gains_own = jnp.pad(jnp.stack([attn_gain, ffn_gain]), ((0, 6), (0, part - attn_gain.shape[0])))
    expert_part = jnp.concatenate(
        [
            lax.dynamic_slice_in_dim(w_gateup, column, part, 2),
            lax.dynamic_slice_in_dim(w_down, column, part, 2),
            jnp.broadcast_to(gains_own[None], (experts, *gains_own.shape)),
        ],
        axis=1,
    )
    expert_part = exchange(expert_part, CHIPS)
    gains_mine = expert_part[:, rows_up + rows_down : rows_up + rows_down + 2, : attn_gain.shape[0]]
    gains = in_core_order(core, gains_mine, lax.ppermute(gains_mine, "c", SWAP))
    gains = gains.transpose(2, 0, 1, 3).reshape(2, width).astype(f32)
    gain_attn, gain_ffn = gains[0], gains[1]
    expert_mine = spread(expert_part[:, : rows_up + rows_down], wide_z, "z")
    expert_other = lax.ppermute(expert_mine, "c", SWAP)
    expert_full = in_core_order(core, expert_mine.transpose(1, 2, 0, 3), expert_other.transpose(1, 2, 0, 3))
    expert_full = expert_full.reshape(experts, 2, rows_up + rows_down, width)
    gateup_full = expert_full[:, :, :rows_up].reshape(width, 2 * ff)
    down_full = expert_full[:, :, rows_up:].reshape(ff, width)

    chosen = routes[:, :, None] == jnp.arange(experts, dtype=jnp.int32)
    member = jnp.any(chosen, axis=1)
    weight = jnp.sum(jnp.where(chosen, gate_weights[:, :, None], 0.0), axis=1)
    place = jnp.cumsum(member.astype(jnp.int32), axis=0) - 1
    slot = jnp.where(member, place, -1).T
    picks = slot[:, None, :] == jnp.arange(CAP, dtype=jnp.int32)[None, :, None]
    pick = picks.astype(bf16).reshape(experts * CAP, rows)
    slot_weight = jnp.sum(jnp.where(picks, weight.T[:, None, :], 0.0), axis=2)
    upstream = cotangent.astype(f32)
    grad_out_sent = matmul(pick, cotangent) * slot_weight.reshape(-1, 1)
    grad_out = exchange(after(grad_out_sent.astype(bf16), expert_mine), CHIPS)

    lengths = seq_lengths[0]
    starts = jnp.cumsum(lengths) - lengths
    row_at = shard * rows + jnp.arange(rows, dtype=jnp.int32)
    first_at = jnp.max(jnp.where(starts[None, :] <= row_at[:, None], starts[None, :], 0), axis=1)
    cosine, sine = rotary_tables(row_at - first_at)
    key_at = (shard - 1) * rows + jnp.arange(2 * rows, dtype=jnp.int32)
    allowed = (key_at[None, :] <= row_at[:, None]) & (key_at[None, :] >= first_at[:, None])

    wide = tokens.astype(f32)
    attn_factor = lax.rsqrt(jnp.mean(wide * wide, axis=-1, keepdims=True) + EPSILON)
    normed = (wide * attn_factor * gain_attn).astype(bf16)
    qkv = matmul(normed, qkv_full)
    turned = rotate(
        qkv[:, : width + kv_width].reshape(rows, QUERY_HEADS + KEY_VALUE_HEADS, HEAD_SIZE),
        cosine,
        sine,
    ).astype(bf16)
    queries = turned[:, :QUERY_HEADS].reshape(rows, KEY_VALUE_HEADS, GROUP, HEAD_SIZE)
    keyval = jnp.concatenate(
        [turned[:, QUERY_HEADS:].reshape(rows, kv_width), qkv[:, width + kv_width :].astype(bf16)],
        axis=1,
    )
    ring = [(i, (i + 1) % shards) for i in range(shards)]
    back_ring = [((i + 1) % shards, i) for i in range(shards)]
    keyval = jnp.concatenate([lax.ppermute(keyval, SHARD, ring), keyval], axis=0)
    keys = keyval[:, :kv_width].reshape(2 * rows, KEY_VALUE_HEADS, HEAD_SIZE)
    values = keyval[:, kv_width:].reshape(2 * rows, KEY_VALUE_HEADS, HEAD_SIZE)
    raw = jnp.einsum("sgrd,tgd->grst", queries, keys, preferred_element_type=f32)
    scores = jnp.where(allowed, raw * scale, -1000000000.0)
    exp_scores = jnp.exp(scores - jnp.max(scores, axis=-1, keepdims=True))
    probs = exp_scores / jnp.sum(exp_scores, axis=-1, keepdims=True)
    prob_low = probs.astype(bf16)
    mixed = jnp.einsum("grst,tgd->sgrd", prob_low, values, preferred_element_type=f32)
    attended = mixed.reshape(rows, width).astype(bf16)
    branch = matmul(attended, out_full).astype(bf16)
    residual = wide + branch.astype(f32)
    ffn_factor = lax.rsqrt(jnp.mean(residual * residual, axis=-1, keepdims=True) + EPSILON)
    normed_ffn = (residual * ffn_factor * gain_ffn).astype(bf16)

    picked = exchange(after(matmul(pick, normed_ffn).astype(bf16), grad_out), CHIPS)
    normed_all = lax.all_gather(after(normed, picked), SHARD, axis=0, tiled=True)
    attended_cols = exchange(after(attended.T, picked), SHARD)
    attended_cols = attended_cols.reshape(shards, width // shards, rows)
    pre = matmul(picked, gateup_full)
    gate, up = pre[:, :ff], pre[:, ff:]
    sigmoid = jax.nn.sigmoid(gate)
    silu = gate * sigmoid
    acted = (silu * up).astype(bf16)
    expert_out = matmul(acted, down_full).astype(bf16)
    grad_act = dot_general(grad_out, down_full, ((1,), (1,)))
    grad_gate = grad_act * up * sigmoid * (1.0 + gate * (1.0 - sigmoid))
    grad_pre = jnp.concatenate([grad_gate, grad_act * silu], axis=1).astype(bf16)
    grad_picked = dot_general(grad_pre, gateup_full, ((1,), (1,)))
    grad_picked = exchange(after(grad_picked.astype(bf16), attended_cols), CHIPS)
    expert_out = exchange(after(expert_out, grad_picked), CHIPS)
    grad_down = dot_general(acted, grad_out, ((0,), (0,)))
    grad_gateup = dot_general(picked, grad_pre, ((0,), (0,)))

    def owned(grad):
        halves = grad.astype(bf16).reshape(experts, 2, -1, width)
        there = lax.dynamic_index_in_dim(halves, 1 - core, 1, keepdims=False)
        here = lax.dynamic_index_in_dim(halves, core, 1, keepdims=False)
        return here.astype(f32) + lax.ppermute(there, "c", SWAP).astype(f32)

    both = jnp.concatenate([owned(grad_gateup), owned(grad_down)], axis=1).astype(bf16)
    over_rep = sum_over_rep(pieces_of(both, wide_z))

    back = pick.astype(f32) * slot_weight.reshape(-1, 1)
    back_high = back.astype(bf16)
    back_low = (back - back_high.astype(f32)).astype(bf16)
    mixture = dot_general(back_high, expert_out, ((0,), (0,)))
    mixture = mixture + dot_general(back_low, expert_out, ((0,), (0,)))
    output = (residual + mixture).astype(bf16)
    grad_ffn_in = dot_general(pick, grad_picked, ((0,), (0,)))
    grad_from_norm, grad_gain_ffn = norm_back(residual, ffn_factor, gain_ffn, grad_ffn_in)
    grad_residual = upstream + grad_from_norm
    grad_branch = grad_residual.astype(bf16)
    grad_branch_all = lax.all_gather(grad_branch, SHARD, axis=0, tiled=True)

    grad_attended = dot_general(grad_branch, out_full, ((1,), (1,))).astype(bf16)
    grad_attended = grad_attended.reshape(rows, KEY_VALUE_HEADS, GROUP, HEAD_SIZE)
    grad_probs = jnp.einsum("sgrd,tgd->grst", grad_attended, values, preferred_element_type=f32)
    grad_values = jnp.einsum("grst,sgrd->tgd", prob_low, grad_attended, preferred_element_type=f32)
    inner = jnp.sum(probs * grad_probs, axis=-1, keepdims=True)
    grad_raw = (probs * (grad_probs - inner) * scale).astype(bf16)
    grad_queries = jnp.einsum("grst,tgd->sgrd", grad_raw, keys, preferred_element_type=f32)
    grad_keys = jnp.einsum("grst,sgrd->tgd", grad_raw, queries, preferred_element_type=f32)
    grad_keyval = jnp.concatenate(
        [grad_keys.reshape(2 * rows, kv_width), grad_values.reshape(2 * rows, kv_width)], axis=1
    )
    from_next = lax.ppermute(grad_keyval[:rows].astype(bf16), SHARD, back_ring)
    grad_keyval = grad_keyval[rows:] + from_next.astype(f32)
    grad_turned = jnp.concatenate(
        [grad_queries.reshape(rows, width), grad_keyval[:, :kv_width]], axis=1
    )
    grad_turned = grad_turned.reshape(rows, QUERY_HEADS + KEY_VALUE_HEADS, HEAD_SIZE)
    grad_qkv = jnp.concatenate(
        [
            rotate(grad_turned, cosine, -sine).reshape(rows, width + kv_width),
            grad_keyval[:, kv_width:],
        ],
        axis=1,
    ).astype(bf16)
    grad_normed = dot_general(grad_qkv, qkv_full, ((1,), (1,)))
    grad_in, grad_gain_attn = norm_back(wide, attn_factor, gain_attn, grad_normed)
    grad_tokens = (grad_residual + grad_in).astype(bf16)

    columns = grad_qkv.shape[1] // shards
    grad_qkv_cols = exchange(
        after(grad_qkv.reshape(rows, shards, columns).transpose(1, 0, 2), expert_out), SHARD
    )
    qkv_block = dot_general(
        normed_all, grad_qkv_cols.reshape(shards * rows, columns), ((0,), (0,))
    ).astype(bf16)
    over_rep = after(over_rep, grad_qkv_cols)
    expert_pieces = exchange(over_rep, CHIPS)
    shard_gateup, shard_down = expert_outputs(gather_over_rep(expert_pieces), rows_up, rows_down)

    out_rows = jnp.einsum(
        "jat,jtn->an",
        attended_cols,
        grad_branch_all.reshape(shards, rows, width),
        preferred_element_type=f32,
    ).astype(bf16)
    qkv_rows = exchange(after(qkv_block, expert_pieces), SHARD)
    qkv_rows = qkv_rows.reshape(shards, width // shards, columns)
    qkv_rows = qkv_rows.transpose(1, 0, 2).reshape(width // shards, shards * columns)
    attn_rows = jnp.concatenate([qkv_rows, out_rows], axis=1)
    attn_pieces = pieces_of(attn_rows, wide_z)
    attn_pieces = attn_pieces.reshape(reps, *attn_pieces.shape[2:])
    attn_rep = exchange(attn_pieces, REP).astype(f32).sum(axis=0).astype(bf16)
    attn_all = spread(attn_rep, reps, REP)
    grad_query, grad_keyval_w, grad_out_w = attention_outputs(
        attn_all, (width, 2 * kv_width, width)
    )

    grad_gains = jnp.stack([grad_gain_attn, grad_gain_ffn]).reshape(2, shards, -1)
    grad_gains = exchange(after(grad_gains.transpose(1, 0, 2).astype(bf16), qkv_rows), SHARD)
    grad_gains = grad_gains.astype(f32).sum(axis=0)
    grad_gains = spread(grad_gains.astype(bf16), reps, REP).astype(f32).sum(axis=0)
    return (
        output,
        grad_tokens,
        grad_gains[0],
        grad_query,
        grad_keyval_w,
        grad_out_w,
        grad_gains[1],
        shard_gateup,
        shard_down,
    )


def solution(mesh):
    reps, shards = mesh.devices.shape
    fine = Mesh(mesh.devices.reshape(2, reps // 2, shards // 4, 2, 2), ALL)
    split = ALL
    placed = (
        P(split, None),
        P(split, None),
        P(REP, None),
        P(REP, None),
        P(split, None),
        P(split, None),
        P(SHARD),
        P(SHARD, None),
        P(SHARD, None),
        P(SHARD, None),
        P(SHARD),
        P(None, SHARD, None),
        P(None, SHARD, None),
    )
    return jax.shard_map(
        per_device,
        mesh=fine,
        in_specs=placed,
        out_specs=(
            P(split, None),
            P(split, None),
            P(SHARD),
            P(SHARD, None),
            P(SHARD, None),
            P(SHARD, None),
            P(SHARD),
            P(None, SHARD, None),
            P(None, SHARD, None),
        ),
        check_vma=False,
    )
```

```python
import jax
import jax.numpy as jnp
from jax import lax
from jax.experimental import pallas as pl
from jax.experimental.pallas import tpu as pltpu
from jax.sharding import Mesh, PartitionSpec as P

QUERY_HEADS = 12
KEY_VALUE_HEADS = 2
GROUP = QUERY_HEADS // KEY_VALUE_HEADS
HEAD_SIZE = 128
CAP = 80

EPSILON = 1e-06
ROPE_BASE = 10000.0
SHARD = ("y", "x", "c")
CHIPS = ("y", "x")
REP = ("h", "z")
ALL = REP + SHARD
SWAP = [(0, 1), (1, 0)]

bf16 = jnp.bfloat16
f32 = jnp.float32


def exchange(parts, axes):
    return lax.all_to_all(parts, axes, 0, 0, tiled=True)


def matmul(left, right):
    return jnp.dot(left, right, preferred_element_type=f32)


def dot_general(left, right, dims):
    return lax.dot_general(left, right, (dims, ((), ())), preferred_element_type=f32)


def in_core_order(core, mine, other):
    return jnp.where(core == 0, jnp.stack([mine, other], 1), jnp.stack([other, mine], 1))


def rotary_tables(position):
    half = HEAD_SIZE // 2
    frequency = ROPE_BASE ** (-jnp.arange(half, dtype=f32) / half)
    angle = position.astype(f32)[:, None] * frequency[None, :]
    return jnp.cos(angle)[:, None, :], jnp.sin(angle)[:, None, :]


def rotate(values, cosine, sine):
    half = values.shape[-1] // 2
    first, second = values[..., :half], values[..., half:]
    return jnp.concatenate(
        [first * cosine - second * sine, second * cosine + first * sine], axis=-1
    )


def norm_back(values, factor, gain_row, upstream):
    grad_normed = upstream * gain_row
    grad_gain = jnp.sum(upstream * values * factor, axis=0)
    cubed = factor * factor * factor
    grad_input = factor * grad_normed - values * cubed * jnp.mean(
        grad_normed * values, axis=-1, keepdims=True
    )
    return grad_input, grad_gain


def after(value, *earlier):
    return lax.optimization_barrier((value, *earlier))[0]


def gather_over_z(part):
    wide = lax.axis_size("z")
    return [part] + [
        lax.ppermute(part, "z", [(i, i ^ k) for i in range(wide)]) for k in range(1, wide)
    ]


def sum_over_rep(here, other):
    wide = here.shape[1]
    z = lax.axis_index("z")

    def piece(k):
        mine = lax.dynamic_index_in_dim(here, z ^ k, 1, keepdims=False)
        return mine.astype(f32) + lax.dynamic_index_in_dim(other, z ^ k, 1, keepdims=False).astype(f32)

    moved = [
        lax.ppermute(piece(k).astype(bf16), "z", [(i, i ^ k) for i in range(wide)])
        for k in range(1, wide)
    ]
    total = piece(0)
    for received in moved:
        total = total + received.astype(f32)
    h = lax.axis_index("h")
    mine = lax.dynamic_index_in_dim(total, h, 0, keepdims=False)
    sent = lax.dynamic_index_in_dim(total, 1 - h, 0, keepdims=False).astype(bf16)
    return (mine + lax.ppermute(sent, "h", SWAP).astype(f32)).astype(bf16)


def gather_over_rep(piece):
    other = lax.ppermute(piece, "h", SWAP)
    low = lax.axis_index("h") == 0
    both = jnp.stack([jnp.where(low, piece, other), jnp.where(low, other, piece)])
    return gather_over_z(both)


def assemble_experts(mine, other, rows_up, rows_down):
    wide = len(mine)
    chips, rows, part = mine[0].shape
    width = wide * part
    place = jnp.stack([lax.axis_index("z"), lax.axis_index("c")]).astype(jnp.int32)

    def kernel(place_ref, *refs):
        up_ref, down_ref = refs[2 * wide], refs[2 * wide + 1]
        for owner, parts in ((place_ref[1], refs[:wide]), (1 - place_ref[1], refs[wide : 2 * wide])):
            for k in range(wide):
                at = pl.multiple_of((place_ref[0] ^ k) * part, 128)
                up_ref[0, owner, :, pl.ds(at, part)] = parts[k][0, :rows_up]
                down_ref[0, owner, :, pl.ds(at, part)] = parts[k][0, rows_up : rows_up + rows_down]

    up, down = pl.pallas_call(
        kernel,
        grid_spec=pltpu.PrefetchScalarGridSpec(
            num_scalar_prefetch=1,
            grid=(chips,),
            in_specs=[pl.BlockSpec((1, rows, part), lambda e, p: (e, 0, 0))] * (2 * wide),
            out_specs=[
                pl.BlockSpec((1, 2, rows_up, width), lambda e, p: (e, 0, 0, 0)),
                pl.BlockSpec((1, 2, rows_down, width), lambda e, p: (e, 0, 0, 0)),
            ],
        ),
        out_shape=[
            jax.ShapeDtypeStruct((chips, 2, rows_up, width), bf16),
            jax.ShapeDtypeStruct((chips, 2, rows_down, width), bf16),
        ],
    )(place, *mine, *other)
    return up.reshape(-1, width), down.reshape(-1, width)


def cut_expert_grads(grad_up, grad_down, rows_up, rows_down, wide):
    width = grad_up.shape[1]
    chips = grad_up.shape[0] // (2 * rows_up)
    half, part = (rows_up + rows_down) // 2, width // wide
    core = lax.axis_index("c").astype(jnp.int32).reshape(1)

    def kernel(core_ref, up_ref, down_ref, here_ref, there_ref):
        for owner, out_ref in ((core_ref[0], here_ref), (1 - core_ref[0], there_ref)):
            up = up_ref[0, owner].astype(f32)
            rest = jnp.concatenate([up[half:], down_ref[0, owner].astype(f32)], axis=0).astype(bf16)
            first = up[:half].astype(bf16)
            for z in range(wide):
                out_ref[0, z, 0] = first[:, z * part : (z + 1) * part]
                out_ref[1, z, 0] = rest[:, z * part : (z + 1) * part]

    pieces = pl.BlockSpec((2, wide, 1, half, part), lambda e, p: (0, 0, e, 0, 0))
    return pl.pallas_call(
        kernel,
        grid_spec=pltpu.PrefetchScalarGridSpec(
            num_scalar_prefetch=1,
            grid=(chips,),
            in_specs=[
                pl.BlockSpec((1, 2, rows_up, width), lambda e, p: (e, 0, 0, 0)),
                pl.BlockSpec((1, 2, rows_down, width), lambda e, p: (e, 0, 0, 0)),
            ],
            out_specs=[pieces, pieces],
        ),
        out_shape=[jax.ShapeDtypeStruct((2, wide, chips, half, part), bf16)] * 2,
    )(
        core,
        grad_up.reshape(chips, 2, rows_up, width),
        grad_down.reshape(chips, 2, rows_down, width),
    )


def pack_attention_grads(blocks, out_rows, wide):
    count, rows, column = blocks.shape
    rows -= 8
    half = rows // 2
    total = count + out_rows.shape[1] // column
    each = total // wide

    def kernel(block_ref, out_ref, piece_ref):
        piece_ref[...] = jnp.zeros_like(piece_ref)
        gains = block_ref[0, rows:].astype(f32)
        for b in range(1, count):
            gains = gains + block_ref[b, rows:].astype(f32)
        for h in range(2):
            at = slice(h * half, (h + 1) * half)
            for b in range(total):
                if b < count:
                    value = block_ref[b, at]
                else:
                    value = out_ref[at, (b - count) * column : (b - count + 1) * column]
                to = (b % each) * column
                piece_ref[h * wide + b // each, :half, to : to + column] = value
        for p in range(2 * wide):
            piece_ref[p, half:, :column] = gains.astype(bf16)

    return pl.pallas_call(
        kernel, out_shape=jax.ShapeDtypeStruct((2 * wide, half + 8, each * column), bf16)
    )(blocks, out_rows)


def sum_and_copy(pieces):
    count, rows, columns = pieces.shape

    def kernel(piece_ref, copy_ref, gain_ref):
        total = piece_ref[0].astype(f32)
        for p in range(1, count):
            total = total + piece_ref[p].astype(f32)
        gain_ref[...] = total[rows - 8 :, :128]
        low = total[: rows - 8].astype(bf16)
        for p in range(count):
            copy_ref[p] = low

    return pl.pallas_call(
        kernel,
        out_shape=[
            jax.ShapeDtypeStruct((count, rows - 8, columns), bf16),
            jax.ShapeDtypeStruct((8, 128), f32),
        ],
    )(pieces)


def expert_outputs(moved, rows_up, rows_down):
    wide = len(moved)
    _, experts, half, part = moved[0].shape
    width = wide * part
    z = lax.axis_index("z").astype(jnp.int32).reshape(1)

    def kernel(z_ref, *refs):
        up_ref, down_ref = refs[wide], refs[wide + 1]
        for k in range(wide):
            at = pl.multiple_of((z_ref[0] ^ k) * part, 128)
            first = refs[k][0, 0].astype(f32)
            second = refs[k][1, 0].astype(f32)
            split = rows_up - half
            up_ref[0, :half, pl.ds(at, part)] = first
            up_ref[0, half:, pl.ds(at, part)] = second[:split]
            down_ref[0, :, pl.ds(at, part)] = second[split:]

    return pl.pallas_call(
        kernel,
        grid_spec=pltpu.PrefetchScalarGridSpec(
            num_scalar_prefetch=1,
            grid=(experts,),
            in_specs=[pl.BlockSpec((2, 1, half, part), lambda e, z_ref: (0, e, 0, 0))] * wide,
            out_specs=[
                pl.BlockSpec((1, rows_up, width), lambda e, z_ref: (e, 0, 0)),
                pl.BlockSpec((1, rows_down, width), lambda e, z_ref: (e, 0, 0)),
            ],
        ),
        out_shape=[
            jax.ShapeDtypeStruct((experts, rows_up, width), f32),
            jax.ShapeDtypeStruct((experts, rows_down, width), f32),
        ],
    )(z, *moved)


def attention_outputs(pieces, widths):
    count, half, part = pieces.shape
    wide = count // 2

    def kernel(piece_ref, *out_refs):
        for h in range(2):
            for z in range(wide):
                left, right, base = z * part, (z + 1) * part, 0
                for ref, size in zip(out_refs, widths):
                    low, high = max(left, base), min(right, base + size)
                    if low < high:
                        ref[h * half : (h + 1) * half, low - base : high - base] = piece_ref[
                            h * wide + z, :, low - left : high - left
                        ].astype(f32)
                    base += size

    return pl.pallas_call(
        kernel,
        out_shape=[jax.ShapeDtypeStruct((2 * half, size), f32) for size in widths],
    )(pieces)


def spread(part, ways, axes):
    return exchange(jnp.broadcast_to(part[None], (ways, *part.shape)), axes)


def per_device(
    tokens,
    cotangent,
    seq_lengths,
    seq_order,
    routes,
    gate_weights,
    attn_gain,
    w_query,
    key_value_weight,
    w_out,
    ffn_gain,
    w_gateup,
    w_down,
):
    wide_z = lax.axis_size("z")
    shards = lax.axis_size("y") * lax.axis_size("x") * lax.axis_size("c")
    core = lax.axis_index("c")
    shard = (lax.axis_index("y") * lax.axis_size("x") + lax.axis_index("x")) * 2 + core
    rows, width = tokens.shape
    experts = w_gateup.shape[0]
    ff = w_gateup.shape[2] // 2
    kv_width = KEY_VALUE_HEADS * HEAD_SIZE
    scale = HEAD_SIZE ** (-0.5)

    attn_full = lax.all_gather(
        jnp.concatenate([w_query, key_value_weight, w_out], 1), SHARD, axis=0, tiled=True
    )
    qkv_full, out_full = attn_full[:, : width + 2 * kv_width], attn_full[:, width + 2 * kv_width :]
    part = width // wide_z
    rows_up, rows_down = w_gateup.shape[1], w_down.shape[1]
    column = lax.axis_index("z") * part
    gains_own = jnp.pad(jnp.stack([attn_gain, ffn_gain]), ((0, 6), (0, part - attn_gain.shape[0])))
    expert_part = jnp.concatenate(
        [
            lax.dynamic_slice_in_dim(w_gateup, column, part, 2),
            lax.dynamic_slice_in_dim(w_down, column, part, 2),
            jnp.broadcast_to(gains_own[None], (experts, *gains_own.shape)),
        ],
        axis=1,
    )
    expert_part = exchange(expert_part, CHIPS)
    gains_mine = expert_part[:, rows_up + rows_down : rows_up + rows_down + 2, : attn_gain.shape[0]]
    gains = in_core_order(core, gains_mine, lax.ppermute(gains_mine, "c", SWAP))
    gains = gains.transpose(2, 0, 1, 3).reshape(2, width).astype(f32)
    gain_attn, gain_ffn = gains[0], gains[1]
    expert_mine = gather_over_z(expert_part)
    expert_other = [lax.ppermute(one, "c", SWAP) for one in expert_mine]
    gateup_full, down_full = assemble_experts(expert_mine, expert_other, rows_up, rows_down)

    chosen = routes[:, :, None] == jnp.arange(experts, dtype=jnp.int32)
    member = jnp.any(chosen, axis=1)
    weight = jnp.sum(jnp.where(chosen, gate_weights[:, :, None], 0.0), axis=1)
    place = jnp.cumsum(member.astype(jnp.int32), axis=0) - 1
    slot = jnp.where(member, place, -1).T
    picks = slot[:, None, :] == jnp.arange(CAP, dtype=jnp.int32)[None, :, None]
    pick = picks.astype(bf16).reshape(experts * CAP, rows)
    slot_weight = jnp.sum(jnp.where(picks, weight.T[:, None, :], 0.0), axis=2)
    upstream = cotangent.astype(f32)
    grad_out_sent = matmul(pick, cotangent) * slot_weight.reshape(-1, 1)
    grad_out = exchange(after(grad_out_sent.astype(bf16), expert_part), CHIPS)

    lengths = seq_lengths[0]
    starts = jnp.cumsum(lengths) - lengths
    row_at = shard * rows + jnp.arange(rows, dtype=jnp.int32)
    first_at = jnp.max(jnp.where(starts[None, :] <= row_at[:, None], starts[None, :], 0), axis=1)
    cosine, sine = rotary_tables(row_at - first_at)
    key_at = (shard - 1) * rows + jnp.arange(2 * rows, dtype=jnp.int32)
    allowed = (key_at[None, :] <= row_at[:, None]) & (key_at[None, :] >= first_at[:, None])

    wide = tokens.astype(f32)
    attn_factor = lax.rsqrt(jnp.mean(wide * wide, axis=-1, keepdims=True) + EPSILON)
    normed = (wide * attn_factor * gain_attn).astype(bf16)
    qkv = matmul(normed, qkv_full)
    turned = rotate(
        qkv[:, : width + kv_width].reshape(rows, QUERY_HEADS + KEY_VALUE_HEADS, HEAD_SIZE),
        cosine,
        sine,
    ).astype(bf16)
    queries = turned[:, :QUERY_HEADS].reshape(rows, KEY_VALUE_HEADS, GROUP, HEAD_SIZE)
    keyval = jnp.concatenate(
        [turned[:, QUERY_HEADS:].reshape(rows, kv_width), qkv[:, width + kv_width :].astype(bf16)],
        axis=1,
    )
    ring = [(i, (i + 1) % shards) for i in range(shards)]
    back_ring = [((i + 1) % shards, i) for i in range(shards)]
    keyval = jnp.concatenate([lax.ppermute(keyval, SHARD, ring), keyval], axis=0)
    keys = keyval[:, :kv_width].reshape(2 * rows, KEY_VALUE_HEADS, HEAD_SIZE)
    values = keyval[:, kv_width:].reshape(2 * rows, KEY_VALUE_HEADS, HEAD_SIZE)
    raw = jnp.einsum("sgrd,tgd->grst", queries, keys, preferred_element_type=f32)
    scores = jnp.where(allowed, raw * scale, -1000000000.0)
    exp_scores = jnp.exp(scores - jnp.max(scores, axis=-1, keepdims=True))
    probs = exp_scores / jnp.sum(exp_scores, axis=-1, keepdims=True)
    prob_low = probs.astype(bf16)
    mixed = jnp.einsum("grst,tgd->sgrd", prob_low, values, preferred_element_type=f32)
    attended = mixed.reshape(rows, width).astype(bf16)
    branch = matmul(after(attended, gateup_full, down_full), out_full).astype(bf16)
    residual = wide + branch.astype(f32)
    ffn_factor = lax.rsqrt(jnp.mean(residual * residual, axis=-1, keepdims=True) + EPSILON)
    normed_ffn = (residual * ffn_factor * gain_ffn).astype(bf16)

    picked = exchange(after(matmul(pick, normed_ffn).astype(bf16), grad_out), CHIPS)
    normed_all = lax.all_gather(after(normed, picked), SHARD, axis=0, tiled=True)
    attended_cols = exchange(after(attended.T, picked), SHARD)
    attended_cols = attended_cols.reshape(shards, width // shards, rows)
    pre = matmul(picked, gateup_full)
    gate, up = pre[:, :ff], pre[:, ff:]
    sigmoid = jax.nn.sigmoid(gate)
    silu = gate * sigmoid
    acted = (silu * up).astype(bf16)
    expert_out = matmul(acted, down_full).astype(bf16)
    grad_act = dot_general(grad_out, down_full, ((1,), (1,)))
    grad_gate = grad_act * up * sigmoid * (1.0 + gate * (1.0 - sigmoid))
    grad_pre = jnp.concatenate([grad_gate, grad_act * silu], axis=1).astype(bf16)
    grad_picked = dot_general(grad_pre, gateup_full, ((1,), (1,)))
    grad_picked = exchange(after(grad_picked.astype(bf16), attended_cols), CHIPS)
    expert_out = exchange(after(expert_out, grad_picked), CHIPS)
    grad_down = dot_general(acted, grad_out, ((0,), (0,)))
    grad_gateup = dot_general(picked, grad_pre, ((0,), (0,)))

    here, there = cut_expert_grads(
        grad_gateup.astype(bf16), grad_down.astype(bf16), rows_up, rows_down, wide_z
    )
    over_rep = sum_over_rep(here, lax.ppermute(there, "c", SWAP))

    back = pick.astype(f32) * slot_weight.reshape(-1, 1)
    back_high = back.astype(bf16)
    back_low = (back - back_high.astype(f32)).astype(bf16)
    mixture = dot_general(back_high, expert_out, ((0,), (0,)))
    mixture = mixture + dot_general(back_low, expert_out, ((0,), (0,)))
    output = (residual + mixture).astype(bf16)
    grad_ffn_in = dot_general(pick, grad_picked, ((0,), (0,)))
    grad_from_norm, grad_gain_ffn = norm_back(residual, ffn_factor, gain_ffn, grad_ffn_in)
    grad_residual = upstream + grad_from_norm
    grad_branch = grad_residual.astype(bf16)
    grad_branch_all = lax.all_gather(grad_branch, SHARD, axis=0, tiled=True)

    grad_attended = dot_general(grad_branch, out_full, ((1,), (1,))).astype(bf16)
    grad_attended = grad_attended.reshape(rows, KEY_VALUE_HEADS, GROUP, HEAD_SIZE)
    grad_probs = jnp.einsum("sgrd,tgd->grst", grad_attended, values, preferred_element_type=f32)
    grad_values = jnp.einsum("grst,sgrd->tgd", prob_low, grad_attended, preferred_element_type=f32)
    inner = jnp.sum(probs * grad_probs, axis=-1, keepdims=True)
    grad_raw = (probs * (grad_probs - inner) * scale).astype(bf16)
    grad_queries = jnp.einsum("grst,tgd->sgrd", grad_raw, keys, preferred_element_type=f32)
    grad_keys = jnp.einsum("grst,sgrd->tgd", grad_raw, queries, preferred_element_type=f32)
    grad_keyval = jnp.concatenate(
        [grad_keys.reshape(2 * rows, kv_width), grad_values.reshape(2 * rows, kv_width)], axis=1
    )
    from_next = lax.ppermute(grad_keyval[:rows].astype(bf16), SHARD, back_ring)
    grad_keyval = grad_keyval[rows:] + from_next.astype(f32)
    grad_turned = jnp.concatenate(
        [grad_queries.reshape(rows, width), grad_keyval[:, :kv_width]], axis=1
    )
    grad_turned = grad_turned.reshape(rows, QUERY_HEADS + KEY_VALUE_HEADS, HEAD_SIZE)
    grad_qkv = jnp.concatenate(
        [
            rotate(grad_turned, cosine, -sine).reshape(rows, width + kv_width),
            grad_keyval[:, kv_width:],
        ],
        axis=1,
    ).astype(bf16)
    grad_normed = dot_general(grad_qkv, qkv_full, ((1,), (1,)))
    grad_in, grad_gain_attn = norm_back(wide, attn_factor, gain_attn, grad_normed)
    grad_tokens = (grad_residual + grad_in).astype(bf16)

    columns = grad_qkv.shape[1] // shards
    grad_qkv_cols = exchange(
        after(grad_qkv.reshape(rows, shards, columns).transpose(1, 0, 2), expert_out), SHARD
    )
    qkv_block = dot_general(
        normed_all, grad_qkv_cols.reshape(shards * rows, columns), ((0,), (0,))
    ).astype(bf16)
    over_rep = after(over_rep, grad_qkv_cols)
    expert_pieces = exchange(over_rep, CHIPS)
    shard_gateup, shard_down = expert_outputs(gather_over_rep(expert_pieces), rows_up, rows_down)

    out_rows = jnp.einsum(
        "jat,jtn->an",
        attended_cols,
        grad_branch_all.reshape(shards, rows, width),
        preferred_element_type=f32,
    ).astype(bf16)
    grad_gains = jnp.stack([grad_gain_attn, grad_gain_ffn]).reshape(2, shards, -1)
    gain_rows = jnp.pad(
        grad_gains.transpose(1, 0, 2).astype(bf16),
        ((0, 0), (0, 6), (0, columns - width // shards)),
    )
    qkv_block = jnp.concatenate(
        [qkv_block.reshape(shards, width // shards, columns), gain_rows], axis=1
    )
    qkv_blocks = exchange(after(qkv_block, expert_pieces), SHARD)
    attn_pieces = exchange(pack_attention_grads(qkv_blocks, out_rows, wide_z), REP)
    attn_copies, gain_sums = sum_and_copy(attn_pieces)
    grad_query, grad_keyval_w, grad_out_w = attention_outputs(
        exchange(attn_copies, REP), (width, 2 * kv_width, width)
    )
    grad_gains = gain_sums[:2, : width // shards]
    return (
        output,
        grad_tokens,
        grad_gains[0],
        grad_query,
        grad_keyval_w,
        grad_out_w,
        grad_gains[1],
        shard_gateup,
        shard_down,
    )


def solution(mesh):
    reps, shards = mesh.devices.shape
    fine = Mesh(mesh.devices.reshape(2, reps // 2, shards // 4, 2, 2), ALL)
    split = ALL
    placed = (
        P(split, None),
        P(split, None),
        P(REP, None),
        P(REP, None),
        P(split, None),
        P(split, None),
        P(SHARD),
        P(SHARD, None),
        P(SHARD, None),
        P(SHARD, None),
        P(SHARD),
        P(None, SHARD, None),
        P(None, SHARD, None),
    )
    return jax.shard_map(
        per_device,
        mesh=fine,
        in_specs=placed,
        out_specs=(
            P(split, None),
            P(split, None),
            P(SHARD),
            P(SHARD, None),
            P(SHARD, None),
            P(SHARD, None),
            P(SHARD),
            P(None, SHARD, None),
            P(None, SHARD, None),
        ),
        check_vma=False,
    )
```

```python
import jax
import jax.numpy as jnp
from jax import lax
from jax.experimental import pallas as pl
from jax.experimental.pallas import tpu as pltpu
from jax.sharding import Mesh, PartitionSpec as P

QUERY_HEADS = 12
KEY_VALUE_HEADS = 2
GROUP = QUERY_HEADS // KEY_VALUE_HEADS
HEAD_SIZE = 128
CAP = 80

EPSILON = 1e-06
ROPE_BASE = 10000.0
SHARD = ("y", "x", "c")
CHIPS = ("y", "x")
REP = ("h", "z")
ALL = REP + SHARD
SWAP = [(0, 1), (1, 0)]

bf16 = jnp.bfloat16
f32 = jnp.float32


def exchange(parts, axes):
    return lax.all_to_all(parts, axes, 0, 0, tiled=True)


def matmul(left, right):
    return jnp.dot(left, right, preferred_element_type=f32)


def dot_general(left, right, dims):
    return lax.dot_general(left, right, (dims, ((), ())), preferred_element_type=f32)


def in_core_order(core, mine, other):
    return jnp.where(core == 0, jnp.stack([mine, other], 1), jnp.stack([other, mine], 1))


def rotary_tables(position):
    half = HEAD_SIZE // 2
    frequency = ROPE_BASE ** (-jnp.arange(half, dtype=f32) / half)
    angle = position.astype(f32)[:, None] * frequency[None, :]
    return jnp.cos(angle)[:, None, :], jnp.sin(angle)[:, None, :]


def rotate(values, cosine, sine):
    half = values.shape[-1] // 2
    first, second = values[..., :half], values[..., half:]
    return jnp.concatenate(
        [first * cosine - second * sine, second * cosine + first * sine], axis=-1
    )


def norm_back(values, factor, gain_row, upstream):
    grad_normed = upstream * gain_row
    grad_gain = jnp.sum(upstream * values * factor, axis=0)
    cubed = factor * factor * factor
    grad_input = factor * grad_normed - values * cubed * jnp.mean(
        grad_normed * values, axis=-1, keepdims=True
    )
    return grad_input, grad_gain


def after(value, *earlier):
    for one in earlier:
        zero = jnp.minimum(jnp.abs(one[(0,) * one.ndim].astype(f32)), 0.0)
        value = value + zero.astype(value.dtype)
    return value


def gather_over_z(part):
    wide = lax.axis_size("z")
    return [part] + [
        lax.ppermute(part, "z", [(i, i ^ k) for i in range(wide)]) for k in range(1, wide)
    ]


def in_z_order(moved):
    z = lax.axis_index("z")
    return jnp.stack(
        [
            lax.select_n(z ^ at, *moved) if len(moved) > 2 else jnp.where(z == at, moved[0], moved[1])
            for at in range(len(moved))
        ]
    )


def sum_over_h(total):
    h = lax.axis_index("h")
    mine = lax.dynamic_index_in_dim(total, h, 0, keepdims=False)
    sent = lax.dynamic_index_in_dim(total, 1 - h, 0, keepdims=False)
    return (mine.astype(f32) + lax.ppermute(sent, "h", SWAP).astype(f32)).astype(bf16)


def gather_over_rep(piece):
    other = lax.ppermute(piece, "h", SWAP)
    low = lax.axis_index("h") == 0
    both = jnp.stack([jnp.where(low, piece, other), jnp.where(low, other, piece)])
    return lax.all_gather(both, "z", axis=0)


def assemble(mine, other, sizes):
    wide, chips, rows, part = mine.shape
    width = wide * part
    core = lax.axis_index("c").astype(jnp.int32).reshape(1)

    def kernel(core_ref, mine_ref, other_ref, *out_refs):
        for owner, part_ref in ((core_ref[0], mine_ref), (1 - core_ref[0], other_ref)):
            for z in range(wide):
                base = 0
                for ref, size in zip(out_refs, sizes):
                    ref[0, owner, :, z * part : (z + 1) * part] = part_ref[z, 0, base : base + size]
                    base += size

    whole = pl.pallas_call(
        kernel,
        grid_spec=pltpu.PrefetchScalarGridSpec(
            num_scalar_prefetch=1,
            grid=(chips,),
            in_specs=[pl.BlockSpec((wide, 1, rows, part), lambda e, p: (0, e, 0, 0))] * 2,
            out_specs=[
                pl.BlockSpec((1, 2, size, width), lambda e, p: (e, 0, 0, 0)) for size in sizes
            ],
        ),
        out_shape=[jax.ShapeDtypeStruct((chips, 2, size, width), bf16) for size in sizes],
    )(core, mine, other)
    return [one.reshape(-1, width) for one in whole]


def cut_expert_grads(grad_up, grad_down, rows_up, rows_down, wide):
    width = grad_up.shape[1]
    chips = grad_up.shape[0] // (2 * rows_up)
    half, part = (rows_up + rows_down) // 2, width // wide
    core = lax.axis_index("c").astype(jnp.int32).reshape(1)

    def kernel(core_ref, up_ref, down_ref, here_ref, there_ref):
        for owner, out_ref in ((core_ref[0], here_ref), (1 - core_ref[0], there_ref)):
            up = up_ref[0, owner].astype(f32)
            rest = jnp.concatenate([up[half:], down_ref[0, owner].astype(f32)], axis=0).astype(bf16)
            first = up[:half].astype(bf16)
            for z in range(wide):
                out_ref[z, 0, 0] = first[:, z * part : (z + 1) * part]
                out_ref[z, 1, 0] = rest[:, z * part : (z + 1) * part]

    pieces = pl.BlockSpec((wide, 2, 1, half, part), lambda e, p: (0, 0, e, 0, 0))
    return pl.pallas_call(
        kernel,
        grid_spec=pltpu.PrefetchScalarGridSpec(
            num_scalar_prefetch=1,
            grid=(chips,),
            in_specs=[
                pl.BlockSpec((1, 2, rows_up, width), lambda e, p: (e, 0, 0, 0)),
                pl.BlockSpec((1, 2, rows_down, width), lambda e, p: (e, 0, 0, 0)),
            ],
            out_specs=[pieces, pieces],
        ),
        out_shape=[jax.ShapeDtypeStruct((wide, 2, chips, half, part), bf16)] * 2,
    )(
        core,
        grad_up.reshape(chips, 2, rows_up, width),
        grad_down.reshape(chips, 2, rows_down, width),
    )


def pack_attention_grads(blocks, out_rows, wide):
    count, rows, column = blocks.shape
    rows -= 8
    half = rows // 2
    total = count + out_rows.shape[1] // column
    each = total // wide

    def kernel(block_ref, out_ref, piece_ref):
        piece_ref[...] = jnp.zeros_like(piece_ref)
        gains = block_ref[0, rows:].astype(f32)
        for b in range(1, count):
            gains = gains + block_ref[b, rows:].astype(f32)
        for h in range(2):
            at = slice(h * half, (h + 1) * half)
            for b in range(total):
                if b < count:
                    value = block_ref[b, at]
                else:
                    value = out_ref[at, (b - count) * column : (b - count + 1) * column]
                to = (b % each) * column
                piece_ref[h * wide + b // each, :half, to : to + column] = value
        for p in range(2 * wide):
            piece_ref[p, half:, :column] = gains.astype(bf16)

    return pl.pallas_call(
        kernel, out_shape=jax.ShapeDtypeStruct((2 * wide, half + 8, each * column), bf16)
    )(blocks, out_rows)


def sum_and_copy(pieces):
    count, rows, columns = pieces.shape

    def kernel(piece_ref, copy_ref, gain_ref):
        total = piece_ref[0].astype(f32)
        for p in range(1, count):
            total = total + piece_ref[p].astype(f32)
        gain_ref[...] = total[rows - 8 :, :128]
        low = total[: rows - 8].astype(bf16)
        for p in range(count):
            copy_ref[p] = low

    return pl.pallas_call(
        kernel,
        out_shape=[
            jax.ShapeDtypeStruct((count, rows - 8, columns), bf16),
            jax.ShapeDtypeStruct((8, 128), f32),
        ],
    )(pieces)


def expert_outputs(pieces, rows_up, rows_down):
    wide, _, experts, half, part = pieces.shape
    width = wide * part
    split = rows_up - half

    def kernel(piece_ref, up_ref, down_ref):
        for z in range(wide):
            at = slice(z * part, (z + 1) * part)
            rest = piece_ref[z, 1, 0].astype(f32)
            up_ref[0, :half, at] = piece_ref[z, 0, 0].astype(f32)
            up_ref[0, half:, at] = rest[:split]
            down_ref[0, :, at] = rest[split:]

    return pl.pallas_call(
        kernel,
        grid=(experts,),
        in_specs=[pl.BlockSpec((wide, 2, 1, half, part), lambda e: (0, 0, e, 0, 0))],
        out_specs=[
            pl.BlockSpec((1, rows_up, width), lambda e: (e, 0, 0)),
            pl.BlockSpec((1, rows_down, width), lambda e: (e, 0, 0)),
        ],
        out_shape=[
            jax.ShapeDtypeStruct((experts, rows_up, width), f32),
            jax.ShapeDtypeStruct((experts, rows_down, width), f32),
        ],
    )(pieces)


def attention_outputs(pieces, widths):
    count, half, part = pieces.shape
    wide = count // 2

    def kernel(piece_ref, *out_refs):
        for h in range(2):
            for z in range(wide):
                left, right, base = z * part, (z + 1) * part, 0
                for ref, size in zip(out_refs, widths):
                    low, high = max(left, base), min(right, base + size)
                    if low < high:
                        ref[h * half : (h + 1) * half, low - base : high - base] = piece_ref[
                            h * wide + z, :, low - left : high - left
                        ].astype(f32)
                    base += size

    return pl.pallas_call(
        kernel,
        out_shape=[jax.ShapeDtypeStruct((2 * half, size), f32) for size in widths],
    )(pieces)


def spread(part, ways, axes):
    return exchange(jnp.broadcast_to(part[None], (ways, *part.shape)), axes)


def per_device(
    tokens,
    cotangent,
    seq_lengths,
    seq_order,
    routes,
    gate_weights,
    attn_gain,
    w_query,
    key_value_weight,
    w_out,
    ffn_gain,
    w_gateup,
    w_down,
):
    wide_z = lax.axis_size("z")
    shards = lax.axis_size("y") * lax.axis_size("x") * lax.axis_size("c")
    core = lax.axis_index("c")
    shard = (lax.axis_index("y") * lax.axis_size("x") + lax.axis_index("x")) * 2 + core
    rows, width = tokens.shape
    experts = w_gateup.shape[0]
    ff = w_gateup.shape[2] // 2
    kv_width = KEY_VALUE_HEADS * HEAD_SIZE
    scale = HEAD_SIZE ** (-0.5)

    qkv_full = lax.all_gather(
        jnp.concatenate([w_query, key_value_weight], 1), SHARD, axis=0, tiled=True
    )
    part = width // wide_z
    rows_out, rows_up, rows_down = w_out.shape[0], w_gateup.shape[1], w_down.shape[1]
    column = lax.axis_index("z") * part
    gains_own = jnp.pad(jnp.stack([attn_gain, ffn_gain]), ((0, 14), (0, part - attn_gain.shape[0])))
    out_and_gains = jnp.concatenate(
        [lax.dynamic_slice_in_dim(w_out, column, part, 1), gains_own], axis=0
    )
    parts = jnp.concatenate(
        [
            jnp.broadcast_to(out_and_gains[None], (experts, *out_and_gains.shape)),
            lax.dynamic_slice_in_dim(w_gateup, column, part, 2),
            lax.dynamic_slice_in_dim(w_down, column, part, 2),
        ],
        axis=1,
    )
    parts = exchange(parts, CHIPS)
    gains_mine = parts[:, rows_out : rows_out + 2, : attn_gain.shape[0]]
    gains = in_core_order(core, gains_mine, lax.ppermute(gains_mine, "c", SWAP))
    gains = gains.transpose(2, 0, 1, 3).reshape(2, width).astype(f32)
    gain_attn, gain_ffn = gains[0], gains[1]

    out_mine = in_z_order(gather_over_z(parts[:, :rows_out]))
    (out_full,) = assemble(out_mine, lax.ppermute(out_mine, "c", SWAP), (rows_out,))
    expert_mine = lax.all_gather(parts[:, rows_out + 16 :], "z", axis=0)
    gateup_full, down_full = assemble(
        expert_mine, lax.ppermute(expert_mine, "c", SWAP), (rows_up, rows_down)
    )

    chosen = routes[:, :, None] == jnp.arange(experts, dtype=jnp.int32)
    member = jnp.any(chosen, axis=1)
    weight = jnp.sum(jnp.where(chosen, gate_weights[:, :, None], 0.0), axis=1)
    place = jnp.cumsum(member.astype(jnp.int32), axis=0) - 1
    slot = jnp.where(member, place, -1).T
    picks = slot[:, None, :] == jnp.arange(CAP, dtype=jnp.int32)[None, :, None]
    pick = picks.astype(bf16).reshape(experts * CAP, rows)
    slot_weight = jnp.sum(jnp.where(picks, weight.T[:, None, :], 0.0), axis=2)
    upstream = cotangent.astype(f32)
    grad_out_sent = matmul(pick, cotangent) * slot_weight.reshape(-1, 1)
    grad_out = exchange(after(grad_out_sent.astype(bf16), parts), CHIPS)

    lengths = seq_lengths[0]
    starts = jnp.cumsum(lengths) - lengths
    row_at = shard * rows + jnp.arange(rows, dtype=jnp.int32)
    first_at = jnp.max(jnp.where(starts[None, :] <= row_at[:, None], starts[None, :], 0), axis=1)
    cosine, sine = rotary_tables(row_at - first_at)
    key_at = (shard - 1) * rows + jnp.arange(2 * rows, dtype=jnp.int32)
    allowed = (key_at[None, :] <= row_at[:, None]) & (key_at[None, :] >= first_at[:, None])

    wide = tokens.astype(f32)
    attn_factor = lax.rsqrt(jnp.mean(wide * wide, axis=-1, keepdims=True) + EPSILON)
    normed = after(wide * attn_factor * gain_attn, grad_out).astype(bf16)
    qkv = matmul(normed, qkv_full)
    turned = rotate(
        qkv[:, : width + kv_width].reshape(rows, QUERY_HEADS + KEY_VALUE_HEADS, HEAD_SIZE),
        cosine,
        sine,
    ).astype(bf16)
    queries = turned[:, :QUERY_HEADS].reshape(rows, KEY_VALUE_HEADS, GROUP, HEAD_SIZE)
    keyval = jnp.concatenate(
        [turned[:, QUERY_HEADS:].reshape(rows, kv_width), qkv[:, width + kv_width :].astype(bf16)],
        axis=1,
    )
    ring = [(i, (i + 1) % shards) for i in range(shards)]
    back_ring = [((i + 1) % shards, i) for i in range(shards)]
    keyval = jnp.concatenate([lax.ppermute(keyval, SHARD, ring), keyval], axis=0)
    keys = keyval[:, :kv_width].reshape(2 * rows, KEY_VALUE_HEADS, HEAD_SIZE)
    values = keyval[:, kv_width:].reshape(2 * rows, KEY_VALUE_HEADS, HEAD_SIZE)
    raw = jnp.einsum("sgrd,tgd->grst", queries, keys, preferred_element_type=f32)
    scores = jnp.where(allowed, raw * scale, -1000000000.0)
    exp_scores = jnp.exp(scores - jnp.max(scores, axis=-1, keepdims=True))
    probs = exp_scores / jnp.sum(exp_scores, axis=-1, keepdims=True)
    prob_low = probs.astype(bf16)
    mixed = jnp.einsum("grst,tgd->sgrd", prob_low, values, preferred_element_type=f32)
    attended = mixed.reshape(rows, width).astype(bf16)
    branch = matmul(attended, out_full).astype(bf16)
    residual = wide + branch.astype(f32)
    ffn_factor = lax.rsqrt(jnp.mean(residual * residual, axis=-1, keepdims=True) + EPSILON)
    normed_ffn = (residual * ffn_factor * gain_ffn).astype(bf16)

    picked = exchange(matmul(pick, normed_ffn).astype(bf16), CHIPS)
    normed_all = lax.all_gather(after(normed, picked), SHARD, axis=0, tiled=True)
    attended_cols = exchange(after(attended.T, picked), SHARD)
    attended_cols = attended_cols.reshape(shards, width // shards, rows)
    pre = matmul(picked, gateup_full)
    gate, up = pre[:, :ff], pre[:, ff:]
    sigmoid = jax.nn.sigmoid(gate)
    silu = gate * sigmoid
    acted = (silu * up).astype(bf16)
    grad_act = dot_general(grad_out, down_full, ((1,), (1,)))
    grad_gate = grad_act * up * sigmoid * (1.0 + gate * (1.0 - sigmoid))
    grad_pre = jnp.concatenate([grad_gate, grad_act * silu], axis=1).astype(bf16)
    grad_picked = dot_general(grad_pre, gateup_full, ((1,), (1,)))
    grad_picked_sent = after(grad_picked, attended_cols).astype(bf16)
    grad_picked = exchange(grad_picked_sent, CHIPS)
    acted, grad_pre = after(acted, grad_picked_sent), after(grad_pre, grad_picked_sent)
    expert_out = matmul(acted, down_full).astype(bf16)
    grad_down = dot_general(acted, grad_out, ((0,), (0,)))
    grad_gateup = dot_general(picked, grad_pre, ((0,), (0,)))

    here, there = cut_expert_grads(
        grad_gateup.astype(bf16), grad_down.astype(bf16), rows_up, rows_down, wide_z
    )
    other = lax.ppermute(there, "c", SWAP)
    expert_out = exchange(expert_out, CHIPS)
    pieces = (here.astype(f32) + other.astype(f32)).astype(bf16)
    over_rep = lax.psum_scatter(pieces, "z", scatter_dimension=0, tiled=False)

    back = pick.astype(f32) * slot_weight.reshape(-1, 1)
    back_high = back.astype(bf16)
    back_low = (back - back_high.astype(f32)).astype(bf16)
    mixture = dot_general(back_high, expert_out, ((0,), (0,)))
    mixture = mixture + dot_general(back_low, expert_out, ((0,), (0,)))
    output = (residual + mixture).astype(bf16)
    grad_ffn_in = after(dot_general(pick, grad_picked, ((0,), (0,))), other, normed_all)
    grad_from_norm, grad_gain_ffn = norm_back(residual, ffn_factor, gain_ffn, grad_ffn_in)
    grad_residual = upstream + grad_from_norm
    grad_branch = grad_residual.astype(bf16)
    grad_branch_all = lax.all_gather(grad_branch, SHARD, axis=0, tiled=True)

    grad_attended = dot_general(grad_branch, out_full, ((1,), (1,))).astype(bf16)
    grad_attended = grad_attended.reshape(rows, KEY_VALUE_HEADS, GROUP, HEAD_SIZE)
    grad_probs = jnp.einsum("sgrd,tgd->grst", grad_attended, values, preferred_element_type=f32)
    grad_values = jnp.einsum("grst,sgrd->tgd", prob_low, grad_attended, preferred_element_type=f32)
    inner = jnp.sum(probs * grad_probs, axis=-1, keepdims=True)
    grad_raw = (probs * (grad_probs - inner) * scale).astype(bf16)
    grad_queries = jnp.einsum("grst,tgd->sgrd", grad_raw, keys, preferred_element_type=f32)
    grad_keys = jnp.einsum("grst,sgrd->tgd", grad_raw, queries, preferred_element_type=f32)
    grad_keyval = jnp.concatenate(
        [grad_keys.reshape(2 * rows, kv_width), grad_values.reshape(2 * rows, kv_width)], axis=1
    )
    from_next = lax.ppermute(grad_keyval[:rows].astype(bf16), SHARD, back_ring)
    grad_keyval = grad_keyval[rows:] + from_next.astype(f32)
    grad_turned = jnp.concatenate(
        [grad_queries.reshape(rows, width), grad_keyval[:, :kv_width]], axis=1
    )
    grad_turned = grad_turned.reshape(rows, QUERY_HEADS + KEY_VALUE_HEADS, HEAD_SIZE)
    grad_qkv = jnp.concatenate(
        [
            rotate(grad_turned, cosine, -sine).reshape(rows, width + kv_width),
            grad_keyval[:, kv_width:],
        ],
        axis=1,
    ).astype(bf16)
    grad_normed = dot_general(grad_qkv, qkv_full, ((1,), (1,)))
    grad_in, grad_gain_attn = norm_back(wide, attn_factor, gain_attn, grad_normed)
    grad_tokens = (grad_residual + grad_in).astype(bf16)

    columns = grad_qkv.shape[1] // shards
    grad_qkv_cols = exchange(
        after(grad_qkv, expert_out).reshape(rows, shards, columns).transpose(1, 0, 2), SHARD
    )
    expert_pieces = exchange(sum_over_h(after(over_rep, grad_qkv_cols)), CHIPS)
    qkv_block = dot_general(
        normed_all, grad_qkv_cols.reshape(shards * rows, columns), ((0,), (0,))
    ).astype(bf16)
    shard_gateup, shard_down = expert_outputs(gather_over_rep(expert_pieces), rows_up, rows_down)

    out_rows = jnp.einsum(
        "jat,jtn->an",
        attended_cols,
        grad_branch_all.reshape(shards, rows, width),
        preferred_element_type=f32,
    ).astype(bf16)
    grad_gains = jnp.stack([grad_gain_attn, grad_gain_ffn]).reshape(2, shards, -1)
    gain_rows = jnp.pad(
        grad_gains.transpose(1, 0, 2).astype(bf16),
        ((0, 0), (0, 6), (0, columns - width // shards)),
    )
    qkv_block = jnp.concatenate(
        [qkv_block.reshape(shards, width // shards, columns), gain_rows], axis=1
    )
    qkv_blocks = exchange(after(qkv_block, expert_pieces), SHARD)
    attn_pieces = exchange(pack_attention_grads(qkv_blocks, out_rows, wide_z), REP)
    attn_copies, gain_sums = sum_and_copy(attn_pieces)
    grad_query, grad_keyval_w, grad_out_w = attention_outputs(
        exchange(attn_copies, REP), (width, 2 * kv_width, width)
    )
    grad_gains = gain_sums[:2, : width // shards]
    return (
        output,
        grad_tokens,
        grad_gains[0],
        grad_query,
        grad_keyval_w,
        grad_out_w,
        grad_gains[1],
        shard_gateup,
        shard_down,
    )


def solution(mesh):
    reps, shards = mesh.devices.shape
    fine = Mesh(mesh.devices.reshape(2, reps // 2, shards // 4, 2, 2), ALL)
    split = ALL
    placed = (
        P(split, None),
        P(split, None),
        P(REP, None),
        P(REP, None),
        P(split, None),
        P(split, None),
        P(SHARD),
        P(SHARD, None),
        P(SHARD, None),
        P(SHARD, None),
        P(SHARD),
        P(None, SHARD, None),
        P(None, SHARD, None),
    )
    return jax.shard_map(
        per_device,
        mesh=fine,
        in_specs=placed,
        out_specs=(
            P(split, None),
            P(split, None),
            P(SHARD),
            P(SHARD, None),
            P(SHARD, None),
            P(SHARD, None),
            P(SHARD),
            P(None, SHARD, None),
            P(None, SHARD, None),
        ),
        check_vma=False,
    )
```

```python
import jax
import jax.numpy as jnp
from jax import lax
from jax.experimental import pallas as pl
from jax.experimental.pallas import tpu as pltpu
from jax.sharding import Mesh, PartitionSpec as P

QUERY_HEADS = 12
KEY_VALUE_HEADS = 2
GROUP = QUERY_HEADS // KEY_VALUE_HEADS
HEAD_SIZE = 128
CAP = 80

EPSILON = 1e-06
ROPE_BASE = 10000.0
SCALE = HEAD_SIZE ** (-0.5)
SHARD = ("y", "x", "c")
CHIPS = ("y", "x")
REP = ("h", "z")
ALL = REP + SHARD
SWAP = [(0, 1), (1, 0)]

bf16 = jnp.bfloat16
f32 = jnp.float32

VMEM_LIMIT = 40 * 1024 * 1024
WHOLE = pl.BlockSpec(memory_space=pltpu.VMEM)
UNUSED = pl.BlockSpec(memory_space=pl.ANY)
SCALAR = pl.BlockSpec(memory_space=pltpu.SMEM)


def exchange(parts, axes):
    return lax.all_to_all(parts, axes, 0, 0, tiled=True)


def spread(part, ways, axes):
    return exchange(jnp.broadcast_to(part[None], (ways, *part.shape)), axes)


def matmul(left, right):
    return jnp.dot(left, right, preferred_element_type=f32)


def dot_general(left, right, dims):
    return lax.dot_general(left, right, (dims, ((), ())), preferred_element_type=f32)


def times_transposed(left, right):
    return dot_general(left, right, ((1,), (1,)))


def transposed_times(left, right):
    return dot_general(left, right, ((0,), (0,)))


def in_core_order(core, mine, other):
    return jnp.where(core == 0, jnp.stack([mine, other], 1), jnp.stack([other, mine], 1))


def call(kernel, out_shape, operands, earlier=(), specs=None, flops=0, scratch=()):
    specs = specs or [WHOLE] * len(operands)
    count = len(operands)

    def body(*refs):
        kernel(*refs[:count], *refs[count + len(earlier) :])

    size = sum(one.size * one.dtype.itemsize for one in (*operands, *out_shape))
    return pl.pallas_call(
        body,
        in_specs=[*specs, *([UNUSED] * len(earlier))],
        out_specs=[WHOLE] * len(out_shape),
        out_shape=out_shape,
        scratch_shapes=scratch,
        compiler_params=pltpu.CompilerParams(vmem_limit_bytes=VMEM_LIMIT),
        cost_estimate=pl.CostEstimate(flops=flops, bytes_accessed=size, transcendentals=0),
    )(*operands, *earlier)


def fetch(source_ref, to_ref, semaphores, along, base=0):
    rows, columns = to_ref.shape
    copies = []
    for i in range(to_ref.shape[along] // 512):
        chunk = pl.ds(i * 512, 512)
        if along:
            source = source_ref.at[:, pl.ds(base + i * 512, 512)]
            copy = pltpu.make_async_copy(source, to_ref.at[:, chunk], semaphores.at[i])
        else:
            source = source_ref.at[chunk, pl.ds(base, columns)]
            copy = pltpu.make_async_copy(source, to_ref.at[chunk, :], semaphores.at[i])
        copy.start()
        copies.append(copy)
    return copies


def shaped(shape, dtype):
    return jax.ShapeDtypeStruct(shape, dtype)


def inverse_rms(values):
    return lax.rsqrt(jnp.mean(values * values, axis=-1, keepdims=True) + EPSILON)


def norm_back(values, gain_row, upstream):
    factor = inverse_rms(values)
    grad_normed = upstream * gain_row
    grad_gain = jnp.sum(upstream * values * factor, axis=0, keepdims=True)
    cubed = factor * factor * factor
    grad_input = factor * grad_normed - values * cubed * jnp.mean(
        grad_normed * values, axis=-1, keepdims=True
    )
    return grad_input, grad_gain


def rotary_tables(position):
    half = HEAD_SIZE // 2
    frequency = ROPE_BASE ** (-jnp.arange(half, dtype=f32) / half)
    angle = position.astype(f32)[:, None] * frequency[None, :]
    cosine, sine = jnp.cos(angle), jnp.sin(angle)
    return jnp.concatenate([cosine, cosine], 1), jnp.concatenate([-sine, sine], 1)


def rotate(values, cosine, sine):
    return values * cosine + pltpu.roll(values, HEAD_SIZE // 2, 1) * sine


def project_qkv(tokens, gain, weights, cosine, sine, earlier):
    rows, width = tokens.shape
    kv_width = KEY_VALUE_HEADS * HEAD_SIZE
    turned = QUERY_HEADS + KEY_VALUE_HEADS
    total = width + 2 * kv_width

    def kernel(
        token_ref, gain_ref, all_ref, cos_ref, sin_ref, normed_ref, query_ref, keyval_ref, w_ref, sem
    ):
        copies = fetch(all_ref, w_ref, sem, 1)
        wide = token_ref[...].astype(f32)
        normed = (wide * inverse_rms(wide) * gain_ref[...]).astype(bf16)
        normed_ref[...] = normed
        cos, sin = cos_ref[...], sin_ref[...]
        for block in range(total // 256):
            if block % 2 == 0:
                copies[block // 2].wait()
            both = matmul(normed, w_ref[:, block * 256 : (block + 1) * 256])
            for i in range(2):
                head = 2 * block + i
                value = both[:, i * HEAD_SIZE : (i + 1) * HEAD_SIZE]
                if head < turned:
                    value = rotate(value, cos, sin)
                value = value.astype(bf16)
                if head < QUERY_HEADS:
                    query_ref[:, head * HEAD_SIZE : (head + 1) * HEAD_SIZE] = value
                else:
                    at = (head - QUERY_HEADS) * HEAD_SIZE
                    keyval_ref[:, at : at + HEAD_SIZE] = value

    return call(
        kernel,
        [
            shaped((rows, width), bf16),
            shaped((rows, width), bf16),
            shaped((rows, 2 * kv_width), bf16),
        ],
        (tokens, gain, weights, cosine, sine),
        earlier,
        specs=[WHOLE, WHOLE, UNUSED, WHOLE, WHOLE],
        flops=2 * rows * width * total,
        scratch=[pltpu.VMEM((width, total), bf16), pltpu.SemaphoreType.DMA((total // 512,))],
    )


def allowed_keys(first_ref, rows):
    row = lax.broadcasted_iota(jnp.int32, (rows, 2 * rows), 0)
    key = lax.broadcasted_iota(jnp.int32, (rows, 2 * rows), 1) - rows
    return (key <= row) & (key >= first_ref[...])


def probabilities(query, keys, allowed):
    scores = jnp.where(allowed, times_transposed(query, keys) * SCALE, -1000000000.0)
    exp_scores = jnp.exp(scores - jnp.max(scores, axis=-1, keepdims=True))
    return exp_scores / jnp.sum(exp_scores, axis=-1, keepdims=True)


def keys_and_values(before_ref, own_ref, group):
    both = []
    for base in (group * HEAD_SIZE, (KEY_VALUE_HEADS + group) * HEAD_SIZE):
        at = slice(base, base + HEAD_SIZE)
        both.append(jnp.concatenate([before_ref[:, at], own_ref[:, at]], axis=0))
    return both


def attend(queries, before, own, first, weights, tokens, gain):
    rows, width = tokens.shape

    def kernel(
        query_ref, before_ref, own_ref, first_ref, all_ref, token_ref, gain_ref,
        attended_ref, turned_ref, residual_ref, normed_ref, w_ref, sem,
    ):
        copies = fetch(all_ref, w_ref, sem, 1, weights.shape[1] - width)
        allowed = allowed_keys(first_ref, rows)
        for group in range(KEY_VALUE_HEADS):
            keys, values = keys_and_values(before_ref, own_ref, group)
            for head in range(group * GROUP, (group + 1) * GROUP):
                at = slice(head * HEAD_SIZE, (head + 1) * HEAD_SIZE)
                probs = probabilities(query_ref[:, at], keys, allowed)
                mixed = matmul(probs.astype(bf16), values)
                attended_ref[:, at] = mixed.astype(bf16)
                turned_ref[at, :] = mixed.T.astype(bf16)
        attended = attended_ref[...]
        for block in range(width // 256):
            at = slice(block * 256, (block + 1) * 256)
            if block % 2 == 0:
                copies[block // 2].wait()
            branch = matmul(attended, w_ref[:, at]).astype(bf16)
            residual_ref[:, at] = token_ref[:, at].astype(f32) + branch.astype(f32)
        residual = residual_ref[...]
        normed_ref[...] = (residual * inverse_rms(residual) * gain_ref[...]).astype(bf16)

    return call(
        kernel,
        [
            shaped((rows, width), bf16),
            shaped((width, rows), bf16),
            shaped((rows, width), f32),
            shaped((rows, width), bf16),
        ],
        (queries, before, own, first, weights, tokens, gain),
        specs=[WHOLE, WHOLE, WHOLE, WHOLE, UNUSED, WHOLE, WHOLE],
        flops=2 * rows * width * width + 8 * rows * rows * width,
        scratch=[pltpu.VMEM((width, width), bf16), pltpu.SemaphoreType.DMA((width // 512,))],
    )


def pick_rows(pick, rows_in, earlier):
    slots, width = pick.shape[0], rows_in.shape[1]

    def kernel(pick_ref, in_ref, out_ref):
        for block in range(width // 512):
            at = slice(block * 512, (block + 1) * 512)
            out_ref[:, at] = matmul(pick_ref[...], in_ref[:, at]).astype(bf16)

    return call(
        kernel,
        [shaped((slots, width), bf16)],
        (pick, rows_in),
        earlier,
        flops=2 * slots * rows_in.size,
    )[0]


def run_experts(picked, grad_out, mine, other, rows_up, rows_down):
    slots, width = picked.shape
    wide = len(mine)
    chips, _, part = mine[0].shape
    ff = chips * 2 * rows_down
    place = jnp.stack([lax.axis_index("c"), lax.axis_index("z")]).astype(jnp.int32)

    def kernel(picked_ref, grad_ref, place_ref, *refs):
        mine_refs, other_refs = refs[:wide], refs[wide : 2 * wide]
        acted_ref, pre_ref, back_ref, down_w = refs[2 * wide : 2 * wide + 4]
        up_w, gate_ref, upper_ref, up_sem, down_sem = refs[2 * wide + 4 :]
        core = place_ref[0]
        ups, downs = [], []
        for k in range(wide):
            to = pl.ds(pl.multiple_of((place_ref[1] ^ k) * part, 128), part)
            for i, (owner, part_ref) in enumerate(((core, mine_refs[k]), (1 - core, other_refs[k]))):
                ups.append(
                    pltpu.make_async_copy(
                        part_ref.at[:, pl.ds(0, rows_up), :],
                        up_w.at[:, owner, :, to],
                        up_sem.at[2 * k + i],
                    )
                )
                downs.append(
                    pltpu.make_async_copy(
                        part_ref.at[:, pl.ds(rows_up, rows_down), :],
                        down_w.at[:, owner, :, to],
                        down_sem.at[2 * k + i],
                    )
                )
        for copy in ups + downs:
            copy.start()
        for copy in ups:
            copy.wait()

        @pl.loop(0, ff // 256)
        def _(j):
            at = pl.multiple_of(j * 256, 256)
            for base, ref in ((0, gate_ref), (ff, upper_ref)):
                weights = up_w[:, :, :, pl.ds(base + at, 256)].reshape(width, 256)
                ref[:, pl.ds(at, 256)] = matmul(picked_ref[...], weights)

        for copy in downs:
            copy.wait()
        half = chips // 2

        @pl.loop(0, 2)
        def _(j):
            at = pl.ds(pl.multiple_of(j * (ff // 2), 128), ff // 2)
            weights = down_w[pl.ds(j * half, half)].reshape(ff // 2, width)
            grad_act = times_transposed(grad_ref[...], weights)
            gate, up = gate_ref[:, at], upper_ref[:, at]
            sigmoid = 1.0 / (1.0 + jnp.exp(-gate))
            silu = gate * sigmoid
            acted_ref[:, at] = (silu * up).astype(bf16)
            grad_gate = grad_act * up * sigmoid * (1.0 + gate * (1.0 - sigmoid))
            pre_ref[:, at] = grad_gate.astype(bf16)
            upper = pl.ds(pl.multiple_of(ff + j * (ff // 2), 128), ff // 2)
            pre_ref[:, upper] = (grad_act * silu).astype(bf16)

        @pl.loop(0, 2)
        def _(j):
            weights = up_w[pl.ds(j * half, half)].reshape(width // 2, 2 * ff)
            to = pl.ds(pl.multiple_of(j * (width // 2), 128), width // 2)
            back_ref[:, to] = times_transposed(pre_ref[...], weights).astype(bf16)

    return call(
        kernel,
        [
            shaped((slots, ff), bf16),
            shaped((slots, 2 * ff), bf16),
            shaped((slots, width), bf16),
            shaped((chips, 2, rows_down, width), bf16),
        ],
        (picked, grad_out, place, *mine, *other),
        specs=[WHOLE, WHOLE, SCALAR, *([UNUSED] * (2 * wide))],
        flops=2 * slots * 5 * width * ff,
        scratch=[
            pltpu.VMEM((chips, 2, rows_up, width), bf16),
            pltpu.VMEM((slots, ff), f32),
            pltpu.VMEM((slots, ff), f32),
            pltpu.SemaphoreType.DMA((2 * wide,)),
            pltpu.SemaphoreType.DMA((2 * wide,)),
        ],
    )


def expert_weight_grads(picked, grad_pre, acted, grad_out, down, rows_up, chips, wide, earlier):
    slots, width = picked.shape
    rows_down = down.shape[0] // (2 * chips)
    half, part = (rows_up + rows_down) // 2, width // wide
    steps = 2
    near = chips // steps
    core = lax.axis_index("c").astype(jnp.int32).reshape(1)

    def kernel(core_ref, picked_ref, pre_ref, acted_ref, grad_ref, all_ref, down_ref, *refs):
        here_ref, there_ref, expert_ref, keep_ref = refs[-4:]
        expert_ref[...] = matmul(all_ref[...], down_ref[...]).astype(bf16)
        columns = width // 2
        for n in range(2):
            at = slice(n * columns, (n + 1) * columns)
            for m in range(near // 2):
                block = slice(m * 4 * rows_up, (m + 1) * 4 * rows_up)
                up = transposed_times(picked_ref[:, block], pre_ref[:, at])
                for i in range(4):
                    k, c = 2 * m + i // 2, i % 2
                    keep_ref[k, c] = up[i * rows_up : (i + 1) * rows_up]
            down = transposed_times(acted_ref[...], grad_ref[:, at])
            for k in range(near):
                for c in range(2):
                    base = (2 * k + c) * rows_down
                    up = keep_ref[k, c]
                    first = up[:half].astype(bf16)
                    rest = jnp.concatenate([up[half:], down[base : base + rows_down]], axis=0)
                    rest = rest.astype(bf16)
                    for mine, out_ref in ((True, here_ref), (False, there_ref)):

                        @pl.when((core_ref[0] == c) == mine)
                        def _():
                            for i in range(columns // part):
                                cut = slice(i * part, (i + 1) * part)
                                z = n * (columns // part) + i
                                out_ref[z, 0, k] = first[:, cut]
                                out_ref[z, 1, k] = rest[:, cut]

    pieces = pl.BlockSpec((wide, 2, near, half, part), lambda s: (0, 0, s, 0, 0))
    return pl.pallas_call(
        kernel,
        grid=(steps,),
        in_specs=[
            SCALAR,
            pl.BlockSpec((slots, width // steps), lambda s: (0, s)),
            pl.BlockSpec(grad_pre.shape, lambda s: (0, 0)),
            pl.BlockSpec((slots, acted.shape[1] // steps), lambda s: (0, s)),
            pl.BlockSpec(grad_out.shape, lambda s: (0, 0)),
            pl.BlockSpec(acted.shape, lambda s: (0, 0)),
            pl.BlockSpec((down.shape[0], width // steps), lambda s: (0, s)),
            *([UNUSED] * len(earlier)),
        ],
        out_specs=[pieces, pieces, pl.BlockSpec((slots, width // steps), lambda s: (0, s))],
        out_shape=[
            *([shaped((wide, 2, chips, half, part), bf16)] * 2),
            shaped((slots, width), bf16),
        ],
        scratch_shapes=[pltpu.VMEM((near, 2, rows_up, width // 2), f32)],
        compiler_params=pltpu.CompilerParams(vmem_limit_bytes=VMEM_LIMIT),
        cost_estimate=pl.CostEstimate(
            flops=2 * slots * 4 * width * acted.shape[1],
            bytes_accessed=4 * 4 * slots * width,
            transcendentals=0,
        ),
    )(core, picked, grad_pre, acted, grad_out, acted, down, *earlier)


def residual_grad(pick, grad_picked, residual, gain, cotangent, earlier):
    rows, width = residual.shape

    def kernel(pick_ref, back_ref, residual_ref, gain_ref, cot_ref, grad_ref, branch_ref, gain_grad_ref):
        for block in range(width // 512):
            at = slice(block * 512, (block + 1) * 512)
            grad_ref[:, at] = transposed_times(pick_ref[...], back_ref[:, at])
        grad, grad_gain = norm_back(residual_ref[...], gain_ref[...], grad_ref[...])
        grad = grad + cot_ref[...].astype(f32)
        grad_ref[...] = grad
        branch_ref[...] = grad.astype(bf16)
        gain_grad_ref[...] = grad_gain

    return call(
        kernel,
        [shaped((rows, width), f32), shaped((rows, width), bf16), shaped((1, width), f32)],
        (pick, grad_picked, residual, gain, cotangent),
        earlier,
        flops=2 * grad_picked.size * rows,
    )


def attend_back(grad_branch, weights, queries, before, own, first, cosine, sine):
    rows, width = grad_branch.shape
    kv_width = KEY_VALUE_HEADS * HEAD_SIZE

    def kernel(
        grad_ref, all_ref, query_ref, before_ref, own_ref, first_ref, cos_ref, sin_ref,
        out_ref, prev_ref, self_ref, attended_ref, w_ref, sem,
    ):
        copies = fetch(all_ref, w_ref, sem, 0, weights.shape[1] - width)
        for block in range(width // 256):
            if block % 2 == 0:
                copies[block // 2].wait()
            at = slice(block * 256, (block + 1) * 256)
            attended_ref[:, at] = times_transposed(grad_ref[...], w_ref[at, :]).astype(bf16)
        allowed = allowed_keys(first_ref, rows)
        cos, sin = cos_ref[...], sin_ref[...]
        for group in range(KEY_VALUE_HEADS):
            keys, values = keys_and_values(before_ref, own_ref, group)
            raws, lows, uppers, asked = [], [], [], []
            for head in range(group * GROUP, (group + 1) * GROUP):
                at = slice(head * HEAD_SIZE, (head + 1) * HEAD_SIZE)
                query, upper = query_ref[:, at], attended_ref[:, at]
                probs = probabilities(query, keys, allowed)
                grad_probs = times_transposed(upper, values)
                inner = jnp.sum(probs * grad_probs, axis=-1, keepdims=True)
                raw = (probs * (grad_probs - inner) * SCALE).astype(bf16)
                out_ref[head] = rotate(matmul(raw, keys), cos, -sin).astype(bf16)
                raws.append(raw)
                lows.append(probs.astype(bf16))
                uppers.append(upper)
                asked.append(query)
            for base, lefts, rights in (
                (group * HEAD_SIZE, raws, asked),
                (kv_width + group * HEAD_SIZE, lows, uppers),
            ):
                grad = transposed_times(
                    jnp.concatenate(lefts, axis=0), jnp.concatenate(rights, axis=0)
                )
                prev_ref[:, base : base + HEAD_SIZE] = grad[:rows].astype(bf16)
                self_ref[:, base : base + HEAD_SIZE] = grad[rows:]

    return call(
        kernel,
        [
            shaped((QUERY_HEADS, rows, HEAD_SIZE), bf16),
            shaped((rows, 2 * kv_width), bf16),
            shaped((rows, 2 * kv_width), f32),
        ],
        (grad_branch, weights, queries, before, own, first, cosine, sine),
        specs=[WHOLE, UNUSED, *([WHOLE] * 6)],
        flops=2 * rows * width * width + 20 * rows * rows * width,
        scratch=[
            pltpu.VMEM((rows, width), bf16),
            pltpu.VMEM((width, width), bf16),
            pltpu.SemaphoreType.DMA((width // 512,)),
        ],
    )


def qkv_blocks_of(grad_queries, grad_own, from_next, cosine, sine, earlier):
    heads, rows, size = grad_queries.shape
    total = heads + 2 * KEY_VALUE_HEADS

    def kernel(query_ref, own_ref, next_ref, cos_ref, sin_ref, out_ref):
        out_ref[:heads] = query_ref[...]
        for i in range(2 * KEY_VALUE_HEADS):
            at = slice(i * size, (i + 1) * size)
            grad = own_ref[:, at] + next_ref[:, at].astype(f32)
            if i < KEY_VALUE_HEADS:
                grad = rotate(grad, cos_ref[...], -sin_ref[...])
            out_ref[heads + i] = grad.astype(bf16)

    return call(
        kernel,
        [shaped((total, rows, size), bf16)],
        (grad_queries, grad_own, from_next, cosine, sine),
        earlier,
    )[0]


def input_grad(blocks, weights, tokens, gain, grad_residual):
    rows, width = tokens.shape
    columns = blocks.shape[0] * HEAD_SIZE

    def kernel(
        block_ref, all_ref, token_ref, gain_ref, residual_ref, out_ref, gain_grad_ref, w_ref, sem
    ):
        copies = fetch(all_ref, w_ref, sem, 1)
        total = jnp.zeros((rows, width), f32)
        for i in range(blocks.shape[0] // 2):
            if i % 2 == 0:
                copies[i // 2].wait()
            pair = jnp.concatenate([block_ref[2 * i], block_ref[2 * i + 1]], axis=1)
            total = total + times_transposed(pair, w_ref[:, i * 256 : (i + 1) * 256])
        grad, grad_gain = norm_back(token_ref[...].astype(f32), gain_ref[...], total)
        out_ref[...] = (residual_ref[...] + grad).astype(bf16)
        gain_grad_ref[...] = grad_gain

    return call(
        kernel,
        [shaped((rows, width), bf16), shaped((1, width), f32)],
        (blocks, weights, tokens, gain, grad_residual),
        specs=[WHOLE, UNUSED, WHOLE, WHOLE, WHOLE],
        flops=2 * rows * width * columns,
        scratch=[pltpu.VMEM((width, columns), bf16), pltpu.SemaphoreType.DMA((columns // 512,))],
    )


def gather_over_z(part):
    wide = lax.axis_size("z")
    return [part] + [
        lax.ppermute(part, "z", [(i, i ^ k) for i in range(wide)]) for k in range(1, wide)
    ]


def gather_over_rep(piece):
    wide = lax.axis_size("z")
    ways = 2 * wide
    moved = []
    for k in range(wide):
        for j in range(2):
            step = j * wide + k
            moved.append(
                lax.ppermute(piece, REP, [(i, i ^ step) for i in range(ways)]) if step else piece
            )
    return moved


def expert_outputs(moved, rows_up, rows_down):
    wide = len(moved) // 2
    experts, half, part = moved[0].shape
    width = wide * part
    split = rows_up - half
    place = jnp.stack([lax.axis_index("h"), lax.axis_index("z")]).astype(jnp.int32)

    def kernel(place_ref, *refs):
        up_ref, down_ref = refs[2 * wide :]
        low = place_ref[0] == 0
        for k in range(wide):
            at = pl.ds(pl.multiple_of((place_ref[1] ^ k) * part, 128), part)
            same, other = refs[2 * k][0].astype(f32), refs[2 * k + 1][0].astype(f32)
            rest = jnp.where(low, other, same)
            up_ref[0, :half, at] = jnp.where(low, same, other)
            up_ref[0, half:, at] = rest[:split]
            down_ref[0, :, at] = rest[split:]

    return pl.pallas_call(
        kernel,
        grid_spec=pltpu.PrefetchScalarGridSpec(
            num_scalar_prefetch=1,
            grid=(experts,),
            in_specs=[pl.BlockSpec((1, half, part), lambda e, p: (e, 0, 0))] * (2 * wide),
            out_specs=[
                pl.BlockSpec((1, rows_up, width), lambda e, p: (e, 0, 0)),
                pl.BlockSpec((1, rows_down, width), lambda e, p: (e, 0, 0)),
            ],
        ),
        out_shape=[
            shaped((experts, rows_up, width), f32),
            shaped((experts, rows_down, width), f32),
        ],
    )(place, *moved)


def after(value, *earlier):
    for one in earlier:
        zero = jnp.minimum(jnp.abs(one[(0,) * one.ndim].astype(f32)), 0.0)
        value = value + zero.astype(value.dtype)
    return value


def pack_attention_grads(blocks, out_rows, wide, earlier):
    count, rows, column = blocks.shape
    rows -= 8
    half = rows // 2
    total = count + out_rows.shape[1] // column
    each = total // wide

    def kernel(block_ref, out_ref, piece_ref):
        piece_ref[...] = jnp.zeros_like(piece_ref)
        gains = block_ref[0, rows:].astype(f32)
        for b in range(1, count):
            gains = gains + block_ref[b, rows:].astype(f32)
        for h in range(2):
            at = slice(h * half, (h + 1) * half)
            for b in range(total):
                if b < count:
                    value = block_ref[b, at]
                else:
                    value = out_ref[at, (b - count) * column : (b - count + 1) * column]
                to = (b % each) * column
                piece_ref[h * wide + b // each, :half, to : to + column] = value
        for p in range(2 * wide):
            piece_ref[p, half:, :column] = gains.astype(bf16)

    return call(
        kernel, [shaped((2 * wide, half + 8, each * column), bf16)], (blocks, out_rows), earlier
    )[0]


def sum_and_copy(pieces):
    count, rows, columns = pieces.shape

    def kernel(piece_ref, copy_ref, gain_ref):
        total = piece_ref[0].astype(f32)
        for p in range(1, count):
            total = total + piece_ref[p].astype(f32)
        gain_ref[...] = total[rows - 8 :, :128]
        low = total[: rows - 8].astype(bf16)
        for p in range(count):
            copy_ref[p] = low

    return pl.pallas_call(
        kernel,
        out_shape=[
            jax.ShapeDtypeStruct((count, rows - 8, columns), bf16),
            jax.ShapeDtypeStruct((8, 128), f32),
        ],
    )(pieces)


def attention_outputs(pieces, widths):
    count, half, part = pieces.shape
    wide = count // 2

    def kernel(piece_ref, *out_refs):
        for h in range(2):
            for z in range(wide):
                left, right, base = z * part, (z + 1) * part, 0
                for ref, size in zip(out_refs, widths):
                    low, high = max(left, base), min(right, base + size)
                    if low < high:
                        ref[h * half : (h + 1) * half, low - base : high - base] = piece_ref[
                            h * wide + z, :, low - left : high - left
                        ].astype(f32)
                    base += size

    return pl.pallas_call(
        kernel,
        out_shape=[jax.ShapeDtypeStruct((2 * half, size), f32) for size in widths],
    )(pieces)


def per_device(
    tokens,
    cotangent,
    seq_lengths,
    seq_order,
    routes,
    gate_weights,
    attn_gain,
    w_query,
    key_value_weight,
    w_out,
    ffn_gain,
    w_gateup,
    w_down,
):
    wide_z = lax.axis_size("z")
    shards = lax.axis_size("y") * lax.axis_size("x") * lax.axis_size("c")
    core = lax.axis_index("c")
    shard = (lax.axis_index("y") * lax.axis_size("x") + lax.axis_index("x")) * 2 + core
    rows, width = tokens.shape
    experts = w_gateup.shape[0]
    kv_width = KEY_VALUE_HEADS * HEAD_SIZE
    owned = width // shards

    attn_full = lax.all_gather(
        jnp.concatenate([w_query, key_value_weight, w_out], 1), SHARD, axis=0, tiled=True
    )
    part = width // wide_z
    rows_up, rows_down = w_gateup.shape[1], w_down.shape[1]
    column = lax.axis_index("z") * part
    gains_own = jnp.pad(jnp.stack([attn_gain, ffn_gain]), ((0, 14), (0, part - owned)))
    parts = jnp.concatenate(
        [
            lax.dynamic_slice_in_dim(w_gateup, column, part, 2),
            lax.dynamic_slice_in_dim(w_down, column, part, 2),
            jnp.broadcast_to(gains_own[None], (experts, *gains_own.shape)),
        ],
        axis=1,
    )
    parts = exchange(parts, CHIPS)
    gains_mine = parts[:, rows_up + rows_down : rows_up + rows_down + 2, :owned]
    gains = in_core_order(core, gains_mine, lax.ppermute(gains_mine, "c", SWAP))
    gains = gains.transpose(2, 0, 1, 3).reshape(2, width).astype(f32)
    gain_attn, gain_ffn = gains[:1], gains[1:]
    expert_mine = gather_over_z(parts)
    expert_other = [lax.ppermute(one, "c", SWAP) for one in expert_mine]

    chosen = routes[:, :, None] == jnp.arange(experts, dtype=jnp.int32)
    member = jnp.any(chosen, axis=1)
    weight = jnp.sum(jnp.where(chosen, gate_weights[:, :, None], 0.0), axis=1)
    place = jnp.cumsum(member.astype(jnp.int32), axis=0) - 1
    slot = jnp.where(member, place, -1).T
    picks = slot[:, None, :] == jnp.arange(CAP, dtype=jnp.int32)[None, :, None]
    pick = picks.astype(bf16).reshape(experts * CAP, rows)
    slot_weight = jnp.sum(jnp.where(picks, weight.T[:, None, :], 0.0), axis=2)
    grad_out = matmul(pick, cotangent) * slot_weight.reshape(-1, 1)
    grad_out = exchange(after(grad_out, parts).astype(bf16), CHIPS)

    lengths = seq_lengths[0]
    starts = jnp.cumsum(lengths) - lengths
    row_at = shard * rows + jnp.arange(rows, dtype=jnp.int32)
    first_at = jnp.max(jnp.where(starts[None, :] <= row_at[:, None], starts[None, :], 0), axis=1)
    cosine, sine = rotary_tables(row_at - first_at)
    first = (first_at - shard * rows).astype(jnp.int32)[:, None]
    normed, queries, keyval = project_qkv(
        tokens, gain_attn, attn_full, cosine, sine, (grad_out,)
    )
    ring = [(i, (i + 1) % shards) for i in range(shards)]
    back_ring = [((i + 1) % shards, i) for i in range(shards)]
    before = lax.ppermute(keyval, SHARD, ring)
    attended, attended_turned, residual, normed_ffn = attend(
        queries, before, keyval, first, attn_full, tokens, gain_ffn
    )

    picked = exchange(pick_rows(pick, normed_ffn, tuple(expert_other)), CHIPS)
    normed_all = lax.all_gather(after(normed, picked), SHARD, axis=0, tiled=True)
    attended_cols = exchange(after(attended_turned, picked), SHARD)
    attended_cols = attended_cols.reshape(shards, owned, rows)
    acted, grad_pre, grad_picked, down = run_experts(
        picked, grad_out, expert_mine, expert_other, rows_up, rows_down
    )
    grad_picked_back = exchange(grad_picked, CHIPS)
    here, there, expert_out = expert_weight_grads(
        picked,
        grad_pre,
        acted,
        grad_out,
        down.reshape(-1, width),
        rows_up,
        experts,
        wide_z,
        (grad_picked, attended_cols),
    )
    other = lax.ppermute(there, "c", SWAP)
    pieces = (here.astype(f32) + other.astype(f32)).astype(bf16)
    over_z = lax.psum_scatter(pieces, "z", scatter_dimension=0, tiled=False)

    grad_residual, grad_branch, grad_gain_ffn = residual_grad(
        pick, grad_picked_back, residual, gain_ffn, cotangent, (here, normed_all)
    )
    grad_branch_all = lax.all_gather(grad_branch, SHARD, axis=0, tiled=True)
    grad_queries, grad_before, grad_own = attend_back(
        grad_branch, attn_full, queries, before, keyval, first, cosine, sine
    )
    from_next = lax.ppermute(grad_before, SHARD, back_ring)
    expert_out = exchange(expert_out, CHIPS)
    grad_blocks = qkv_blocks_of(
        grad_queries, grad_own, from_next, cosine, sine, (expert_out,)
    )
    grad_tokens, grad_gain_attn = input_grad(
        grad_blocks, attn_full, tokens, gain_attn, grad_residual
    )

    grad_cols = exchange(grad_blocks, SHARD)
    over_z = over_z.reshape(2 * experts, *over_z.shape[2:])
    over_rep = exchange(over_z, ("h", *CHIPS)).reshape(2, experts, *over_z.shape[1:])
    over_rep = (over_rep[0].astype(f32) + over_rep[1].astype(f32)).astype(bf16)
    moved = gather_over_rep(over_rep)
    shard_gateup, shard_down = expert_outputs(moved, rows_up, rows_down)
    qkv_block = transposed_times(normed_all, grad_cols.reshape(shards * rows, HEAD_SIZE))
    grad_gains = jnp.concatenate([grad_gain_attn, grad_gain_ffn]).reshape(2, shards, owned)
    gain_rows = jnp.pad(
        grad_gains.transpose(1, 0, 2).astype(bf16), ((0, 0), (0, 6), (0, HEAD_SIZE - owned))
    )
    qkv_block = jnp.concatenate(
        [qkv_block.astype(bf16).reshape(shards, owned, HEAD_SIZE), gain_rows], axis=1
    )
    out_rows = jnp.einsum(
        "jat,jtn->an",
        attended_cols,
        grad_branch_all.reshape(shards, rows, width),
        preferred_element_type=f32,
    ).astype(bf16)
    qkv_blocks = exchange(after(qkv_block, over_rep), SHARD)
    attn_pieces = exchange(pack_attention_grads(qkv_blocks, out_rows, wide_z, moved[1:4]), REP)
    attn_copies, gain_sums = sum_and_copy(attn_pieces)
    grad_query, grad_keyval, grad_out_w = attention_outputs(
        exchange(attn_copies, REP), (width, 2 * kv_width, width)
    )

    back = pick.astype(f32) * slot_weight.reshape(-1, 1)
    back_high = back.astype(bf16)
    back_low = (back - back_high.astype(f32)).astype(bf16)
    mixture = transposed_times(back_high, expert_out) + transposed_times(back_low, expert_out)
    output = (residual + mixture).astype(bf16)
    return (
        output,
        grad_tokens,
        gain_sums[0, :owned],
        grad_query,
        grad_keyval,
        grad_out_w,
        gain_sums[1, :owned],
        shard_gateup,
        shard_down,
    )


def solution(mesh):
    reps, shards = mesh.devices.shape
    fine = Mesh(mesh.devices.reshape(2, reps // 2, shards // 4, 2, 2), ALL)
    split = ALL
    placed = (
        P(split, None),
        P(split, None),
        P(REP, None),
        P(REP, None),
        P(split, None),
        P(split, None),
        P(SHARD),
        P(SHARD, None),
        P(SHARD, None),
        P(SHARD, None),
        P(SHARD),
        P(None, SHARD, None),
        P(None, SHARD, None),
    )
    return jax.shard_map(
        per_device,
        mesh=fine,
        in_specs=placed,
        out_specs=(
            P(split, None),
            P(split, None),
            P(SHARD),
            P(SHARD, None),
            P(SHARD, None),
            P(SHARD, None),
            P(SHARD),
            P(None, SHARD, None),
            P(None, SHARD, None),
        ),
        check_vma=False,
    )
```

```python
import jax
import jax.numpy as jnp
from jax import lax
from jax.experimental import pallas as pl
from jax.experimental.pallas import tpu as pltpu
from jax.sharding import Mesh, PartitionSpec as P

QUERY_HEADS = 12
KEY_VALUE_HEADS = 2
GROUP = QUERY_HEADS // KEY_VALUE_HEADS
HEAD_SIZE = 128
CAP = 80

EPSILON = 1e-06
ROPE_BASE = 10000.0
SCALE = HEAD_SIZE ** (-0.5)
SHARD = ("y", "x", "c")
CHIPS = ("y", "x")
REP = ("h", "z")
ALL = REP + SHARD
SWAP = [(0, 1), (1, 0)]

bf16 = jnp.bfloat16
f32 = jnp.float32

VMEM_LIMIT = 60 * 1024 * 1024
WHOLE = pl.BlockSpec(memory_space=pltpu.VMEM)
UNUSED = pl.BlockSpec(memory_space=pl.ANY)
SCALAR = pl.BlockSpec(memory_space=pltpu.SMEM)


def exchange(parts, axes):
    return lax.all_to_all(parts, axes, 0, 0, tiled=True)


def spread(part, ways, axes):
    return exchange(jnp.broadcast_to(part[None], (ways, *part.shape)), axes)


def matmul(left, right):
    return jnp.dot(left, right, preferred_element_type=f32)


def dot_general(left, right, dims):
    return lax.dot_general(left, right, (dims, ((), ())), preferred_element_type=f32)


def times_transposed(left, right):
    return dot_general(left, right, ((1,), (1,)))


def transposed_times(left, right):
    return dot_general(left, right, ((0,), (0,)))


def in_core_order(core, mine, other):
    return jnp.where(core == 0, jnp.stack([mine, other], 1), jnp.stack([other, mine], 1))


def call(kernel, out_shape, operands, earlier=(), specs=None, flops=0, scratch=()):
    specs = specs or [WHOLE] * len(operands)
    count = len(operands)

    def body(*refs):
        kernel(*refs[:count], *refs[count + len(earlier) :])

    size = sum(one.size * one.dtype.itemsize for one in (*operands, *out_shape))
    return pl.pallas_call(
        body,
        in_specs=[*specs, *([UNUSED] * len(earlier))],
        out_specs=[WHOLE] * len(out_shape),
        out_shape=out_shape,
        scratch_shapes=scratch,
        compiler_params=pltpu.CompilerParams(vmem_limit_bytes=VMEM_LIMIT),
        cost_estimate=pl.CostEstimate(flops=flops, bytes_accessed=size, transcendentals=0),
    )(*operands, *earlier)


def fetch(source_ref, to_ref, semaphores, along, base=0):
    rows, columns = to_ref.shape
    copies = []
    for i in range(to_ref.shape[along] // 512):
        chunk = pl.ds(i * 512, 512)
        if along:
            source = source_ref.at[:, pl.ds(base + i * 512, 512)]
            copy = pltpu.make_async_copy(source, to_ref.at[:, chunk], semaphores.at[i])
        else:
            source = source_ref.at[chunk, pl.ds(base, columns)]
            copy = pltpu.make_async_copy(source, to_ref.at[chunk, :], semaphores.at[i])
        copy.start()
        copies.append(copy)
    return copies


def fetch_parts(place_ref, mine_refs, other_refs, to_ref, semaphores):
    rows = to_ref.shape[2]
    part = to_ref.shape[3] // len(mine_refs)
    copies = []
    for k in range(len(mine_refs)):
        to = pl.ds(pl.multiple_of((place_ref[1] ^ k) * part, 128), part)
        owners = ((place_ref[0], mine_refs[k]), (1 - place_ref[0], other_refs[k]))
        for i, (owner, part_ref) in enumerate(owners):
            copy = pltpu.make_async_copy(
                part_ref.at[:, pl.ds(0, rows), :],
                to_ref.at[:, owner, :, to],
                semaphores.at[2 * k + i],
            )
            copy.start()
            copies.append(copy)
    return copies


def device_place():
    return jnp.stack([lax.axis_index("c"), lax.axis_index("z")]).astype(jnp.int32)


def shaped(shape, dtype):
    return jax.ShapeDtypeStruct(shape, dtype)


def inverse_rms(values):
    return lax.rsqrt(jnp.mean(values * values, axis=-1, keepdims=True) + EPSILON)


def norm_back(values, gain_row, upstream):
    factor = inverse_rms(values)
    grad_normed = upstream * gain_row
    grad_gain = jnp.sum(upstream * values * factor, axis=0, keepdims=True)
    cubed = factor * factor * factor
    grad_input = factor * grad_normed - values * cubed * jnp.mean(
        grad_normed * values, axis=-1, keepdims=True
    )
    return grad_input, grad_gain


def rotary_tables(position):
    half = HEAD_SIZE // 2
    frequency = ROPE_BASE ** (-jnp.arange(half, dtype=f32) / half)
    angle = position.astype(f32)[:, None] * frequency[None, :]
    cosine, sine = jnp.cos(angle), jnp.sin(angle)
    return jnp.concatenate([cosine, cosine], 1), jnp.concatenate([-sine, sine], 1)


def rotate(values, cosine, sine):
    return values * cosine + pltpu.roll(values, HEAD_SIZE // 2, 1) * sine


def project_qkv(tokens, gain, weights, cosine, sine, earlier):
    rows, width = tokens.shape
    kv_width = KEY_VALUE_HEADS * HEAD_SIZE
    turned = QUERY_HEADS + KEY_VALUE_HEADS
    total = width + 2 * kv_width

    def kernel(
        token_ref, gain_ref, all_ref, cos_ref, sin_ref, normed_ref, query_ref, keyval_ref, w_ref, sem
    ):
        copies = fetch(all_ref, w_ref, sem, 1)
        wide = token_ref[...].astype(f32)
        normed = (wide * inverse_rms(wide) * gain_ref[...]).astype(bf16)
        normed_ref[...] = normed
        cos, sin = cos_ref[...], sin_ref[...]
        for block in range(total // 256):
            if block % 2 == 0:
                copies[block // 2].wait()
            both = matmul(normed, w_ref[:, block * 256 : (block + 1) * 256])
            for i in range(2):
                head = 2 * block + i
                value = both[:, i * HEAD_SIZE : (i + 1) * HEAD_SIZE]
                if head < turned:
                    value = rotate(value, cos, sin)
                value = value.astype(bf16)
                if head < QUERY_HEADS:
                    query_ref[:, head * HEAD_SIZE : (head + 1) * HEAD_SIZE] = value
                else:
                    at = (head - QUERY_HEADS) * HEAD_SIZE
                    keyval_ref[:, at : at + HEAD_SIZE] = value

    return call(
        kernel,
        [
            shaped((rows, width), bf16),
            shaped((rows, width), bf16),
            shaped((rows, 2 * kv_width), bf16),
        ],
        (tokens, gain, weights, cosine, sine),
        earlier,
        specs=[WHOLE, WHOLE, UNUSED, WHOLE, WHOLE],
        flops=2 * rows * width * total,
        scratch=[pltpu.VMEM((width, total), bf16), pltpu.SemaphoreType.DMA((total // 512,))],
    )


def allowed_keys(first_ref, rows):
    row = lax.broadcasted_iota(jnp.int32, (rows, 2 * rows), 0)
    key = lax.broadcasted_iota(jnp.int32, (rows, 2 * rows), 1) - rows
    return (key <= row) & (key >= first_ref[...])


def probabilities(query, keys, allowed):
    scores = jnp.where(allowed, times_transposed(query, keys) * SCALE, -1000000000.0)
    exp_scores = jnp.exp(scores - jnp.max(scores, axis=-1, keepdims=True))
    return exp_scores / jnp.sum(exp_scores, axis=-1, keepdims=True)


def keys_and_values(before_ref, own_ref, group):
    both = []
    for base in (group * HEAD_SIZE, (KEY_VALUE_HEADS + group) * HEAD_SIZE):
        at = slice(base, base + HEAD_SIZE)
        both.append(jnp.concatenate([before_ref[:, at], own_ref[:, at]], axis=0))
    return both


def attend(queries, before, own, first, mine, other, tokens, gain, earlier):
    rows, width = tokens.shape
    wide = len(mine)
    chips = mine[0].shape[0]

    def kernel(
        query_ref, before_ref, own_ref, first_ref, token_ref, gain_ref, place_ref, *refs
    ):
        turned_ref, residual_ref, normed_ref, attended_ref, w_ref, sem = refs[2 * wide :]
        copies = fetch_parts(place_ref, refs[:wide], refs[wide : 2 * wide], w_ref, sem)
        allowed = allowed_keys(first_ref, rows)
        for group in range(KEY_VALUE_HEADS):
            keys, values = keys_and_values(before_ref, own_ref, group)
            for head in range(group * GROUP, (group + 1) * GROUP):
                at = slice(head * HEAD_SIZE, (head + 1) * HEAD_SIZE)
                probs = probabilities(query_ref[:, at], keys, allowed)
                mixed = matmul(probs.astype(bf16), values)
                attended_ref[:, at] = mixed.astype(bf16)
                turned_ref[at, :] = mixed.T.astype(bf16)
        attended = attended_ref[...]
        for copy in copies:
            copy.wait()
        for block in range(width // 256):
            at = slice(block * 256, (block + 1) * 256)
            weights = w_ref[:, :, :, at].reshape(width, 256)
            branch = matmul(attended, weights).astype(bf16)
            residual_ref[:, at] = token_ref[:, at].astype(f32) + branch.astype(f32)
        residual = residual_ref[...]
        normed_ref[...] = (residual * inverse_rms(residual) * gain_ref[...]).astype(bf16)

    return call(
        kernel,
        [
            shaped((width, rows), bf16),
            shaped((rows, width), f32),
            shaped((rows, width), bf16),
        ],
        (queries, before, own, first, tokens, gain, device_place(), *mine, *other),
        earlier,
        specs=[*([WHOLE] * 6), SCALAR, *([UNUSED] * (2 * wide))],
        flops=2 * rows * width * width + 8 * rows * rows * width,
        scratch=[
            pltpu.VMEM((rows, width), bf16),
            pltpu.VMEM((chips, 2, width // (2 * chips), width), bf16),
            pltpu.SemaphoreType.DMA((2 * wide,)),
        ],
    )


def pick_rows(pick, rows_in, earlier):
    slots, width = pick.shape[0], rows_in.shape[1]

    def kernel(pick_ref, in_ref, out_ref):
        for block in range(width // 512):
            at = slice(block * 512, (block + 1) * 512)
            out_ref[:, at] = matmul(pick_ref[...], in_ref[:, at]).astype(bf16)

    return call(
        kernel,
        [shaped((slots, width), bf16)],
        (pick, rows_in),
        earlier,
        flops=2 * slots * rows_in.size,
    )[0]


def run_experts(picked, grad_out, parts, rows_up, rows_down):
    slots, width = picked.shape
    ways, chips, _, part = parts.shape
    ff = chips * 2 * rows_down
    each = slots // chips

    def kernel(
        picked_ref, grad_ref, part_ref, acted_ref, pre_ref, back_ref,
        up_w, down_w, gate_ref, upper_ref, up_sem, down_sem,
    ):
        ups, downs = [], []
        for i in range(ways):
            to = pl.ds(i // 2 * part, part)
            ups.append(
                pltpu.make_async_copy(
                    part_ref.at[i, :, pl.ds(0, rows_up), :], up_w.at[:, i % 2, :, to], up_sem.at[i]
                )
            )
            downs.append(
                pltpu.make_async_copy(
                    part_ref.at[i, :, pl.ds(rows_up, rows_down), :],
                    down_w.at[:, i % 2, :, to],
                    down_sem.at[i],
                )
            )
        for copy in ups + downs:
            copy.start()
        for copy in ups:
            copy.wait()

        @pl.loop(0, ff // 256)
        def _(j):
            at = pl.multiple_of(j * 256, 256)
            for base, ref in ((0, gate_ref), (ff, upper_ref)):
                weights = up_w[:, :, :, pl.ds(base + at, 256)].reshape(width, 256)
                ref[:, pl.ds(at, 256)] = matmul(picked_ref[...], weights)

        for copy in downs:
            copy.wait()
        half = chips // 2

        @pl.loop(0, 2)
        def _(j):
            at = pl.ds(pl.multiple_of(j * (ff // 2), 128), ff // 2)
            weights = down_w[pl.ds(j * half, half)].reshape(ff // 2, width)
            grad_act = times_transposed(grad_ref[...], weights)
            gate, up = gate_ref[:, at], upper_ref[:, at]
            sigmoid = 1.0 / (1.0 + jnp.exp(-gate))
            silu = gate * sigmoid
            acted_ref[:, at] = (silu * up).astype(bf16)
            grad_gate = grad_act * up * sigmoid * (1.0 + gate * (1.0 - sigmoid))
            pre_ref[:, at] = grad_gate.astype(bf16)
            upper = pl.ds(pl.multiple_of(ff + j * (ff // 2), 128), ff // 2)
            pre_ref[:, upper] = (grad_act * silu).astype(bf16)

        @pl.loop(0, 2)
        def _(j):
            to = pl.ds(pl.multiple_of(j * (width // 2), 128), width // 2)
            weights = up_w[pl.ds(j * half, half)].reshape(width // 2, 2 * ff)
            back = times_transposed(pre_ref[...], weights).astype(bf16)
            back_ref[:, 0, :, to] = back.reshape(chips, each, width // 2)
            weights = down_w[:, :, :, to].reshape(ff, width // 2)
            forward = matmul(acted_ref[...], weights).astype(bf16)
            back_ref[:, 1, :, to] = forward.reshape(chips, each, width // 2)

    return call(
        kernel,
        [
            shaped((slots, ff), bf16),
            shaped((slots, 2 * ff), bf16),
            shaped((chips, 2, each, width), bf16),
        ],
        (picked, grad_out, parts),
        specs=[WHOLE, WHOLE, UNUSED],
        flops=2 * slots * 6 * width * ff,
        scratch=[
            pltpu.VMEM((chips, 2, rows_up, width), bf16),
            pltpu.VMEM((chips, 2, rows_down, width), bf16),
            pltpu.VMEM((slots, ff), f32),
            pltpu.VMEM((slots, ff), f32),
            pltpu.SemaphoreType.DMA((ways,)),
            pltpu.SemaphoreType.DMA((ways,)),
        ],
    )


def expert_weight_grads(picked, grad_pre, acted, grad_out, rows_up, rows_down, chips, wide, earlier):
    slots, width = picked.shape
    half, part = (rows_up + rows_down) // 2, width // wide
    steps = 2
    near = chips // steps

    def kernel(picked_ref, pre_ref, acted_ref, grad_ref, *refs):
        out_ref, keep_ref = refs[-2:]
        columns = width // 2
        for n in range(2):
            at = slice(n * columns, (n + 1) * columns)
            for m in range(near // 2):
                block = slice(m * 4 * rows_up, (m + 1) * 4 * rows_up)
                up = transposed_times(picked_ref[:, block], pre_ref[:, at])
                for i in range(4):
                    rows = up[i * rows_up : (i + 1) * rows_up]
                    k, c = 2 * m + i // 2, i % 2
                    keep_ref[k, c] = rows[half:]
                    low = rows[:half].astype(bf16)
                    for j in range(columns // part):
                        z = n * (columns // part) + j
                        out_ref[z, c, 0, k] = low[:, j * part : (j + 1) * part]
            down = transposed_times(acted_ref[...], grad_ref[:, at])
            for k in range(near):
                for c in range(2):
                    base = (2 * k + c) * rows_down
                    rest = jnp.concatenate([keep_ref[k, c], down[base : base + rows_down]], axis=0)
                    rest = rest.astype(bf16)
                    for j in range(columns // part):
                        z = n * (columns // part) + j
                        out_ref[z, c, 1, k] = rest[:, j * part : (j + 1) * part]

    return pl.pallas_call(
        kernel,
        grid=(steps,),
        in_specs=[
            pl.BlockSpec((slots, width // steps), lambda s: (0, s)),
            pl.BlockSpec(grad_pre.shape, lambda s: (0, 0)),
            pl.BlockSpec((slots, acted.shape[1] // steps), lambda s: (0, s)),
            pl.BlockSpec(grad_out.shape, lambda s: (0, 0)),
            *([UNUSED] * len(earlier)),
        ],
        out_specs=pl.BlockSpec((wide, 2, 2, near, half, part), lambda s: (0, 0, 0, s, 0, 0)),
        out_shape=shaped((wide, 2, 2, chips, half, part), bf16),
        scratch_shapes=[pltpu.VMEM((near, 2, rows_up - half, width // 2), f32)],
        compiler_params=pltpu.CompilerParams(vmem_limit_bytes=VMEM_LIMIT),
        cost_estimate=pl.CostEstimate(
            flops=2 * slots * 3 * width * acted.shape[1],
            bytes_accessed=4 * 4 * slots * width,
            transcendentals=0,
        ),
    )(picked, grad_pre, acted, grad_out, *earlier)


def residual_grad(pick, returned, residual, gain, cotangent, earlier):
    rows, width = residual.shape
    slots = pick.shape[0]

    def kernel(pick_ref, back_ref, residual_ref, gain_ref, cot_ref, grad_ref, branch_ref, gain_grad_ref):
        for block in range(width // 512):
            at = slice(block * 512, (block + 1) * 512)
            back = back_ref[:, 0, :, at].reshape(slots, 512)
            grad_ref[:, at] = transposed_times(pick_ref[...], back)
        grad, grad_gain = norm_back(residual_ref[...], gain_ref[...], grad_ref[...])
        grad = grad + cot_ref[...].astype(f32)
        grad_ref[...] = grad
        branch_ref[...] = grad.astype(bf16)
        gain_grad_ref[...] = grad_gain

    return call(
        kernel,
        [shaped((rows, width), f32), shaped((rows, width), bf16), shaped((1, width), f32)],
        (pick, returned, residual, gain, cotangent),
        earlier,
        flops=2 * slots * width * rows,
    )


def add_expert_rows(pick, weight, returned, residual, earlier):
    rows, width = residual.shape
    slots = pick.shape[0]

    def kernel(pick_ref, weight_ref, back_ref, residual_ref, out_ref):
        back = jnp.where(pick_ref[...] > 0, weight_ref[...], 0.0)
        high = back.astype(bf16)
        low = (back - high.astype(f32)).astype(bf16)
        for block in range(width // 512):
            at = slice(block * 512, (block + 1) * 512)
            expert = back_ref[:, 1, :, at].reshape(slots, 512)
            mixture = transposed_times(high, expert) + transposed_times(low, expert)
            out_ref[:, at] = (residual_ref[:, at] + mixture).astype(bf16)

    return call(
        kernel,
        [shaped((rows, width), bf16)],
        (pick, weight, returned, residual),
        earlier,
        flops=4 * slots * width * rows,
    )[0]


def attend_back(grad_branch, mine, other, queries, before, own, first, cosine, sine):
    rows, width = grad_branch.shape
    kv_width = KEY_VALUE_HEADS * HEAD_SIZE
    wide = len(mine)
    chips = mine[0].shape[0]

    def kernel(
        grad_ref, query_ref, before_ref, own_ref, first_ref, cos_ref, sin_ref, place_ref, *refs
    ):
        out_ref, prev_ref, self_ref, attended_ref, w_ref, sem = refs[2 * wide :]
        copies = fetch_parts(place_ref, refs[:wide], refs[wide : 2 * wide], w_ref, sem)
        for copy in copies:
            copy.wait()
        for half in range(2):
            at = slice(half * (width // 2), (half + 1) * (width // 2))
            weights = w_ref[half * (chips // 2) : (half + 1) * (chips // 2)]
            weights = weights.reshape(width // 2, width)
            attended_ref[:, at] = times_transposed(grad_ref[...], weights).astype(bf16)
        allowed = allowed_keys(first_ref, rows)
        cos, sin = cos_ref[...], sin_ref[...]
        for group in range(KEY_VALUE_HEADS):
            keys, values = keys_and_values(before_ref, own_ref, group)
            raws, lows, uppers, asked = [], [], [], []
            for head in range(group * GROUP, (group + 1) * GROUP):
                at = slice(head * HEAD_SIZE, (head + 1) * HEAD_SIZE)
                query, upper = query_ref[:, at], attended_ref[:, at]
                probs = probabilities(query, keys, allowed)
                grad_probs = times_transposed(upper, values)
                inner = jnp.sum(probs * grad_probs, axis=-1, keepdims=True)
                raw = (probs * (grad_probs - inner) * SCALE).astype(bf16)
                out_ref[head] = rotate(matmul(raw, keys), cos, -sin).astype(bf16)
                raws.append(raw)
                lows.append(probs.astype(bf16))
                uppers.append(upper)
                asked.append(query)
            for base, lefts, rights in (
                (group * HEAD_SIZE, raws, asked),
                (kv_width + group * HEAD_SIZE, lows, uppers),
            ):
                grad = transposed_times(
                    jnp.concatenate(lefts, axis=0), jnp.concatenate(rights, axis=0)
                )
                prev_ref[:, base : base + HEAD_SIZE] = grad[:rows].astype(bf16)
                self_ref[:, base : base + HEAD_SIZE] = grad[rows:]

    return call(
        kernel,
        [
            shaped((QUERY_HEADS, rows, HEAD_SIZE), bf16),
            shaped((rows, 2 * kv_width), bf16),
            shaped((rows, 2 * kv_width), f32),
        ],
        (grad_branch, queries, before, own, first, cosine, sine, device_place(), *mine, *other),
        specs=[*([WHOLE] * 7), SCALAR, *([UNUSED] * (2 * wide))],
        flops=2 * rows * width * width + 20 * rows * rows * width,
        scratch=[
            pltpu.VMEM((rows, width), bf16),
            pltpu.VMEM((chips, 2, width // (2 * chips), width), bf16),
            pltpu.SemaphoreType.DMA((2 * wide,)),
        ],
    )


def qkv_blocks_of(grad_queries, grad_own, from_next, cosine, sine, earlier):
    heads, rows, size = grad_queries.shape
    total = heads + 2 * KEY_VALUE_HEADS

    def kernel(query_ref, own_ref, next_ref, cos_ref, sin_ref, out_ref):
        out_ref[:heads] = query_ref[...]
        for i in range(2 * KEY_VALUE_HEADS):
            at = slice(i * size, (i + 1) * size)
            grad = own_ref[:, at] + next_ref[:, at].astype(f32)
            if i < KEY_VALUE_HEADS:
                grad = rotate(grad, cos_ref[...], -sin_ref[...])
            out_ref[heads + i] = grad.astype(bf16)

    return call(
        kernel,
        [shaped((total, rows, size), bf16)],
        (grad_queries, grad_own, from_next, cosine, sine),
        earlier,
    )[0]


def input_grad(blocks, weights, tokens, gain, grad_residual):
    rows, width = tokens.shape
    columns = blocks.shape[0] * HEAD_SIZE

    def kernel(
        block_ref, all_ref, token_ref, gain_ref, residual_ref, out_ref, gain_grad_ref, w_ref, sem
    ):
        copies = fetch(all_ref, w_ref, sem, 1)
        total = jnp.zeros((rows, width), f32)
        for i in range(blocks.shape[0] // 2):
            if i % 2 == 0:
                copies[i // 2].wait()
            pair = jnp.concatenate([block_ref[2 * i], block_ref[2 * i + 1]], axis=1)
            total = total + times_transposed(pair, w_ref[:, i * 256 : (i + 1) * 256])
        grad, grad_gain = norm_back(token_ref[...].astype(f32), gain_ref[...], total)
        out_ref[...] = (residual_ref[...] + grad).astype(bf16)
        gain_grad_ref[...] = grad_gain

    return call(
        kernel,
        [shaped((rows, width), bf16), shaped((1, width), f32)],
        (blocks, weights, tokens, gain, grad_residual),
        specs=[WHOLE, UNUSED, WHOLE, WHOLE, WHOLE],
        flops=2 * rows * width * columns,
        scratch=[pltpu.VMEM((width, columns), bf16), pltpu.SemaphoreType.DMA((columns // 512,))],
    )


def gather_over_z(part):
    wide = lax.axis_size("z")
    return [part] + [
        lax.ppermute(part, "z", [(i, i ^ k) for i in range(wide)]) for k in range(1, wide)
    ]


def gather_over_rep(piece):
    wide = lax.axis_size("z")
    ways = 2 * wide
    moved = []
    for k in range(wide):
        for j in range(2):
            step = j * wide + k
            moved.append(
                lax.ppermute(piece, REP, [(i, i ^ step) for i in range(ways)]) if step else piece
            )
    return moved


def expert_outputs(moved, rows_up, rows_down):
    wide = len(moved) // 2
    experts, half, part = moved[0].shape
    width = wide * part
    split = rows_up - half
    place = jnp.stack([lax.axis_index("h"), lax.axis_index("z")]).astype(jnp.int32)

    def kernel(place_ref, *refs):
        up_ref, down_ref = refs[2 * wide :]
        low = place_ref[0] == 0
        for k in range(wide):
            at = pl.ds(pl.multiple_of((place_ref[1] ^ k) * part, 128), part)
            same, other = refs[2 * k][0].astype(f32), refs[2 * k + 1][0].astype(f32)
            rest = jnp.where(low, other, same)
            up_ref[0, :half, at] = jnp.where(low, same, other)
            up_ref[0, half:, at] = rest[:split]
            down_ref[0, :, at] = rest[split:]

    return pl.pallas_call(
        kernel,
        grid_spec=pltpu.PrefetchScalarGridSpec(
            num_scalar_prefetch=1,
            grid=(experts,),
            in_specs=[pl.BlockSpec((1, half, part), lambda e, p: (e, 0, 0))] * (2 * wide),
            out_specs=[
                pl.BlockSpec((1, rows_up, width), lambda e, p: (e, 0, 0)),
                pl.BlockSpec((1, rows_down, width), lambda e, p: (e, 0, 0)),
            ],
        ),
        out_shape=[
            shaped((experts, rows_up, width), f32),
            shaped((experts, rows_down, width), f32),
        ],
    )(place, *moved)


def after(value, *earlier):
    for one in earlier:
        zero = jnp.minimum(jnp.abs(one[(0,) * one.ndim].astype(f32)), 0.0)
        value = value + zero.astype(value.dtype)
    return value


def pack_attention_grads(blocks, out_rows, wide, earlier):
    count, rows, column = blocks.shape
    rows -= 8
    half = rows // 2
    total = count + out_rows.shape[1] // column
    each = total // wide

    def kernel(block_ref, out_ref, piece_ref):
        piece_ref[...] = jnp.zeros_like(piece_ref)
        gains = block_ref[0, rows:].astype(f32)
        for b in range(1, count):
            gains = gains + block_ref[b, rows:].astype(f32)
        for h in range(2):
            at = slice(h * half, (h + 1) * half)
            for b in range(total):
                if b < count:
                    value = block_ref[b, at]
                else:
                    value = out_ref[at, (b - count) * column : (b - count + 1) * column]
                to = (b % each) * column
                piece_ref[h * wide + b // each, :half, to : to + column] = value
        for p in range(2 * wide):
            piece_ref[p, half:, :column] = gains.astype(bf16)

    return call(
        kernel, [shaped((2 * wide, half + 8, each * column), bf16)], (blocks, out_rows), earlier
    )[0]


def sum_and_copy(pieces):
    count, rows, columns = pieces.shape

    def kernel(piece_ref, copy_ref, gain_ref):
        total = piece_ref[0].astype(f32)
        for p in range(1, count):
            total = total + piece_ref[p].astype(f32)
        gain_ref[...] = total[rows - 8 :, :128]
        low = total[: rows - 8].astype(bf16)
        for p in range(count):
            copy_ref[p] = low

    return pl.pallas_call(
        kernel,
        out_shape=[
            jax.ShapeDtypeStruct((count, rows - 8, columns), bf16),
            jax.ShapeDtypeStruct((8, 128), f32),
        ],
    )(pieces)


def attention_outputs(pieces, widths):
    count, half, part = pieces.shape
    wide = count // 2

    def kernel(piece_ref, *out_refs):
        for h in range(2):
            for z in range(wide):
                left, right, base = z * part, (z + 1) * part, 0
                for ref, size in zip(out_refs, widths):
                    low, high = max(left, base), min(right, base + size)
                    if low < high:
                        ref[h * half : (h + 1) * half, low - base : high - base] = piece_ref[
                            h * wide + z, :, low - left : high - left
                        ].astype(f32)
                    base += size

    return pl.pallas_call(
        kernel,
        out_shape=[jax.ShapeDtypeStruct((2 * half, size), f32) for size in widths],
    )(pieces)


def per_device(
    tokens,
    cotangent,
    seq_lengths,
    seq_order,
    routes,
    gate_weights,
    attn_gain,
    w_query,
    key_value_weight,
    w_out,
    ffn_gain,
    w_gateup,
    w_down,
):
    wide_z = lax.axis_size("z")
    shards = lax.axis_size("y") * lax.axis_size("x") * lax.axis_size("c")
    core = lax.axis_index("c")
    shard = (lax.axis_index("y") * lax.axis_size("x") + lax.axis_index("x")) * 2 + core
    rows, width = tokens.shape
    experts = w_gateup.shape[0]
    kv_width = KEY_VALUE_HEADS * HEAD_SIZE
    owned = width // shards

    qkv_full = lax.all_gather(
        jnp.concatenate([w_query, key_value_weight], 1), SHARD, axis=0, tiled=True
    )
    part = width // wide_z
    rows_out, rows_up, rows_down = w_out.shape[0], w_gateup.shape[1], w_down.shape[1]
    column = lax.axis_index("z") * part
    gains_own = jnp.pad(jnp.stack([attn_gain, ffn_gain]), ((0, 14), (0, part - owned)))
    out_part = jnp.concatenate(
        [lax.dynamic_slice_in_dim(w_out, column, part, 1), gains_own], axis=0
    )
    out_part = spread(out_part, experts, CHIPS)
    expert_part = jnp.concatenate(
        [
            lax.dynamic_slice_in_dim(w_gateup, column, part, 2),
            lax.dynamic_slice_in_dim(w_down, column, part, 2),
        ],
        axis=1,
    )
    gains_mine = out_part[:, rows_out : rows_out + 2, :owned]
    gains = in_core_order(core, gains_mine, lax.ppermute(gains_mine, "c", SWAP))
    gains = gains.transpose(2, 0, 1, 3).reshape(2, width).astype(f32)
    gain_attn, gain_ffn = gains[:1], gains[1:]
    out_mine = gather_over_z(out_part)
    out_other = [lax.ppermute(one, "c", SWAP) for one in out_mine]
    chosen = routes[:, :, None] == jnp.arange(experts, dtype=jnp.int32)
    member = jnp.any(chosen, axis=1)
    weight = jnp.sum(jnp.where(chosen, gate_weights[:, :, None], 0.0), axis=1)
    place = jnp.cumsum(member.astype(jnp.int32), axis=0) - 1
    slot = jnp.where(member, place, -1).T
    picks = slot[:, None, :] == jnp.arange(CAP, dtype=jnp.int32)[None, :, None]
    pick = picks.astype(bf16).reshape(experts * CAP, rows)
    slot_weight = jnp.sum(jnp.where(picks, weight.T[:, None, :], 0.0), axis=2)
    grad_out = matmul(pick, cotangent) * slot_weight.reshape(-1, 1)
    grad_out = exchange(after(grad_out, out_part).astype(bf16), CHIPS)

    expert_part = exchange(after(expert_part, grad_out, *out_mine[1:]), CHIPS)
    expert_parts = lax.all_gather(expert_part, ("z", "c"), axis=0)

    lengths = seq_lengths[0]
    starts = jnp.cumsum(lengths) - lengths
    row_at = shard * rows + jnp.arange(rows, dtype=jnp.int32)
    first_at = jnp.max(jnp.where(starts[None, :] <= row_at[:, None], starts[None, :], 0), axis=1)
    cosine, sine = rotary_tables(row_at - first_at)
    first = (first_at - shard * rows).astype(jnp.int32)[:, None]
    normed, queries, keyval = project_qkv(
        tokens, gain_attn, qkv_full, cosine, sine, ()
    )
    ring = [(i, (i + 1) % shards) for i in range(shards)]
    back_ring = [((i + 1) % shards, i) for i in range(shards)]
    before = lax.ppermute(keyval, SHARD, ring)
    attended_turned, residual, normed_ffn = attend(
        queries, before, keyval, first, out_mine, out_other, tokens, gain_ffn, (grad_out,)
    )

    picked = exchange(pick_rows(pick, normed_ffn, ()), CHIPS)
    normed_all = lax.all_gather(after(normed, picked), SHARD, axis=0, tiled=True)
    attended_cols = exchange(after(attended_turned, picked), SHARD)
    attended_cols = attended_cols.reshape(shards, owned, rows)
    acted, grad_pre, returned = run_experts(
        picked, grad_out, expert_parts, rows_up, rows_down
    )
    pieces = expert_weight_grads(
        picked,
        grad_pre,
        acted,
        grad_out,
        rows_up,
        rows_down,
        experts,
        wide_z,
        (returned, attended_cols),
    )
    returned = exchange(returned, CHIPS)
    pieces = pieces.reshape(2 * wide_z, *pieces.shape[2:])
    over_z = lax.psum_scatter(pieces, ("z", "c"), scatter_dimension=0, tiled=False)

    grad_residual, grad_branch, grad_gain_ffn = residual_grad(
        pick, returned, residual, gain_ffn, cotangent, (normed_all,)
    )
    grad_branch_all = lax.all_gather(grad_branch, SHARD, axis=0, tiled=True)
    grad_queries, grad_before, grad_own = attend_back(
        grad_branch, out_mine, out_other, queries, before, keyval, first, cosine, sine
    )
    from_next = lax.ppermute(grad_before, SHARD, back_ring)
    over_z = over_z.reshape(2 * experts, *over_z.shape[2:])
    over_rep = exchange(over_z, ("h", *CHIPS)).reshape(2, experts, *over_z.shape[1:])
    over_rep = (over_rep[0].astype(f32) + over_rep[1].astype(f32)).astype(bf16)
    grad_blocks = qkv_blocks_of(
        grad_queries, grad_own, from_next, cosine, sine, (over_rep,)
    )
    grad_tokens, grad_gain_attn = input_grad(
        grad_blocks, qkv_full, tokens, gain_attn, grad_residual
    )

    grad_cols = exchange(grad_blocks, SHARD)
    moved = gather_over_rep(over_rep)
    shard_gateup, shard_down = expert_outputs(moved, rows_up, rows_down)
    qkv_block = transposed_times(normed_all, grad_cols.reshape(shards * rows, HEAD_SIZE))
    grad_gains = jnp.concatenate([grad_gain_attn, grad_gain_ffn]).reshape(2, shards, owned)
    gain_rows = jnp.pad(
        grad_gains.transpose(1, 0, 2).astype(bf16), ((0, 0), (0, 6), (0, HEAD_SIZE - owned))
    )
    qkv_block = jnp.concatenate(
        [qkv_block.astype(bf16).reshape(shards, owned, HEAD_SIZE), gain_rows], axis=1
    )
    out_rows = jnp.einsum(
        "jat,jtn->an",
        attended_cols,
        grad_branch_all.reshape(shards, rows, width),
        preferred_element_type=f32,
    ).astype(bf16)
    qkv_blocks = exchange(after(qkv_block, over_rep), SHARD)
    attn_pieces = exchange(pack_attention_grads(qkv_blocks, out_rows, wide_z, moved[1:]), REP)
    attn_copies, gain_sums = sum_and_copy(attn_pieces)
    grad_query, grad_keyval, grad_out_w = attention_outputs(
        exchange(attn_copies, REP), (width, 2 * kv_width, width)
    )

    output = add_expert_rows(
        pick, slot_weight.reshape(-1, 1), returned, residual, (grad_blocks,)
    )
    return (
        output,
        grad_tokens,
        gain_sums[0, :owned],
        grad_query,
        grad_keyval,
        grad_out_w,
        gain_sums[1, :owned],
        shard_gateup,
        shard_down,
    )


def solution(mesh):
    reps, shards = mesh.devices.shape
    fine = Mesh(mesh.devices.reshape(2, reps // 2, shards // 4, 2, 2), ALL)
    split = ALL
    placed = (
        P(split, None),
        P(split, None),
        P(REP, None),
        P(REP, None),
        P(split, None),
        P(split, None),
        P(SHARD),
        P(SHARD, None),
        P(SHARD, None),
        P(SHARD, None),
        P(SHARD),
        P(None, SHARD, None),
        P(None, SHARD, None),
    )
    return jax.shard_map(
        per_device,
        mesh=fine,
        in_specs=placed,
        out_specs=(
            P(split, None),
            P(split, None),
            P(SHARD),
            P(SHARD, None),
            P(SHARD, None),
            P(SHARD, None),
            P(SHARD),
            P(None, SHARD, None),
            P(None, SHARD, None),
        ),
        check_vma=False,
    )
```

```python
import jax
import jax.numpy as jnp
from jax import lax
from jax.experimental import pallas as pl
from jax.experimental.pallas import tpu as pltpu
from jax.sharding import Mesh, PartitionSpec as P

QUERY_HEADS = 12
KEY_VALUE_HEADS = 2
GROUP = QUERY_HEADS // KEY_VALUE_HEADS
HEAD_SIZE = 128
CAP = 80

EPSILON = 1e-06
ROPE_BASE = 10000.0
SCALE = HEAD_SIZE ** (-0.5)
SHARD = ("y", "x", "c")
CHIPS = ("y", "x")
REP = ("h", "z")
ALL = REP + SHARD
SWAP = [(0, 1), (1, 0)]

bf16 = jnp.bfloat16
f32 = jnp.float32

VMEM_LIMIT = 60 * 1024 * 1024
WHOLE = pl.BlockSpec(memory_space=pltpu.VMEM)
UNUSED = pl.BlockSpec(memory_space=pl.ANY)
SCALAR = pl.BlockSpec(memory_space=pltpu.SMEM)


def exchange(parts, axes):
    return lax.all_to_all(parts, axes, 0, 0, tiled=True)


def spread(part, ways, axes):
    return exchange(jnp.broadcast_to(part[None], (ways, *part.shape)), axes)


def matmul(left, right):
    return jnp.dot(left, right, preferred_element_type=f32)


def dot_general(left, right, dims):
    return lax.dot_general(left, right, (dims, ((), ())), preferred_element_type=f32)


def times_transposed(left, right):
    return dot_general(left, right, ((1,), (1,)))


def transposed_times(left, right):
    return dot_general(left, right, ((0,), (0,)))


def in_core_order(core, mine, other):
    return jnp.where(core == 0, jnp.stack([mine, other], 1), jnp.stack([other, mine], 1))


def call(kernel, out_shape, operands, earlier=(), specs=None, flops=0, scratch=()):
    specs = specs or [WHOLE] * len(operands)
    count = len(operands)

    def body(*refs):
        kernel(*refs[:count], *refs[count + len(earlier) :])

    size = sum(one.size * one.dtype.itemsize for one in (*operands, *out_shape))
    return pl.pallas_call(
        body,
        in_specs=[*specs, *([UNUSED] * len(earlier))],
        out_specs=[WHOLE] * len(out_shape),
        out_shape=out_shape,
        scratch_shapes=scratch,
        compiler_params=pltpu.CompilerParams(vmem_limit_bytes=VMEM_LIMIT),
        cost_estimate=pl.CostEstimate(flops=flops, bytes_accessed=size, transcendentals=0),
    )(*operands, *earlier)


def fetch(source_ref, to_ref, semaphores, along, base=0):
    rows, columns = to_ref.shape
    copies = []
    for i in range(to_ref.shape[along] // 512):
        chunk = pl.ds(i * 512, 512)
        if along:
            source = source_ref.at[:, pl.ds(base + i * 512, 512)]
            copy = pltpu.make_async_copy(source, to_ref.at[:, chunk], semaphores.at[i])
        else:
            source = source_ref.at[chunk, pl.ds(base, columns)]
            copy = pltpu.make_async_copy(source, to_ref.at[chunk, :], semaphores.at[i])
        copy.start()
        copies.append(copy)
    return copies


def fetch_parts(place_ref, mine_refs, other_refs, to_ref, semaphores):
    rows = to_ref.shape[2]
    part = to_ref.shape[3] // len(mine_refs)
    copies = []
    for k in range(len(mine_refs)):
        to = pl.ds(pl.multiple_of((place_ref[1] ^ k) * part, 128), part)
        owners = ((place_ref[0], mine_refs[k]), (1 - place_ref[0], other_refs[k]))
        for i, (owner, part_ref) in enumerate(owners):
            copy = pltpu.make_async_copy(
                part_ref.at[:, pl.ds(0, rows), :],
                to_ref.at[:, owner, :, to],
                semaphores.at[2 * k + i],
            )
            copy.start()
            copies.append(copy)
    return copies


def device_place():
    return jnp.stack([lax.axis_index("c"), lax.axis_index("z")]).astype(jnp.int32)


def shaped(shape, dtype):
    return jax.ShapeDtypeStruct(shape, dtype)


def inverse_rms(values):
    return lax.rsqrt(jnp.mean(values * values, axis=-1, keepdims=True) + EPSILON)


def norm_back(values, gain_row, upstream):
    factor = inverse_rms(values)
    grad_normed = upstream * gain_row
    grad_gain = upstream * values * factor
    cubed = factor * factor * factor
    grad_input = factor * grad_normed - values * cubed * jnp.mean(
        grad_normed * values, axis=-1, keepdims=True
    )
    return grad_input, grad_gain


def gain_tile(grad_gain, lower):
    rows = grad_gain.shape[0]
    lane = lax.broadcasted_iota(jnp.int32, (rows, 128), 1)
    return transposed_times(grad_gain, ((lane < 64) == lower).astype(f32))


def rotary_tables(position):
    half = HEAD_SIZE // 2
    frequency = ROPE_BASE ** (-jnp.arange(half, dtype=f32) / half)
    angle = position.astype(f32)[:, None] * frequency[None, :]
    cosine, sine = jnp.cos(angle), jnp.sin(angle)
    return jnp.concatenate([cosine, cosine], 1), jnp.concatenate([-sine, sine], 1)


def rotate(values, cosine, sine):
    return values * cosine + pltpu.roll(values, HEAD_SIZE // 2, 1) * sine


def project_qkv(tokens, gain, weights, cosine, sine, earlier):
    rows, width = tokens.shape
    kv_width = KEY_VALUE_HEADS * HEAD_SIZE
    turned = QUERY_HEADS + KEY_VALUE_HEADS
    total = width + 2 * kv_width

    def kernel(
        token_ref, gain_ref, all_ref, cos_ref, sin_ref, normed_ref, query_ref, keyval_ref, w_ref, sem
    ):
        copies = fetch(all_ref, w_ref, sem, 1)
        wide = token_ref[...].astype(f32)
        normed = (wide * inverse_rms(wide) * gain_ref[...]).astype(bf16)
        normed_ref[...] = normed
        cos, sin = cos_ref[...], sin_ref[...]
        for block in range(total // 256):
            if block % 2 == 0:
                copies[block // 2].wait()
            both = matmul(normed, w_ref[:, block * 256 : (block + 1) * 256])
            for i in range(2):
                head = 2 * block + i
                value = both[:, i * HEAD_SIZE : (i + 1) * HEAD_SIZE]
                if head < turned:
                    value = rotate(value, cos, sin)
                value = value.astype(bf16)
                if head < QUERY_HEADS:
                    query_ref[:, head * HEAD_SIZE : (head + 1) * HEAD_SIZE] = value
                else:
                    at = (head - QUERY_HEADS) * HEAD_SIZE
                    keyval_ref[:, at : at + HEAD_SIZE] = value

    return call(
        kernel,
        [
            shaped((rows, width), bf16),
            shaped((rows, width), bf16),
            shaped((rows, 2 * kv_width), bf16),
        ],
        (tokens, gain, weights, cosine, sine),
        earlier,
        specs=[WHOLE, WHOLE, UNUSED, WHOLE, WHOLE],
        flops=2 * rows * width * total,
        scratch=[pltpu.VMEM((width, total), bf16), pltpu.SemaphoreType.DMA((total // 512,))],
    )


def allowed_keys(first_ref, rows):
    row = lax.broadcasted_iota(jnp.int32, (rows, 2 * rows), 0)
    key = lax.broadcasted_iota(jnp.int32, (rows, 2 * rows), 1) - rows
    return (key <= row) & (key >= first_ref[...])


def probabilities(query, keys, allowed):
    scores = jnp.where(allowed, times_transposed(query, keys) * SCALE, -1000000000.0)
    exp_scores = jnp.exp(scores - jnp.max(scores, axis=-1, keepdims=True))
    return exp_scores / jnp.sum(exp_scores, axis=-1, keepdims=True)


def keys_and_values(before_ref, own_ref, group):
    both = []
    for base in (group * HEAD_SIZE, (KEY_VALUE_HEADS + group) * HEAD_SIZE):
        at = slice(base, base + HEAD_SIZE)
        both.append(jnp.concatenate([before_ref[:, at], own_ref[:, at]], axis=0))
    return both


def attend(queries, before, own, first, mine, other, tokens, gain, pick, earlier):
    rows, width = tokens.shape
    wide = len(mine)
    chips = mine[0].shape[0]

    def kernel(
        query_ref, before_ref, own_ref, first_ref, token_ref, gain_ref, pick_ref, place_ref, *refs
    ):
        turned_ref, residual_ref, picked_ref, attended_ref, w_ref, sem = refs[2 * wide :]
        copies = fetch_parts(place_ref, refs[:wide], refs[wide : 2 * wide], w_ref, sem)
        allowed = allowed_keys(first_ref, rows)
        for group in range(KEY_VALUE_HEADS):
            keys, values = keys_and_values(before_ref, own_ref, group)
            for head in range(group * GROUP, (group + 1) * GROUP):
                at = slice(head * HEAD_SIZE, (head + 1) * HEAD_SIZE)
                probs = probabilities(query_ref[:, at], keys, allowed)
                mixed = matmul(probs.astype(bf16), values)
                attended_ref[:, at] = mixed.astype(bf16)
                turned_ref[at, :] = mixed.T.astype(bf16)
        attended = attended_ref[...]
        for copy in copies:
            copy.wait()
        for block in range(width // 256):
            at = slice(block * 256, (block + 1) * 256)
            weights = w_ref[:, :, :, at].reshape(width, 256)
            branch = matmul(attended, weights).astype(bf16)
            residual_ref[:, at] = token_ref[:, at].astype(f32) + branch.astype(f32)
        residual = residual_ref[...]
        normed = (residual * inverse_rms(residual) * gain_ref[...]).astype(bf16)
        for block in range(width // 512):
            at = slice(block * 512, (block + 1) * 512)
            picked_ref[:, at] = matmul(pick_ref[...], normed[:, at]).astype(bf16)

    return call(
        kernel,
        [
            shaped((width, rows), bf16),
            shaped((rows, width), f32),
            shaped((pick.shape[0], width), bf16),
        ],
        (queries, before, own, first, tokens, gain, pick, device_place(), *mine, *other),
        earlier,
        specs=[*([WHOLE] * 7), SCALAR, *([UNUSED] * (2 * wide))],
        flops=2 * rows * width * width + 8 * rows * rows * width,
        scratch=[
            pltpu.VMEM((rows, width), bf16),
            pltpu.VMEM((chips, 2, width // (2 * chips), width), bf16),
            pltpu.SemaphoreType.DMA((2 * wide,)),
        ],
    )


def run_experts(picked, grad_out, parts, rows_up, rows_down):
    slots, width = picked.shape
    ways, chips, _, part = parts.shape
    wide = ways // 2
    ff = chips * 2 * rows_down
    each = slots // chips
    half = (rows_up + rows_down) // 2
    near = chips // 2

    def kernel(
        picked_any, grad_any, part_ref, back_any, piece_any,
        picked_ref, grad_ref, up_w, down_w, gate_ref, upper_ref, acted_ref, pre_ref, back_ref,
        keep_ref, piece_ref, in_sem, up_sem, down_sem, out_sem,
    ):
        rows_in = pltpu.make_async_copy(picked_any, picked_ref, in_sem.at[0])
        grads_in = pltpu.make_async_copy(grad_any, grad_ref, in_sem.at[1])
        ups, downs = [], []
        for i in range(ways):
            to = pl.ds(i // 2 * part, part)
            ups.append(
                pltpu.make_async_copy(
                    part_ref.at[i, :, pl.ds(0, rows_up), :], up_w.at[:, i % 2, :, to], up_sem.at[i]
                )
            )
            downs.append(
                pltpu.make_async_copy(
                    part_ref.at[i, :, pl.ds(rows_up, rows_down), :],
                    down_w.at[:, i % 2, :, to],
                    down_sem.at[i],
                )
            )
        for copy in [rows_in, *ups, grads_in, *downs]:
            copy.start()
        for copy in [rows_in, *ups]:
            copy.wait()

        @pl.loop(0, ff // 256)
        def _(j):
            at = pl.multiple_of(j * 256, 256)
            for base, ref in ((0, gate_ref), (ff, upper_ref)):
                weights = up_w[:, :, :, pl.ds(base + at, 256)].reshape(width, 256)
                ref[:, pl.ds(at, 256)] = matmul(picked_ref[...], weights)

        for copy in [grads_in, *downs]:
            copy.wait()

        @pl.loop(0, 2)
        def _(j):
            at = pl.ds(pl.multiple_of(j * (ff // 2), 128), ff // 2)
            weights = down_w[pl.ds(j * near, near)].reshape(ff // 2, width)
            grad_act = times_transposed(grad_ref[...], weights)
            gate, up = gate_ref[:, at], upper_ref[:, at]
            sigmoid = 1.0 / (1.0 + jnp.exp(-gate))
            silu = gate * sigmoid
            acted_ref[:, at] = (silu * up).astype(bf16)
            grad_gate = grad_act * up * sigmoid * (1.0 + gate * (1.0 - sigmoid))
            pre_ref[:, at] = grad_gate.astype(bf16)
            upper = pl.ds(pl.multiple_of(ff + j * (ff // 2), 128), ff // 2)
            pre_ref[:, upper] = (grad_act * silu).astype(bf16)

        columns = width // 2

        @pl.loop(0, 2)
        def _(j):
            to = pl.ds(pl.multiple_of(j * columns, 128), columns)
            weights = up_w[pl.ds(j * near, near)].reshape(columns, 2 * ff)
            back = times_transposed(pre_ref[...], weights).astype(bf16)
            back_ref[:, 0, :, to] = back.reshape(chips, each, columns)
            weights = down_w[:, :, :, to].reshape(ff, columns)
            forward = matmul(acted_ref[...], weights).astype(bf16)
            back_ref[:, 1, :, to] = forward.reshape(chips, each, columns)

        back_out = pltpu.make_async_copy(back_ref, back_any, out_sem.at[0])
        back_out.start()

        @pl.loop(0, 2)
        def _(s):
            for n in range(2):
                at = slice(n * columns, (n + 1) * columns)
                for m in range(near // 2):
                    base = pl.multiple_of(s * near * 2 * rows_up + m * 4 * rows_up, 128)
                    block = picked_ref[:, pl.ds(base, 4 * rows_up)]
                    up = transposed_times(block, pre_ref[:, at])
                    for i in range(4):
                        rows = up[i * rows_up : (i + 1) * rows_up]
                        k, c = 2 * m + i // 2, i % 2
                        keep_ref[k, c] = rows[half:]
                        low = rows[:half].astype(bf16)
                        for j in range(columns // part):
                            z = n * (columns // part) + j
                            piece_ref[z, c, s * near + k, 0] = low[:, j * part : (j + 1) * part]
                base = pl.multiple_of(s * near * 2 * rows_down, 128)
                block = acted_ref[:, pl.ds(base, near * 2 * rows_down)]
                down = transposed_times(block, grad_ref[:, at])
                for k in range(near):
                    for c in range(2):
                        low = (2 * k + c) * rows_down
                        rest = jnp.concatenate([keep_ref[k, c], down[low : low + rows_down]], axis=0)
                        rest = rest.astype(bf16)
                        for j in range(columns // part):
                            z = n * (columns // part) + j
                            piece_ref[z, c, s * near + k, 1] = rest[:, j * part : (j + 1) * part]
            chip = pl.ds(s * near, near)
            pltpu.make_async_copy(
                piece_ref.at[:, :, chip], piece_any.at[:, :, chip], out_sem.at[1 + s]
            ).start()

        back_out.wait()
        for s in range(2):
            chip = pl.ds(s * near, near)
            pltpu.make_async_copy(
                piece_ref.at[:, :, chip], piece_any.at[:, :, chip], out_sem.at[1 + s]
            ).wait()

    back = shaped((chips, 2, each, width), bf16)
    pieces = shaped((wide, 2, chips, 2, half, part), bf16)
    return pl.pallas_call(
        kernel,
        in_specs=[UNUSED] * 3,
        out_specs=[UNUSED] * 2,
        out_shape=[back, pieces],
        scratch_shapes=[
            pltpu.VMEM((slots, width), bf16),
            pltpu.VMEM((slots, width), bf16),
            pltpu.VMEM((chips, 2, rows_up, width), bf16),
            pltpu.VMEM((chips, 2, rows_down, width), bf16),
            pltpu.VMEM((slots, ff), f32),
            pltpu.VMEM((slots, ff), f32),
            pltpu.VMEM((slots, ff), bf16),
            pltpu.VMEM((slots, 2 * ff), bf16),
            pltpu.VMEM(back.shape, bf16),
            pltpu.VMEM((near, 2, rows_up - half, width // 2), f32),
            pltpu.VMEM(pieces.shape, bf16),
            pltpu.SemaphoreType.DMA((2,)),
            pltpu.SemaphoreType.DMA((ways,)),
            pltpu.SemaphoreType.DMA((ways,)),
            pltpu.SemaphoreType.DMA((3,)),
        ],
        compiler_params=pltpu.CompilerParams(vmem_limit_bytes=VMEM_LIMIT),
        cost_estimate=pl.CostEstimate(
            flops=2 * slots * 9 * width * ff,
            bytes_accessed=12 * slots * width + 8 * width * 3 * ff,
            transcendentals=0,
        ),
    )(picked, grad_out, parts)


def residual_grad(pick, returned, residual, gain, cotangent, earlier):
    rows, width = residual.shape
    slots = pick.shape[0]

    def kernel(pick_ref, back_ref, residual_ref, gain_ref, cot_ref, grad_ref, branch_ref, gain_grad_ref):
        for block in range(width // 512):
            at = slice(block * 512, (block + 1) * 512)
            back = back_ref[:, 0, :, at].reshape(slots, 512)
            grad_ref[:, at] = transposed_times(pick_ref[...], back)
        grad, grad_gain = norm_back(residual_ref[...], gain_ref[...], grad_ref[...])
        grad = grad + cot_ref[...].astype(f32)
        grad_ref[...] = grad
        branch_ref[...] = grad.astype(bf16)
        gain_grad_ref[...] = gain_tile(grad_gain, False)

    return call(
        kernel,
        [shaped((rows, width), f32), shaped((rows, width), bf16), shaped((width, 128), f32)],
        (pick, returned, residual, gain, cotangent),
        earlier,
        flops=2 * slots * width * rows,
    )


def add_expert_rows(pick, weight, returned, residual, earlier):
    rows, width = residual.shape
    slots = pick.shape[0]

    def kernel(pick_ref, weight_ref, back_ref, residual_ref, out_ref):
        back = jnp.where(pick_ref[...] > 0, weight_ref[...], 0.0)
        high = back.astype(bf16)
        low = (back - high.astype(f32)).astype(bf16)
        for block in range(width // 512):
            at = slice(block * 512, (block + 1) * 512)
            expert = back_ref[:, 1, :, at].reshape(slots, 512)
            mixture = transposed_times(high, expert) + transposed_times(low, expert)
            out_ref[:, at] = (residual_ref[:, at] + mixture).astype(bf16)

    return call(
        kernel,
        [shaped((rows, width), bf16)],
        (pick, weight, returned, residual),
        earlier,
        flops=4 * slots * width * rows,
    )[0]


def attend_back(grad_branch, mine, other, queries, before, own, first, cosine, sine, earlier):
    rows, width = grad_branch.shape
    kv_width = KEY_VALUE_HEADS * HEAD_SIZE
    wide = len(mine)
    chips = mine[0].shape[0]

    def kernel(
        grad_ref, query_ref, before_ref, own_ref, first_ref, cos_ref, sin_ref, place_ref, *refs
    ):
        out_ref, prev_ref, self_ref, attended_ref, w_ref, sem = refs[2 * wide :]
        copies = fetch_parts(place_ref, refs[:wide], refs[wide : 2 * wide], w_ref, sem)
        for copy in copies:
            copy.wait()
        for half in range(2):
            at = slice(half * (width // 2), (half + 1) * (width // 2))
            weights = w_ref[half * (chips // 2) : (half + 1) * (chips // 2)]
            weights = weights.reshape(width // 2, width)
            attended_ref[:, at] = times_transposed(grad_ref[...], weights).astype(bf16)
        allowed = allowed_keys(first_ref, rows)
        cos, sin = cos_ref[...], sin_ref[...]
        for group in range(KEY_VALUE_HEADS):
            keys, values = keys_and_values(before_ref, own_ref, group)
            raws, lows, uppers, asked = [], [], [], []
            for head in range(group * GROUP, (group + 1) * GROUP):
                at = slice(head * HEAD_SIZE, (head + 1) * HEAD_SIZE)
                query, upper = query_ref[:, at], attended_ref[:, at]
                probs = probabilities(query, keys, allowed)
                grad_probs = times_transposed(upper, values)
                inner = jnp.sum(probs * grad_probs, axis=-1, keepdims=True)
                raw = (probs * (grad_probs - inner) * SCALE).astype(bf16)
                out_ref[head] = rotate(matmul(raw, keys), cos, -sin).astype(bf16)
                raws.append(raw)
                lows.append(probs.astype(bf16))
                uppers.append(upper)
                asked.append(query)
            for base, lefts, rights in (
                (group * HEAD_SIZE, raws, asked),
                (kv_width + group * HEAD_SIZE, lows, uppers),
            ):
                grad = transposed_times(
                    jnp.concatenate(lefts, axis=0), jnp.concatenate(rights, axis=0)
                )
                prev_ref[:, base : base + HEAD_SIZE] = grad[:rows].astype(bf16)
                self_ref[:, base : base + HEAD_SIZE] = grad[rows:]

    return call(
        kernel,
        [
            shaped((QUERY_HEADS, rows, HEAD_SIZE), bf16),
            shaped((rows, 2 * kv_width), bf16),
            shaped((rows, 2 * kv_width), f32),
        ],
        (grad_branch, queries, before, own, first, cosine, sine, device_place(), *mine, *other),
        earlier,
        specs=[*([WHOLE] * 7), SCALAR, *([UNUSED] * (2 * wide))],
        flops=2 * rows * width * width + 20 * rows * rows * width,
        scratch=[
            pltpu.VMEM((rows, width), bf16),
            pltpu.VMEM((chips, 2, width // (2 * chips), width), bf16),
            pltpu.SemaphoreType.DMA((2 * wide,)),
        ],
    )


def qkv_blocks_of(grad_queries, grad_own, from_next, cosine, sine, earlier):
    heads, rows, size = grad_queries.shape
    total = heads + 2 * KEY_VALUE_HEADS

    def kernel(query_ref, own_ref, next_ref, cos_ref, sin_ref, out_ref):
        out_ref[:heads] = query_ref[...]
        for i in range(2 * KEY_VALUE_HEADS):
            at = slice(i * size, (i + 1) * size)
            grad = own_ref[:, at] + next_ref[:, at].astype(f32)
            if i < KEY_VALUE_HEADS:
                grad = rotate(grad, cos_ref[...], -sin_ref[...])
            out_ref[heads + i] = grad.astype(bf16)

    return call(
        kernel,
        [shaped((total, rows, size), bf16)],
        (grad_queries, grad_own, from_next, cosine, sine),
        earlier,
    )[0]


def input_grad(blocks, weights, tokens, gain, grad_residual, gain_grad, earlier):
    rows, width = tokens.shape
    columns = blocks.shape[0] * HEAD_SIZE

    def kernel(
        block_ref, all_ref, token_ref, gain_ref, residual_ref, other_ref, out_ref, tile_ref, w_ref, sem
    ):
        copies = fetch(all_ref, w_ref, sem, 1)
        total = jnp.zeros((rows, width), f32)
        for i in range(blocks.shape[0] // 2):
            if i % 2 == 0:
                copies[i // 2].wait()
            pair = jnp.concatenate([block_ref[2 * i], block_ref[2 * i + 1]], axis=1)
            total = total + times_transposed(pair, w_ref[:, i * 256 : (i + 1) * 256])
        grad, grad_gain = norm_back(token_ref[...].astype(f32), gain_ref[...], total)
        out_ref[...] = (residual_ref[...] + grad).astype(bf16)
        tile_ref[...] = (other_ref[...] + gain_tile(grad_gain, True)).astype(bf16)

    return call(
        kernel,
        [shaped((rows, width), bf16), shaped((width, 128), bf16)],
        (blocks, weights, tokens, gain, grad_residual, gain_grad),
        earlier,
        specs=[WHOLE, UNUSED, WHOLE, WHOLE, WHOLE, WHOLE],
        flops=2 * rows * width * columns,
        scratch=[pltpu.VMEM((width, columns), bf16), pltpu.SemaphoreType.DMA((columns // 512,))],
    )


def gather_over_z(part):
    wide = lax.axis_size("z")
    return [part] + [
        lax.ppermute(part, "z", [(i, i ^ k) for i in range(wide)]) for k in range(1, wide)
    ]


def expert_outputs(pieces, rows_up, rows_down):
    wide, experts, _, half, part = pieces.shape
    width = wide * part
    split = rows_up - half

    def kernel(piece_ref, up_ref, down_ref):
        for z in range(wide):
            at = slice(z * part, (z + 1) * part)
            rest = piece_ref[z, 0, 1].astype(f32)
            up_ref[0, :half, at] = piece_ref[z, 0, 0].astype(f32)
            up_ref[0, half:, at] = rest[:split]
            down_ref[0, :, at] = rest[split:]

    return pl.pallas_call(
        kernel,
        grid=(experts,),
        in_specs=[pl.BlockSpec((wide, 1, 2, half, part), lambda e: (0, e, 0, 0, 0))],
        out_specs=[
            pl.BlockSpec((1, rows_up, width), lambda e: (e, 0, 0)),
            pl.BlockSpec((1, rows_down, width), lambda e: (e, 0, 0)),
        ],
        out_shape=[
            shaped((experts, rows_up, width), f32),
            shaped((experts, rows_down, width), f32),
        ],
    )(pieces)


def after(value, *earlier):
    for one in earlier:
        zero = jnp.minimum(jnp.abs(one[(0,) * one.ndim].astype(f32)), 0.0)
        value = value + zero.astype(value.dtype)
    return value


def to_square(value):
    return jnp.stack([value, lax.ppermute(value, "x", SWAP)])


def part_to_square(value, across, axis):
    size = value.shape[axis] // 2
    mine = lax.dynamic_slice_in_dim(value, across * size, size, axis)
    sent = lax.dynamic_slice_in_dim(value, (1 - across) * size, size, axis)
    return jnp.stack([mine, lax.ppermute(sent, "x", SWAP)])


def part_to_core(value, core, axis):
    size = value.shape[axis] // 2
    return lax.ppermute(lax.dynamic_slice_in_dim(value, (1 - core) * size, size, axis), "c", SWAP)


def twice(value, earlier):
    size = value.shape[0]

    def kernel(in_ref, out_ref):
        out_ref[:size] = in_ref[...]
        out_ref[size:] = in_ref[...]

    return call(kernel, [shaped((2 * size, *value.shape[1:]), value.dtype)], (value,), earlier)[0]


def sum_of_halves(value, earlier):
    size = value.shape[0] // 2

    def kernel(in_ref, out_ref):
        out_ref[...] = (in_ref[:size].astype(f32) + in_ref[size:].astype(f32)).astype(bf16)

    return call(kernel, [shaped((size, *value.shape[1:]), value.dtype)], (value,), earlier)[0]


def hold(values, earlier):
    def kernel(*refs):
        del refs

    return pl.pallas_call(
        kernel,
        in_specs=[UNUSED] * (len(values) + len(earlier)),
        out_specs=[UNUSED] * len(values),
        out_shape=[shaped(one.shape, one.dtype) for one in values],
        input_output_aliases={i: i for i in range(len(values))},
    )(*values, *earlier)


def out_weight_grads(near, far, grad_near, grad_far, ways, earlier):
    _, width, rows = near.shape
    columns = grad_far.shape[2]
    core = lax.axis_index("c").astype(jnp.int32).reshape(1)

    def kernel(core_ref, near_ref, far_ref, grad_near_ref, grad_far_ref, out_ref, left_ref):
        at = pl.ds(pl.multiple_of(core_ref[0] * columns, 128), columns)
        for i in range(2):
            left_ref[:, i * rows : (i + 1) * rows] = near_ref[i]
            left_ref[:, (2 + i) * rows : (3 + i) * rows] = far_ref[i]
        right = jnp.concatenate(
            [grad_near_ref[0, :, at], grad_near_ref[1, :, at], grad_far_ref[0], grad_far_ref[1]],
            axis=0,
        )
        each = width // ways
        for i in range(ways):
            left = left_ref[i * each : (i + 1) * each, :]
            out_ref[i] = matmul(left, right).astype(bf16)

    return call(
        kernel,
        [shaped((ways, width // ways, columns), bf16)],
        (core, near, far, grad_near, grad_far),
        earlier,
        specs=[SCALAR, *([WHOLE] * 4)],
        flops=8 * width * rows * columns,
        scratch=[pltpu.VMEM((width, 4 * rows), bf16)],
    )[0]


def qkv_weight_grads(near, far, grad_near, grad_far, ways):
    _, rows, width = near.shape
    heads = grad_far.shape[1]
    columns = heads * HEAD_SIZE
    core = lax.axis_index("c").astype(jnp.int32).reshape(1)

    def kernel(core_ref, near_ref, far_ref, grad_near_ref, grad_far_ref, out_ref, left_ref, right_ref):
        for i in range(2):
            left_ref[i * rows : (i + 1) * rows, :] = near_ref[i]
            left_ref[(2 + i) * rows : (3 + i) * rows, :] = far_ref[i]
            for head in range(heads):
                at = slice(head * HEAD_SIZE, (head + 1) * HEAD_SIZE)
                mine = grad_near_ref[i, core_ref[0] * heads + head]
                right_ref[i * rows : (i + 1) * rows, at] = mine
                right_ref[(2 + i) * rows : (3 + i) * rows, at] = grad_far_ref[i, head]
        each = width // ways
        for i in range(ways):
            block = slice(i * each, (i + 1) * each)
            out_ref[i] = transposed_times(left_ref[:, block], right_ref[...]).astype(bf16)

    return call(
        kernel,
        [shaped((ways, width // ways, columns), bf16)],
        (core, near, far, grad_near, grad_far),
        specs=[SCALAR, *([WHOLE] * 4)],
        flops=8 * width * rows * columns,
        scratch=[pltpu.VMEM((4 * rows, width), bf16), pltpu.VMEM((4 * rows, columns), bf16)],
    )[0]


def moved_over_y(blocks):
    wide = lax.axis_size("y")
    y = lax.axis_index("y")
    moved = [lax.dynamic_index_in_dim(blocks, y, 0, keepdims=False)]
    for k in range(1, wide):
        sent = lax.dynamic_index_in_dim(blocks, y ^ k, 0, keepdims=False)
        moved.append(lax.ppermute(sent, "y", [(i, i ^ k) for i in range(wide)]))
    return moved


def tiles_of(qkv, out, gains, tiles, squares):
    terms = qkv.shape[0]
    rows = qkv.shape[1] // squares
    count = qkv.shape[2] // HEAD_SIZE

    def kernel(qkv_ref, out_ref, *refs):
        gain_refs, tile_ref = refs[:-1], refs[-1]
        for t in range(tiles):
            for p in range(squares):
                block = slice(p * rows, (p + 1) * rows)
                if t < count:
                    at = slice(t * HEAD_SIZE, (t + 1) * HEAD_SIZE)
                    values = [qkv_ref[i, block, at] for i in range(terms)]
                elif t < tiles - 1:
                    at = slice((t - count) * HEAD_SIZE, (t - count + 1) * HEAD_SIZE)
                    values = [out_ref[block, at]]
                else:
                    values = [ref[block] for ref in gain_refs]
                total = values[0].astype(f32)
                for value in values[1:]:
                    total = total + value.astype(f32)
                tile_ref[t * squares + p] = total.astype(bf16)

    return call(
        kernel, [shaped((tiles * squares, rows, HEAD_SIZE), bf16)], (qkv, out, *gains)
    )[0]


def sum_and_copy(parts, squares, copies, earlier):
    count, rows, columns = parts.shape

    def kernel(part_ref, copy_ref):
        for p in range(squares):
            total = part_ref[p].astype(f32)
            for i in range(1, count // squares):
                total = total + part_ref[i * squares + p].astype(f32)
            low = total.astype(bf16)
            for i in range(copies):
                copy_ref[i, p] = low

    return call(kernel, [shaped((copies, squares, rows, columns), bf16)], (parts,), earlier)[0]


def attention_outputs(tiles, query_width, kv_width):
    count, squares, rows, column = tiles.shape
    heads = (query_width + kv_width) // column // squares
    outs = count - 1 - heads

    def kernel(tile_ref, query_ref, keyval_ref, out_ref, gain_ref):
        gains = jnp.zeros((rows, column), f32)
        for q in range(squares):
            for t in range(heads):
                at = (q * heads + t) * column
                value = tile_ref[t, q].astype(f32)
                if at < query_width:
                    query_ref[:, at : at + column] = value
                else:
                    keyval_ref[:, at - query_width : at - query_width + column] = value
            for t in range(outs):
                at = (q * outs + t) * column
                out_ref[:, at : at + column] = tile_ref[heads + t, q].astype(f32)
            gains = gains + tile_ref[count - 1, q].astype(f32)
        gain_ref[...] = gains

    return call(
        kernel,
        [
            shaped((rows, query_width), f32),
            shaped((rows, kv_width), f32),
            shaped((rows, squares * outs * column), f32),
            shaped((rows, column), f32),
        ],
        (tiles,),
    )


def per_device(
    tokens,
    cotangent,
    seq_lengths,
    seq_order,
    routes,
    gate_weights,
    attn_gain,
    w_query,
    key_value_weight,
    w_out,
    ffn_gain,
    w_gateup,
    w_down,
):
    wide_z = lax.axis_size("z")
    shards = lax.axis_size("y") * lax.axis_size("x") * lax.axis_size("c")
    core = lax.axis_index("c")
    shard = (lax.axis_index("y") * lax.axis_size("x") + lax.axis_index("x")) * 2 + core
    rows, width = tokens.shape
    experts = w_gateup.shape[0]
    kv_width = KEY_VALUE_HEADS * HEAD_SIZE
    owned = width // shards

    qkv_full = lax.all_gather(
        jnp.concatenate([w_query, key_value_weight], 1), SHARD, axis=0, tiled=True
    )
    part = width // wide_z
    rows_out, rows_up, rows_down = w_out.shape[0], w_gateup.shape[1], w_down.shape[1]
    column = lax.axis_index("z") * part
    gains_own = jnp.pad(jnp.stack([attn_gain, ffn_gain]), ((0, 14), (0, part - owned)))
    out_part = jnp.concatenate(
        [lax.dynamic_slice_in_dim(w_out, column, part, 1), gains_own], axis=0
    )
    expert_part = jnp.concatenate(
        [
            lax.dynamic_slice_in_dim(w_gateup, column, part, 2),
            lax.dynamic_slice_in_dim(w_down, column, part, 2),
        ],
        axis=1,
    )
    out_part = spread(out_part, experts, CHIPS)
    expert_part = exchange(after(expert_part, out_part), CHIPS)
    gains_mine = out_part[:, rows_out : rows_out + 2, :owned]
    gains = in_core_order(core, gains_mine, lax.ppermute(gains_mine, "c", SWAP))
    gains = gains.transpose(2, 0, 1, 3).reshape(2, width).astype(f32)
    gain_attn, gain_ffn = gains[:1], gains[1:]
    out_mine = gather_over_z(out_part)
    out_other = [lax.ppermute(one, "c", SWAP) for one in out_mine]
    chosen = routes[:, :, None] == jnp.arange(experts, dtype=jnp.int32)
    member = jnp.any(chosen, axis=1)
    weight = jnp.sum(jnp.where(chosen, gate_weights[:, :, None], 0.0), axis=1)
    place = jnp.cumsum(member.astype(jnp.int32), axis=0) - 1
    slot = jnp.where(member, place, -1).T
    picks = slot[:, None, :] == jnp.arange(CAP, dtype=jnp.int32)[None, :, None]
    pick = picks.astype(bf16).reshape(experts * CAP, rows)
    slot_weight = jnp.sum(jnp.where(picks, weight.T[:, None, :], 0.0), axis=2)
    grad_out = matmul(pick, cotangent) * slot_weight.reshape(-1, 1)
    grad_out_sent = after(grad_out, expert_part).astype(bf16)
    grad_out = exchange(grad_out_sent, CHIPS)

    expert_parts = lax.all_gather(
        after(expert_part, *out_mine[1:], grad_out_sent), ("z", "c"), axis=0
    )

    lengths = seq_lengths[0]
    starts = jnp.cumsum(lengths) - lengths
    row_at = shard * rows + jnp.arange(rows, dtype=jnp.int32)
    first_at = jnp.max(jnp.where(starts[None, :] <= row_at[:, None], starts[None, :], 0), axis=1)
    cosine, sine = rotary_tables(row_at - first_at)
    first = (first_at - shard * rows).astype(jnp.int32)[:, None]
    normed, queries, keyval = project_qkv(
        tokens, gain_attn, qkv_full, cosine, sine, ()
    )
    ring = [(i, (i + 1) % shards) for i in range(shards)]
    back_ring = [((i + 1) % shards, i) for i in range(shards)]
    before = lax.ppermute(keyval, SHARD, ring)
    attended_turned, residual, picked = attend(
        queries, before, keyval, first, out_mine, out_other, tokens, gain_ffn, pick, ()
    )

    picked = exchange(hold((picked,), (grad_out,))[0], CHIPS)
    normed_near = to_square(after(normed, picked))
    attended_near = to_square(after(attended_turned, picked))
    returned, pieces = run_experts(picked, grad_out, expert_parts, rows_up, rows_down)
    returned, pieces = hold((returned, pieces), (normed_near, attended_near))
    returned = exchange(returned, CHIPS)
    normed_far = lax.ppermute(normed_near, "c", SWAP)
    attended_far = lax.ppermute(attended_near, "c", SWAP)
    pieces = pieces.reshape(2 * wide_z, *pieces.shape[2:])
    over_z = lax.psum_scatter(pieces, ("z", "c"), scatter_dimension=0, tiled=False)

    grad_residual, grad_branch, gain_grad = residual_grad(
        pick, returned, residual, gain_ffn, cotangent, (normed_far, attended_far)
    )
    across = lax.axis_index("x")
    branch_near = part_to_square(grad_branch, across, 1)
    over_rep = twice(over_z, (branch_near,))
    grad_queries, grad_before, grad_own = attend_back(
        grad_branch,
        out_mine,
        out_other,
        queries,
        before,
        keyval,
        first,
        cosine,
        sine,
        (over_rep,),
    )
    over_rep = exchange(over_rep, ("h", *CHIPS))
    out_terms = out_weight_grads(
        attended_near,
        attended_far,
        branch_near,
        part_to_core(branch_near, core, 2),
        lax.axis_size("y"),
        (grad_before,),
    )
    out_grads = lax.psum_scatter(out_terms, "y", scatter_dimension=0, tiled=True)
    from_next = lax.ppermute(grad_before, SHARD, back_ring)
    grad_blocks = qkv_blocks_of(
        grad_queries, grad_own, from_next, cosine, sine, (over_rep, out_terms)
    )

    blocks_near = part_to_square(grad_blocks, across, 0)
    qkv_grads = qkv_weight_grads(
        normed_near,
        normed_far,
        blocks_near,
        part_to_core(blocks_near, core, 1),
        lax.axis_size("y"),
    )
    over_rep = sum_of_halves(over_rep, (qkv_grads,))
    grad_tokens, tile = input_grad(
        grad_blocks, qkv_full, tokens, gain_attn, grad_residual, gain_grad, (qkv_grads,)
    )
    gain_terms = moved_over_y(tile.reshape(lax.axis_size("y"), -1, HEAD_SIZE))
    qkv_grads = exchange(qkv_grads, "y")
    shard_gateup, shard_down = expert_outputs(
        lax.all_gather(over_rep, "z", axis=0), rows_up, rows_down
    )
    reps = 2 * wide_z
    tiles = exchange(tiles_of(qkv_grads, out_grads.reshape(-1, part), gain_terms, reps, 4), REP + ("x", "c"))
    tiles = exchange(sum_and_copy(tiles, 4, reps, (shard_down,)), REP)
    grad_query, grad_keyval, grad_out_w, gain_sums = attention_outputs(
        tiles, width, 2 * kv_width
    )

    output = add_expert_rows(
        pick, slot_weight.reshape(-1, 1), returned, residual, (qkv_grads,)
    )
    return (
        output,
        grad_tokens,
        gain_sums[:, 0],
        grad_query,
        grad_keyval,
        grad_out_w,
        gain_sums[:, 64],
        shard_gateup,
        shard_down,
    )


def solution(mesh):
    reps, shards = mesh.devices.shape
    fine = Mesh(mesh.devices.reshape(2, reps // 2, shards // 4, 2, 2), ALL)
    split = ALL
    placed = (
        P(split, None),
        P(split, None),
        P(REP, None),
        P(REP, None),
        P(split, None),
        P(split, None),
        P(SHARD),
        P(SHARD, None),
        P(SHARD, None),
        P(SHARD, None),
        P(SHARD),
        P(None, SHARD, None),
        P(None, SHARD, None),
    )
    return jax.shard_map(
        per_device,
        mesh=fine,
        in_specs=placed,
        out_specs=(
            P(split, None),
            P(split, None),
            P(SHARD),
            P(SHARD, None),
            P(SHARD, None),
            P(SHARD, None),
            P(SHARD),
            P(None, SHARD, None),
            P(None, SHARD, None),
        ),
        check_vma=False,
    )
```

```python
import jax
import jax.numpy as jnp
from jax import lax
from jax.experimental import pallas as pl
from jax.experimental.pallas import tpu as pltpu
from jax.sharding import Mesh, PartitionSpec as P

QUERY_HEADS = 12
KEY_VALUE_HEADS = 2
GROUP = QUERY_HEADS // KEY_VALUE_HEADS
HEAD_SIZE = 128
CAP = 80

EPSILON = 1e-06
ROPE_BASE = 10000.0
SCALE = HEAD_SIZE ** (-0.5)
SHARD = ("y", "x", "c")
CHIPS = ("y", "x")
REP = ("h", "z")
ALL = REP + SHARD
SWAP = [(0, 1), (1, 0)]

bf16 = jnp.bfloat16
f32 = jnp.float32

VMEM_LIMIT = 60 * 1024 * 1024
WHOLE = pl.BlockSpec(memory_space=pltpu.VMEM)
UNUSED = pl.BlockSpec(memory_space=pl.ANY)
SCALAR = pl.BlockSpec(memory_space=pltpu.SMEM)


def exchange(parts, axes):
    return lax.all_to_all(parts, axes, 0, 0, tiled=True)


def spread(part, ways, axes):
    return exchange(jnp.broadcast_to(part[None], (ways, *part.shape)), axes)


def matmul(left, right):
    return jnp.dot(left, right, preferred_element_type=f32)


def dot_general(left, right, dims):
    return lax.dot_general(left, right, (dims, ((), ())), preferred_element_type=f32)


def times_transposed(left, right):
    return dot_general(left, right, ((1,), (1,)))


def transposed_times(left, right):
    return dot_general(left, right, ((0,), (0,)))


def in_core_order(core, mine, other):
    return jnp.where(core == 0, jnp.stack([mine, other], 1), jnp.stack([other, mine], 1))


def call(kernel, out_shape, operands, earlier=(), specs=None, flops=0, scratch=()):
    specs = specs or [WHOLE] * len(operands)
    count = len(operands)

    def body(*refs):
        kernel(*refs[:count], *refs[count + len(earlier) :])

    size = sum(one.size * one.dtype.itemsize for one in (*operands, *out_shape))
    return pl.pallas_call(
        body,
        in_specs=[*specs, *([UNUSED] * len(earlier))],
        out_specs=[WHOLE] * len(out_shape),
        out_shape=out_shape,
        scratch_shapes=scratch,
        compiler_params=pltpu.CompilerParams(vmem_limit_bytes=VMEM_LIMIT),
        cost_estimate=pl.CostEstimate(flops=flops, bytes_accessed=size, transcendentals=0),
    )(*operands, *earlier)


def fetch(source_ref, to_ref, semaphores, along, base=0):
    rows, columns = to_ref.shape
    copies = []
    for i in range(to_ref.shape[along] // 512):
        chunk = pl.ds(i * 512, 512)
        if along:
            source = source_ref.at[:, pl.ds(base + i * 512, 512)]
            copy = pltpu.make_async_copy(source, to_ref.at[:, chunk], semaphores.at[i])
        else:
            source = source_ref.at[chunk, pl.ds(base, columns)]
            copy = pltpu.make_async_copy(source, to_ref.at[chunk, :], semaphores.at[i])
        copy.start()
        copies.append(copy)
    return copies


def fetch_parts(place_ref, mine_refs, other_refs, to_ref, semaphores):
    rows = to_ref.shape[2]
    part = to_ref.shape[3] // len(mine_refs)
    copies = []
    for k in range(len(mine_refs)):
        to = pl.ds(pl.multiple_of((place_ref[1] ^ k) * part, 128), part)
        owners = ((place_ref[0], mine_refs[k]), (1 - place_ref[0], other_refs[k]))
        for i, (owner, part_ref) in enumerate(owners):
            copy = pltpu.make_async_copy(
                part_ref.at[:, pl.ds(0, rows), :],
                to_ref.at[:, owner, :, to],
                semaphores.at[2 * k + i],
            )
            copy.start()
            copies.append(copy)
    return copies


def device_place():
    return jnp.stack([lax.axis_index("c"), lax.axis_index("z")]).astype(jnp.int32)


def shaped(shape, dtype):
    return jax.ShapeDtypeStruct(shape, dtype)


def inverse_rms(values):
    return lax.rsqrt(jnp.mean(values * values, axis=-1, keepdims=True) + EPSILON)


def norm_back(values, gain_row, upstream):
    factor = inverse_rms(values)
    grad_normed = upstream * gain_row
    grad_gain = upstream * values * factor
    cubed = factor * factor * factor
    grad_input = factor * grad_normed - values * cubed * jnp.mean(
        grad_normed * values, axis=-1, keepdims=True
    )
    return grad_input, grad_gain


def gain_tile(grad_gain, lower):
    rows = grad_gain.shape[0]
    lane = lax.broadcasted_iota(jnp.int32, (rows, 128), 1)
    return transposed_times(grad_gain, ((lane < 64) == lower).astype(f32))


def rotary_tables(position):
    half = HEAD_SIZE // 2
    frequency = ROPE_BASE ** (-jnp.arange(half, dtype=f32) / half)
    angle = position.astype(f32)[:, None] * frequency[None, :]
    cosine, sine = jnp.cos(angle), jnp.sin(angle)
    return jnp.concatenate([cosine, cosine], 1), jnp.concatenate([-sine, sine], 1)


def rotate(values, cosine, sine):
    return values * cosine + pltpu.roll(values, HEAD_SIZE // 2, 1) * sine


def project_qkv(tokens, gain, weights, cosine, sine, earlier):
    rows, width = tokens.shape
    kv_width = KEY_VALUE_HEADS * HEAD_SIZE
    turned = QUERY_HEADS + KEY_VALUE_HEADS
    total = width + 2 * kv_width

    def kernel(
        token_ref, gain_ref, all_ref, cos_ref, sin_ref, normed_ref, query_ref, keyval_ref, w_ref, sem
    ):
        copies = fetch(all_ref, w_ref, sem, 1)
        wide = token_ref[...].astype(f32)
        normed = (wide * inverse_rms(wide) * gain_ref[...]).astype(bf16)
        normed_ref[...] = normed
        cos, sin = cos_ref[...], sin_ref[...]
        for block in range(total // 256):
            if block % 2 == 0:
                copies[block // 2].wait()
            both = matmul(normed, w_ref[:, block * 256 : (block + 1) * 256])
            for i in range(2):
                head = 2 * block + i
                value = both[:, i * HEAD_SIZE : (i + 1) * HEAD_SIZE]
                if head < turned:
                    value = rotate(value, cos, sin)
                value = value.astype(bf16)
                if head < QUERY_HEADS:
                    query_ref[:, head * HEAD_SIZE : (head + 1) * HEAD_SIZE] = value
                else:
                    at = (head - QUERY_HEADS) * HEAD_SIZE
                    keyval_ref[:, at : at + HEAD_SIZE] = value

    return call(
        kernel,
        [
            shaped((rows, width), bf16),
            shaped((rows, width), bf16),
            shaped((rows, 2 * kv_width), bf16),
        ],
        (tokens, gain, weights, cosine, sine),
        earlier,
        specs=[WHOLE, WHOLE, UNUSED, WHOLE, WHOLE],
        flops=2 * rows * width * total,
        scratch=[pltpu.VMEM((width, total), bf16), pltpu.SemaphoreType.DMA((total // 512,))],
    )


def allowed_keys(first_ref, rows):
    row = lax.broadcasted_iota(jnp.int32, (rows, 2 * rows), 0)
    key = lax.broadcasted_iota(jnp.int32, (rows, 2 * rows), 1) - rows
    return (key <= row) & (key >= first_ref[...])


def probabilities(query, keys, allowed):
    scores = jnp.where(allowed, times_transposed(query, keys) * SCALE, -1000000000.0)
    exp_scores = jnp.exp(scores - jnp.max(scores, axis=-1, keepdims=True))
    return exp_scores / jnp.sum(exp_scores, axis=-1, keepdims=True)


def keys_and_values(before_ref, own_ref, group):
    both = []
    for base in (group * HEAD_SIZE, (KEY_VALUE_HEADS + group) * HEAD_SIZE):
        at = slice(base, base + HEAD_SIZE)
        both.append(jnp.concatenate([before_ref[:, at], own_ref[:, at]], axis=0))
    return both


def attend(queries, before, own, first, mine, other, tokens, gain, pick, earlier):
    rows, width = tokens.shape
    wide = len(mine)
    chips = mine[0].shape[0]

    def kernel(
        query_ref, before_ref, own_ref, first_ref, token_ref, gain_ref, pick_ref, place_ref, *refs
    ):
        turned_ref, residual_ref, picked_ref, attended_ref, w_ref, sem = refs[2 * wide :]
        copies = fetch_parts(place_ref, refs[:wide], refs[wide : 2 * wide], w_ref, sem)
        allowed = allowed_keys(first_ref, rows)
        for group in range(KEY_VALUE_HEADS):
            keys, values = keys_and_values(before_ref, own_ref, group)
            for head in range(group * GROUP, (group + 1) * GROUP):
                at = slice(head * HEAD_SIZE, (head + 1) * HEAD_SIZE)
                probs = probabilities(query_ref[:, at], keys, allowed)
                mixed = matmul(probs.astype(bf16), values)
                attended_ref[:, at] = mixed.astype(bf16)
                turned_ref[at, :] = mixed.T.astype(bf16)
        attended = attended_ref[...]
        for copy in copies:
            copy.wait()
        for block in range(width // 256):
            at = slice(block * 256, (block + 1) * 256)
            weights = w_ref[:, :, :, at].reshape(width, 256)
            branch = matmul(attended, weights).astype(bf16)
            residual_ref[:, at] = token_ref[:, at].astype(f32) + branch.astype(f32)
        residual = residual_ref[...]
        normed = (residual * inverse_rms(residual) * gain_ref[...]).astype(bf16)
        for block in range(width // 512):
            at = slice(block * 512, (block + 1) * 512)
            picked_ref[:, at] = matmul(pick_ref[...], normed[:, at]).astype(bf16)

    return call(
        kernel,
        [
            shaped((width, rows), bf16),
            shaped((rows, width), f32),
            shaped((pick.shape[0], width), bf16),
        ],
        (queries, before, own, first, tokens, gain, pick, device_place(), *mine, *other),
        earlier,
        specs=[*([WHOLE] * 7), SCALAR, *([UNUSED] * (2 * wide))],
        flops=2 * rows * width * width + 8 * rows * rows * width,
        scratch=[
            pltpu.VMEM((rows, width), bf16),
            pltpu.VMEM((chips, 2, width // (2 * chips), width), bf16),
            pltpu.SemaphoreType.DMA((2 * wide,)),
        ],
    )


def run_experts(picked, grad_out, parts, rows_up, rows_down):
    slots, width = picked.shape
    ways, chips, _, part = parts.shape
    wide = ways // 2
    ff = chips * 2 * rows_down
    each = slots // chips
    half = (rows_up + rows_down) // 2
    near = chips // 2

    def kernel(
        picked_any, grad_any, part_ref, back_any, expert_any, piece_any,
        picked_ref, grad_ref, up_w, down_w, gate_ref, upper_ref, acted_ref, pre_ref, back_ref, expert_ref,
        keep_ref, piece_ref, in_sem, up_sem, down_sem, out_sem,
    ):
        rows_in = pltpu.make_async_copy(picked_any, picked_ref, in_sem.at[0])
        grads_in = pltpu.make_async_copy(grad_any, grad_ref, in_sem.at[1])
        ups, downs = [], []
        for i in range(ways):
            to = pl.ds(i // 2 * part, part)
            ups.append(
                pltpu.make_async_copy(
                    part_ref.at[i, :, pl.ds(0, rows_up), :], up_w.at[:, i % 2, :, to], up_sem.at[i]
                )
            )
            downs.append(
                pltpu.make_async_copy(
                    part_ref.at[i, :, pl.ds(rows_up, rows_down), :],
                    down_w.at[:, i % 2, :, to],
                    down_sem.at[i],
                )
            )
        for copy in [rows_in, *ups, grads_in, *downs]:
            copy.start()
        for copy in [rows_in, *ups]:
            copy.wait()

        @pl.loop(0, ff // 256)
        def _(j):
            at = pl.multiple_of(j * 256, 256)
            for base, ref in ((0, gate_ref), (ff, upper_ref)):
                weights = up_w[:, :, :, pl.ds(base + at, 256)].reshape(width, 256)
                ref[:, pl.ds(at, 256)] = matmul(picked_ref[...], weights)

        for copy in [grads_in, *downs]:
            copy.wait()

        @pl.loop(0, 2)
        def _(j):
            at = pl.ds(pl.multiple_of(j * (ff // 2), 128), ff // 2)
            weights = down_w[pl.ds(j * near, near)].reshape(ff // 2, width)
            grad_act = times_transposed(grad_ref[...], weights)
            gate, up = gate_ref[:, at], upper_ref[:, at]
            sigmoid = 1.0 / (1.0 + jnp.exp(-gate))
            silu = gate * sigmoid
            acted_ref[:, at] = (silu * up).astype(bf16)
            grad_gate = grad_act * up * sigmoid * (1.0 + gate * (1.0 - sigmoid))
            pre_ref[:, at] = grad_gate.astype(bf16)
            upper = pl.ds(pl.multiple_of(ff + j * (ff // 2), 128), ff // 2)
            pre_ref[:, upper] = (grad_act * silu).astype(bf16)

        columns = width // 2

        @pl.loop(0, 2)
        def _(j):
            to = pl.ds(pl.multiple_of(j * columns, 128), columns)
            weights = up_w[pl.ds(j * near, near)].reshape(columns, 2 * ff)
            back = times_transposed(pre_ref[...], weights).astype(bf16)
            back_ref[:, :, to] = back.reshape(chips, each, columns)
            weights = down_w[:, :, :, to].reshape(ff, columns)
            forward = matmul(acted_ref[...], weights).astype(bf16)
            expert_ref[:, :, to] = forward.reshape(chips, each, columns)

        back_out = pltpu.make_async_copy(back_ref, back_any, out_sem.at[0])
        expert_out = pltpu.make_async_copy(expert_ref, expert_any, out_sem.at[3])
        back_out.start()
        expert_out.start()

        @pl.loop(0, 2)
        def _(s):
            for n in range(2):
                at = slice(n * columns, (n + 1) * columns)
                for m in range(near // 2):
                    base = pl.multiple_of(s * near * 2 * rows_up + m * 4 * rows_up, 128)
                    block = picked_ref[:, pl.ds(base, 4 * rows_up)]
                    up = transposed_times(block, pre_ref[:, at])
                    for i in range(4):
                        rows = up[i * rows_up : (i + 1) * rows_up]
                        k, c = 2 * m + i // 2, i % 2
                        keep_ref[k, c] = rows[half:]
                        low = rows[:half].astype(bf16)
                        for j in range(columns // part):
                            z = n * (columns // part) + j
                            piece_ref[z, c, s * near + k, 0] = low[:, j * part : (j + 1) * part]
                base = pl.multiple_of(s * near * 2 * rows_down, 128)
                block = acted_ref[:, pl.ds(base, near * 2 * rows_down)]
                down = transposed_times(block, grad_ref[:, at])
                for k in range(near):
                    for c in range(2):
                        low = (2 * k + c) * rows_down
                        rest = jnp.concatenate([keep_ref[k, c], down[low : low + rows_down]], axis=0)
                        rest = rest.astype(bf16)
                        for j in range(columns // part):
                            z = n * (columns // part) + j
                            piece_ref[z, c, s * near + k, 1] = rest[:, j * part : (j + 1) * part]
            chip = pl.ds(s * near, near)
            pltpu.make_async_copy(
                piece_ref.at[:, :, chip], piece_any.at[:, :, chip], out_sem.at[1 + s]
            ).start()

        back_out.wait()
        expert_out.wait()
        for s in range(2):
            chip = pl.ds(s * near, near)
            pltpu.make_async_copy(
                piece_ref.at[:, :, chip], piece_any.at[:, :, chip], out_sem.at[1 + s]
            ).wait()

    back = shaped((chips, each, width), bf16)
    pieces = shaped((wide, 2, chips, 2, half, part), bf16)
    return pl.pallas_call(
        kernel,
        in_specs=[UNUSED] * 3,
        out_specs=[UNUSED] * 3,
        out_shape=[back, back, pieces],
        scratch_shapes=[
            pltpu.VMEM((slots, width), bf16),
            pltpu.VMEM((slots, width), bf16),
            pltpu.VMEM((chips, 2, rows_up, width), bf16),
            pltpu.VMEM((chips, 2, rows_down, width), bf16),
            pltpu.VMEM((slots, ff), f32),
            pltpu.VMEM((slots, ff), f32),
            pltpu.VMEM((slots, ff), bf16),
            pltpu.VMEM((slots, 2 * ff), bf16),
            pltpu.VMEM(back.shape, bf16),
            pltpu.VMEM(back.shape, bf16),
            pltpu.VMEM((near, 2, rows_up - half, width // 2), f32),
            pltpu.VMEM(pieces.shape, bf16),
            pltpu.SemaphoreType.DMA((2,)),
            pltpu.SemaphoreType.DMA((ways,)),
            pltpu.SemaphoreType.DMA((ways,)),
            pltpu.SemaphoreType.DMA((4,)),
        ],
        compiler_params=pltpu.CompilerParams(vmem_limit_bytes=VMEM_LIMIT),
        cost_estimate=pl.CostEstimate(
            flops=2 * slots * 9 * width * ff,
            bytes_accessed=12 * slots * width + 8 * width * 3 * ff,
            transcendentals=0,
        ),
    )(picked, grad_out, parts)


def residual_grad(pick, returned, residual, gain, cotangent, earlier):
    rows, width = residual.shape
    slots = pick.shape[0]

    def kernel(pick_ref, back_ref, residual_ref, gain_ref, cot_ref, grad_ref, branch_ref, gain_grad_ref):
        for block in range(width // 512):
            at = slice(block * 512, (block + 1) * 512)
            back = back_ref[:, :, at].reshape(slots, 512)
            grad_ref[:, at] = transposed_times(pick_ref[...], back)
        grad, grad_gain = norm_back(residual_ref[...], gain_ref[...], grad_ref[...])
        grad = grad + cot_ref[...].astype(f32)
        grad_ref[...] = grad
        branch_ref[...] = grad.astype(bf16)
        gain_grad_ref[...] = gain_tile(grad_gain, False)

    return call(
        kernel,
        [shaped((rows, width), f32), shaped((rows, width), bf16), shaped((width, 128), f32)],
        (pick, returned, residual, gain, cotangent),
        earlier,
        flops=2 * slots * width * rows,
    )


def add_expert_rows(pick, weight, returned, residual, earlier):
    rows, width = residual.shape
    slots = pick.shape[0]

    def kernel(pick_ref, weight_ref, back_ref, residual_ref, out_ref):
        back = jnp.where(pick_ref[...] > 0, weight_ref[...], 0.0)
        high = back.astype(bf16)
        low = (back - high.astype(f32)).astype(bf16)
        for block in range(width // 512):
            at = slice(block * 512, (block + 1) * 512)
            expert = back_ref[:, :, at].reshape(slots, 512)
            mixture = transposed_times(high, expert) + transposed_times(low, expert)
            out_ref[:, at] = (residual_ref[:, at] + mixture).astype(bf16)

    return call(
        kernel,
        [shaped((rows, width), bf16)],
        (pick, weight, returned, residual),
        earlier,
        flops=4 * slots * width * rows,
    )[0]


def attend_back(grad_branch, mine, other, queries, before, own, first, cosine, sine, earlier):
    rows, width = grad_branch.shape
    kv_width = KEY_VALUE_HEADS * HEAD_SIZE
    wide = len(mine)
    chips = mine[0].shape[0]

    def kernel(
        grad_ref, query_ref, before_ref, own_ref, first_ref, cos_ref, sin_ref, place_ref, *refs
    ):
        out_ref, prev_ref, self_ref, attended_ref, prob_ref, w_ref, sem = refs[2 * wide :]
        copies = fetch_parts(place_ref, refs[:wide], refs[wide : 2 * wide], w_ref, sem)
        allowed = allowed_keys(first_ref, rows)
        for head in range(QUERY_HEADS):
            at = slice(head * HEAD_SIZE, (head + 1) * HEAD_SIZE)
            keys, _ = keys_and_values(before_ref, own_ref, head // GROUP)
            prob_ref[head] = probabilities(query_ref[:, at], keys, allowed)
        for copy in copies:
            copy.wait()
        for half in range(2):
            at = slice(half * (width // 2), (half + 1) * (width // 2))
            weights = w_ref[half * (chips // 2) : (half + 1) * (chips // 2)]
            weights = weights.reshape(width // 2, width)
            attended_ref[:, at] = times_transposed(grad_ref[...], weights).astype(bf16)
        cos, sin = cos_ref[...], sin_ref[...]
        for group in range(KEY_VALUE_HEADS):
            keys, values = keys_and_values(before_ref, own_ref, group)
            raws, lows, uppers, asked = [], [], [], []
            for head in range(group * GROUP, (group + 1) * GROUP):
                at = slice(head * HEAD_SIZE, (head + 1) * HEAD_SIZE)
                query, upper = query_ref[:, at], attended_ref[:, at]
                probs = prob_ref[head]
                grad_probs = times_transposed(upper, values)
                inner = jnp.sum(probs * grad_probs, axis=-1, keepdims=True)
                raw = (probs * (grad_probs - inner) * SCALE).astype(bf16)
                out_ref[head] = rotate(matmul(raw, keys), cos, -sin).astype(bf16)
                raws.append(raw)
                lows.append(probs.astype(bf16))
                uppers.append(upper)
                asked.append(query)
            for base, lefts, rights in (
                (group * HEAD_SIZE, raws, asked),
                (kv_width + group * HEAD_SIZE, lows, uppers),
            ):
                grad = transposed_times(
                    jnp.concatenate(lefts, axis=0), jnp.concatenate(rights, axis=0)
                )
                prev_ref[:, base : base + HEAD_SIZE] = grad[:rows].astype(bf16)
                self_ref[:, base : base + HEAD_SIZE] = grad[rows:]

    return call(
        kernel,
        [
            shaped((QUERY_HEADS, rows, HEAD_SIZE), bf16),
            shaped((rows, 2 * kv_width), bf16),
            shaped((rows, 2 * kv_width), f32),
        ],
        (grad_branch, queries, before, own, first, cosine, sine, device_place(), *mine, *other),
        earlier,
        specs=[*([WHOLE] * 7), SCALAR, *([UNUSED] * (2 * wide))],
        flops=2 * rows * width * width + 20 * rows * rows * width,
        scratch=[
            pltpu.VMEM((rows, width), bf16),
            pltpu.VMEM((QUERY_HEADS, rows, 2 * rows), f32),
            pltpu.VMEM((chips, 2, width // (2 * chips), width), bf16),
            pltpu.SemaphoreType.DMA((2 * wide,)),
        ],
    )


def qkv_blocks_of(grad_queries, grad_own, from_next, cosine, sine, earlier):
    heads, rows, size = grad_queries.shape
    total = heads + 2 * KEY_VALUE_HEADS

    def kernel(query_ref, own_ref, next_ref, cos_ref, sin_ref, out_ref):
        out_ref[:heads] = query_ref[...]
        for i in range(2 * KEY_VALUE_HEADS):
            at = slice(i * size, (i + 1) * size)
            grad = own_ref[:, at] + next_ref[:, at].astype(f32)
            if i < KEY_VALUE_HEADS:
                grad = rotate(grad, cos_ref[...], -sin_ref[...])
            out_ref[heads + i] = grad.astype(bf16)

    return call(
        kernel,
        [shaped((total, rows, size), bf16)],
        (grad_queries, grad_own, from_next, cosine, sine),
        earlier,
    )[0]


def input_grad(blocks, weights, tokens, gain, grad_residual, gain_grad, earlier):
    rows, width = tokens.shape
    columns = blocks.shape[0] * HEAD_SIZE

    def kernel(
        block_ref, all_ref, token_ref, gain_ref, residual_ref, other_ref, out_ref, tile_ref, w_ref, sem
    ):
        copies = fetch(all_ref, w_ref, sem, 1)
        total = jnp.zeros((rows, width), f32)
        for i in range(blocks.shape[0] // 2):
            if i % 2 == 0:
                copies[i // 2].wait()
            pair = jnp.concatenate([block_ref[2 * i], block_ref[2 * i + 1]], axis=1)
            total = total + times_transposed(pair, w_ref[:, i * 256 : (i + 1) * 256])
        grad, grad_gain = norm_back(token_ref[...].astype(f32), gain_ref[...], total)
        out_ref[...] = (residual_ref[...] + grad).astype(bf16)
        tile_ref[...] = (other_ref[...] + gain_tile(grad_gain, True)).astype(bf16)

    return call(
        kernel,
        [shaped((rows, width), bf16), shaped((width, 128), bf16)],
        (blocks, weights, tokens, gain, grad_residual, gain_grad),
        earlier,
        specs=[WHOLE, UNUSED, WHOLE, WHOLE, WHOLE, WHOLE],
        flops=2 * rows * width * columns,
        scratch=[pltpu.VMEM((width, columns), bf16), pltpu.SemaphoreType.DMA((columns // 512,))],
    )


def gather_over_z(part):
    wide = lax.axis_size("z")
    return [part] + [
        lax.ppermute(part, "z", [(i, i ^ k) for i in range(wide)]) for k in range(1, wide)
    ]


def expert_outputs(pieces, rows_up, rows_down):
    wide, experts, _, half, part = pieces.shape
    width = wide * part
    split = rows_up - half

    def kernel(piece_ref, up_ref, down_ref):
        for z in range(wide):
            at = slice(z * part, (z + 1) * part)
            rest = piece_ref[z, 0, 1].astype(f32)
            up_ref[0, :half, at] = piece_ref[z, 0, 0].astype(f32)
            up_ref[0, half:, at] = rest[:split]
            down_ref[0, :, at] = rest[split:]

    return pl.pallas_call(
        kernel,
        grid=(experts,),
        in_specs=[pl.BlockSpec((wide, 1, 2, half, part), lambda e: (0, e, 0, 0, 0))],
        out_specs=[
            pl.BlockSpec((1, rows_up, width), lambda e: (e, 0, 0)),
            pl.BlockSpec((1, rows_down, width), lambda e: (e, 0, 0)),
        ],
        out_shape=[
            shaped((experts, rows_up, width), f32),
            shaped((experts, rows_down, width), f32),
        ],
    )(pieces)


def part_to_square(value, across, axis):
    size = value.shape[axis] // 2
    mine = lax.dynamic_slice_in_dim(value, across * size, size, axis)
    sent = lax.dynamic_slice_in_dim(value, (1 - across) * size, size, axis)
    return jnp.stack([mine, lax.ppermute(sent, "x", SWAP)])


def part_to_core(value, core, axis):
    size = value.shape[axis] // 2
    return lax.ppermute(lax.dynamic_slice_in_dim(value, (1 - core) * size, size, axis), "c", SWAP)


def twice(value, earlier):
    size = value.shape[0]

    def kernel(in_ref, out_ref):
        out_ref[:size] = in_ref[...]
        out_ref[size:] = in_ref[...]

    return call(kernel, [shaped((2 * size, *value.shape[1:]), value.dtype)], (value,), earlier)[0]


def sum_of_halves(value, earlier):
    size = value.shape[0] // 2

    def kernel(in_ref, out_ref):
        out_ref[...] = (in_ref[:size].astype(f32) + in_ref[size:].astype(f32)).astype(bf16)

    return call(kernel, [shaped((size, *value.shape[1:]), value.dtype)], (value,), earlier)[0]


def hold(values, earlier):
    def kernel(*refs):
        del refs

    return pl.pallas_call(
        kernel,
        in_specs=[UNUSED] * (len(values) + len(earlier)),
        out_specs=[UNUSED] * len(values),
        out_shape=[shaped(one.shape, one.dtype) for one in values],
        input_output_aliases={i: i for i in range(len(values))},
    )(*values, *earlier)


def out_weight_grads(near, far, grad_near, grad_far, ways, earlier):
    _, width, rows = near.shape
    columns = grad_far.shape[2]
    core = lax.axis_index("c").astype(jnp.int32).reshape(1)

    def kernel(core_ref, near_ref, far_ref, grad_near_ref, grad_far_ref, out_ref, left_ref):
        at = pl.ds(pl.multiple_of(core_ref[0] * columns, 128), columns)
        for i in range(2):
            left_ref[:, i * rows : (i + 1) * rows] = near_ref[i]
            left_ref[:, (2 + i) * rows : (3 + i) * rows] = far_ref[i]
        right = jnp.concatenate(
            [grad_near_ref[0, :, at], grad_near_ref[1, :, at], grad_far_ref[0], grad_far_ref[1]],
            axis=0,
        )
        each = width // ways
        for i in range(ways):
            left = left_ref[i * each : (i + 1) * each, :]
            out_ref[i] = matmul(left, right).astype(bf16)

    return call(
        kernel,
        [shaped((ways, width // ways, columns), bf16)],
        (core, near, far, grad_near, grad_far),
        earlier,
        specs=[SCALAR, *([WHOLE] * 4)],
        flops=8 * width * rows * columns,
        scratch=[pltpu.VMEM((width, 4 * rows), bf16)],
    )[0]


def qkv_weight_grads(near, far, grad_near, grad_far, ways, earlier):
    _, rows, width = near.shape
    heads = grad_far.shape[1]
    columns = heads * HEAD_SIZE
    core = lax.axis_index("c").astype(jnp.int32).reshape(1)

    def kernel(core_ref, near_ref, far_ref, grad_near_ref, grad_far_ref, out_ref, left_ref, right_ref):
        for i in range(2):
            left_ref[i * rows : (i + 1) * rows, :] = near_ref[i]
            left_ref[(2 + i) * rows : (3 + i) * rows, :] = far_ref[i]
            for head in range(heads):
                at = slice(head * HEAD_SIZE, (head + 1) * HEAD_SIZE)
                mine = grad_near_ref[i, core_ref[0] * heads + head]
                right_ref[i * rows : (i + 1) * rows, at] = mine
                right_ref[(2 + i) * rows : (3 + i) * rows, at] = grad_far_ref[i, head]
        each = width // ways
        for i in range(ways):
            block = slice(i * each, (i + 1) * each)
            out_ref[i] = transposed_times(left_ref[:, block], right_ref[...]).astype(bf16)

    return call(
        kernel,
        [shaped((ways, width // ways, columns), bf16)],
        (core, near, far, grad_near, grad_far),
        earlier,
        specs=[SCALAR, *([WHOLE] * 4)],
        flops=8 * width * rows * columns,
        scratch=[pltpu.VMEM((4 * rows, width), bf16), pltpu.VMEM((4 * rows, columns), bf16)],
    )[0]


def moved_over_y(blocks):
    wide = lax.axis_size("y")
    y = lax.axis_index("y")
    moved = [lax.dynamic_index_in_dim(blocks, y, 0, keepdims=False)]
    for k in range(1, wide):
        sent = lax.dynamic_index_in_dim(blocks, y ^ k, 0, keepdims=False)
        moved.append(lax.ppermute(sent, "y", [(i, i ^ k) for i in range(wide)]))
    return moved


def tiles_of(qkv, out, gains, tiles, squares):
    terms = qkv.shape[0]
    rows = qkv.shape[1] // squares
    count = qkv.shape[2] // HEAD_SIZE

    def kernel(qkv_ref, out_ref, *refs):
        gain_refs, tile_ref = refs[:-1], refs[-1]
        for t in range(tiles):
            for p in range(squares):
                block = slice(p * rows, (p + 1) * rows)
                if t < count:
                    at = slice(t * HEAD_SIZE, (t + 1) * HEAD_SIZE)
                    values = [qkv_ref[i, block, at] for i in range(terms)]
                elif t < tiles - 1:
                    at = slice((t - count) * HEAD_SIZE, (t - count + 1) * HEAD_SIZE)
                    values = [out_ref[block, at]]
                else:
                    values = [ref[block] for ref in gain_refs]
                total = values[0].astype(f32)
                for value in values[1:]:
                    total = total + value.astype(f32)
                tile_ref[t * squares + p] = total.astype(bf16)

    return call(
        kernel, [shaped((tiles * squares, rows, HEAD_SIZE), bf16)], (qkv, out, *gains)
    )[0]


def sum_and_copy(parts, squares, copies, earlier):
    count, rows, columns = parts.shape

    def kernel(part_ref, copy_ref):
        for p in range(squares):
            total = part_ref[p].astype(f32)
            for i in range(1, count // squares):
                total = total + part_ref[i * squares + p].astype(f32)
            low = total.astype(bf16)
            for i in range(copies):
                copy_ref[i, p] = low

    return call(kernel, [shaped((copies, squares, rows, columns), bf16)], (parts,), earlier)[0]


def attention_outputs(tiles, query_width, kv_width, earlier):
    count, squares, rows, column = tiles.shape
    heads = (query_width + kv_width) // column // squares
    outs = count - 1 - heads

    def kernel(tile_ref, query_ref, keyval_ref, out_ref, gain_ref):
        gains = jnp.zeros((rows, column), f32)
        for q in range(squares):
            for t in range(heads):
                at = (q * heads + t) * column
                value = tile_ref[t, q].astype(f32)
                if at < query_width:
                    query_ref[:, at : at + column] = value
                else:
                    keyval_ref[:, at - query_width : at - query_width + column] = value
            for t in range(outs):
                at = (q * outs + t) * column
                out_ref[:, at : at + column] = tile_ref[heads + t, q].astype(f32)
            gains = gains + tile_ref[count - 1, q].astype(f32)
        gain_ref[...] = gains

    return call(
        kernel,
        [
            shaped((rows, query_width), f32),
            shaped((rows, kv_width), f32),
            shaped((rows, squares * outs * column), f32),
            shaped((rows, column), f32),
        ],
        (tiles,),
        earlier,
    )


def per_device(
    tokens,
    cotangent,
    seq_lengths,
    seq_order,
    routes,
    gate_weights,
    attn_gain,
    w_query,
    key_value_weight,
    w_out,
    ffn_gain,
    w_gateup,
    w_down,
):
    wide_z = lax.axis_size("z")
    shards = lax.axis_size("y") * lax.axis_size("x") * lax.axis_size("c")
    core = lax.axis_index("c")
    shard = (lax.axis_index("y") * lax.axis_size("x") + lax.axis_index("x")) * 2 + core
    rows, width = tokens.shape
    experts = w_gateup.shape[0]
    kv_width = KEY_VALUE_HEADS * HEAD_SIZE
    owned = width // shards

    qkv_full = lax.all_gather(
        jnp.concatenate([w_query, key_value_weight], 1), SHARD, axis=0, tiled=True
    )
    part = width // wide_z
    rows_out, rows_up, rows_down = w_out.shape[0], w_gateup.shape[1], w_down.shape[1]
    column = lax.axis_index("z") * part
    gains_own = jnp.pad(jnp.stack([attn_gain, ffn_gain]), ((0, 14), (0, part - owned)))
    out_part = jnp.concatenate(
        [lax.dynamic_slice_in_dim(w_out, column, part, 1), gains_own], axis=0
    )
    expert_part = jnp.concatenate(
        [
            lax.dynamic_slice_in_dim(w_gateup, column, part, 2),
            lax.dynamic_slice_in_dim(w_down, column, part, 2),
        ],
        axis=1,
    )
    out_part = spread(out_part, experts, CHIPS)
    expert_part = exchange(hold((expert_part,), (out_part,))[0], CHIPS)
    gains_mine = out_part[:, rows_out : rows_out + 2, :owned]
    gains = in_core_order(core, gains_mine, lax.ppermute(gains_mine, "c", SWAP))
    gains = gains.transpose(2, 0, 1, 3).reshape(2, width).astype(f32)
    gain_attn, gain_ffn = gains[:1], gains[1:]
    out_mine = gather_over_z(out_part)
    out_other = [lax.ppermute(one, "c", SWAP) for one in out_mine]
    chosen = routes[:, :, None] == jnp.arange(experts, dtype=jnp.int32)
    member = jnp.any(chosen, axis=1)
    weight = jnp.sum(jnp.where(chosen, gate_weights[:, :, None], 0.0), axis=1)
    place = jnp.cumsum(member.astype(jnp.int32), axis=0) - 1
    slot = jnp.where(member, place, -1).T
    picks = slot[:, None, :] == jnp.arange(CAP, dtype=jnp.int32)[None, :, None]
    pick = picks.astype(bf16).reshape(experts * CAP, rows)
    slot_weight = jnp.sum(jnp.where(picks, weight.T[:, None, :], 0.0), axis=2)
    grad_out = matmul(pick, cotangent) * slot_weight.reshape(-1, 1)
    grad_out_sent = hold((grad_out.astype(bf16),), (expert_part,))[0]
    grad_out = exchange(grad_out_sent, CHIPS)


    lengths = seq_lengths[0]
    starts = jnp.cumsum(lengths) - lengths
    row_at = shard * rows + jnp.arange(rows, dtype=jnp.int32)
    first_at = jnp.max(jnp.where(starts[None, :] <= row_at[:, None], starts[None, :], 0), axis=1)
    cosine, sine = rotary_tables(row_at - first_at)
    first = (first_at - shard * rows).astype(jnp.int32)[:, None]
    normed, queries, keyval = project_qkv(
        tokens, gain_attn, qkv_full, cosine, sine, (*out_mine[1:], expert_part, grad_out_sent)
    )
    expert_parts = lax.all_gather(hold((expert_part,), (queries,))[0], ("z", "c"), axis=0)
    ring = [(i, (i + 1) % shards) for i in range(shards)]
    back_ring = [((i + 1) % shards, i) for i in range(shards)]
    before = lax.ppermute(keyval, SHARD, ring)
    attended_turned, residual, picked = attend(
        queries, before, keyval, first, out_mine, out_other, tokens, gain_ffn, pick, ()
    )

    picked = exchange(hold((picked,), (grad_out,))[0], CHIPS)
    normed, attended_turned = hold((normed, attended_turned), (picked,))
    normed_moved = lax.ppermute(normed, "x", SWAP)
    attended_moved = lax.ppermute(attended_turned, "x", SWAP)
    returned, expert_rows, pieces = run_experts(
        picked, grad_out, expert_parts, rows_up, rows_down
    )
    returned, expert_rows, pieces = hold(
        (returned, expert_rows, pieces), (normed_moved, attended_moved)
    )
    normed_near = jnp.stack([normed, normed_moved])
    attended_near = jnp.stack([attended_turned, attended_moved])
    returned = exchange(returned, CHIPS)
    expert_rows = exchange(expert_rows, CHIPS)
    normed_far = lax.ppermute(normed_near, "c", SWAP)
    attended_far = lax.ppermute(attended_near, "c", SWAP)
    pieces = pieces.reshape(2 * wide_z, *pieces.shape[2:])
    over_z = lax.psum_scatter(pieces, ("z", "c"), scatter_dimension=0, tiled=False)

    grad_residual, grad_branch, gain_grad = residual_grad(
        pick, returned, residual, gain_ffn, cotangent, (normed_far, attended_far)
    )
    across = lax.axis_index("x")
    branch_near = part_to_square(grad_branch, across, 1)
    grad_queries, grad_before, grad_own = attend_back(
        grad_branch,
        out_mine,
        out_other,
        queries,
        before,
        keyval,
        first,
        cosine,
        sine,
        (),
    )
    from_next = lax.ppermute(grad_before, SHARD, back_ring)
    grad_blocks = qkv_blocks_of(
        grad_queries, grad_own, from_next, cosine, sine, ()
    )

    blocks_near = part_to_square(grad_blocks, across, 0)
    doubled = twice(over_z, (expert_rows, blocks_near))
    qkv_grads = qkv_weight_grads(
        normed_near,
        normed_far,
        blocks_near,
        part_to_core(blocks_near, core, 1),
        lax.axis_size("y"),
        (doubled,),
    )
    over_rep = exchange(doubled, ("h", *CHIPS))
    out_terms = out_weight_grads(
        attended_near,
        attended_far,
        branch_near,
        part_to_core(branch_near, core, 2),
        lax.axis_size("y"),
        (doubled,),
    )
    out_grads = lax.psum_scatter(out_terms, "y", scatter_dimension=0, tiled=True)
    grad_tokens, tile = input_grad(
        grad_blocks, qkv_full, tokens, gain_attn, grad_residual, gain_grad, (qkv_grads,)
    )
    over_rep = sum_of_halves(over_rep, (tile,))
    gain_terms = moved_over_y(tile.reshape(lax.axis_size("y"), -1, HEAD_SIZE))
    qkv_grads = exchange(qkv_grads, "y")
    shard_gateup, shard_down = expert_outputs(
        lax.all_gather(over_rep, "z", axis=0), rows_up, rows_down
    )
    reps = 2 * wide_z
    tiles = exchange(tiles_of(qkv_grads, out_grads.reshape(-1, part), gain_terms, reps, 4), REP + ("x", "c"))
    tiles = exchange(sum_and_copy(tiles, 4, reps, ()), REP)
    grad_query, grad_keyval, grad_out_w, gain_sums = attention_outputs(
        tiles, width, 2 * kv_width, (shard_down,)
    )

    output = add_expert_rows(
        pick, slot_weight.reshape(-1, 1), expert_rows, residual, (qkv_grads,)
    )
    return (
        output,
        grad_tokens,
        gain_sums[:, 0],
        grad_query,
        grad_keyval,
        grad_out_w,
        gain_sums[:, 64],
        shard_gateup,
        shard_down,
    )


def solution(mesh):
    reps, shards = mesh.devices.shape
    fine = Mesh(mesh.devices.reshape(2, reps // 2, shards // 4, 2, 2), ALL)
    split = ALL
    placed = (
        P(split, None),
        P(split, None),
        P(REP, None),
        P(REP, None),
        P(split, None),
        P(split, None),
        P(SHARD),
        P(SHARD, None),
        P(SHARD, None),
        P(SHARD, None),
        P(SHARD),
        P(None, SHARD, None),
        P(None, SHARD, None),
    )
    return jax.shard_map(
        per_device,
        mesh=fine,
        in_specs=placed,
        out_specs=(
            P(split, None),
            P(split, None),
            P(SHARD),
            P(SHARD, None),
            P(SHARD, None),
            P(SHARD, None),
            P(SHARD),
            P(None, SHARD, None),
            P(None, SHARD, None),
        ),
        check_vma=False,
    )
```

```python
import jax
import jax.numpy as jnp
from jax import lax
from jax.experimental import pallas as pl
from jax.experimental.pallas import tpu as pltpu
from jax.sharding import Mesh, PartitionSpec as P

QUERY_HEADS = 12
KEY_VALUE_HEADS = 2
GROUP = QUERY_HEADS // KEY_VALUE_HEADS
HEAD_SIZE = 128
CAP = 80

EPSILON = 1e-06
ROPE_BASE = 10000.0
SCALE = HEAD_SIZE ** (-0.5)
SHARD = ("y", "x", "c")
CHIPS = ("y", "x")
REP = ("h", "z")
ALL = REP + SHARD
SWAP = [(0, 1), (1, 0)]

bf16 = jnp.bfloat16
f32 = jnp.float32

VMEM_LIMIT = 63 * 1024 * 1024
WHOLE = pl.BlockSpec(memory_space=pltpu.VMEM)
UNUSED = pl.BlockSpec(memory_space=pl.ANY)
SCALAR = pl.BlockSpec(memory_space=pltpu.SMEM)


def exchange(parts, axes):
    return lax.all_to_all(parts, axes, 0, 0, tiled=True)


def spread(part, ways, axes):
    return exchange(jnp.broadcast_to(part[None], (ways, *part.shape)), axes)


def matmul(left, right):
    return jnp.dot(left, right, preferred_element_type=f32)


def dot_general(left, right, dims):
    return lax.dot_general(left, right, (dims, ((), ())), preferred_element_type=f32)


def times_transposed(left, right):
    return dot_general(left, right, ((1,), (1,)))


def transposed_times(left, right):
    return dot_general(left, right, ((0,), (0,)))


def in_core_order(core, mine, other):
    return jnp.where(core == 0, jnp.stack([mine, other], 1), jnp.stack([other, mine], 1))


def call(kernel, out_shape, operands, earlier=(), specs=None, flops=0, scratch=()):
    specs = specs or [WHOLE] * len(operands)
    count = len(operands)

    def body(*refs):
        kernel(*refs[:count], *refs[count + len(earlier) :])

    size = sum(one.size * one.dtype.itemsize for one in (*operands, *out_shape))
    return pl.pallas_call(
        body,
        in_specs=[*specs, *([UNUSED] * len(earlier))],
        out_specs=[WHOLE] * len(out_shape),
        out_shape=out_shape,
        scratch_shapes=scratch,
        compiler_params=pltpu.CompilerParams(vmem_limit_bytes=VMEM_LIMIT),
        cost_estimate=pl.CostEstimate(flops=flops, bytes_accessed=size, transcendentals=0),
    )(*operands, *earlier)


def fetch(source_ref, to_ref, semaphores, along, base=0):
    rows, columns = to_ref.shape
    copies = []
    for i in range(to_ref.shape[along] // 512):
        chunk = pl.ds(i * 512, 512)
        if along:
            source = source_ref.at[:, pl.ds(base + i * 512, 512)]
            copy = pltpu.make_async_copy(source, to_ref.at[:, chunk], semaphores.at[i])
        else:
            source = source_ref.at[chunk, pl.ds(base, columns)]
            copy = pltpu.make_async_copy(source, to_ref.at[chunk, :], semaphores.at[i])
        copy.start()
        copies.append(copy)
    return copies


def fetch_parts(place_ref, mine_refs, other_refs, to_ref, semaphores):
    rows = to_ref.shape[2]
    part = to_ref.shape[3] // len(mine_refs)
    copies = []
    for k in range(len(mine_refs)):
        to = pl.ds(pl.multiple_of((place_ref[1] ^ k) * part, 128), part)
        owners = ((place_ref[0], mine_refs[k]), (1 - place_ref[0], other_refs[k]))
        for i, (owner, part_ref) in enumerate(owners):
            copy = pltpu.make_async_copy(
                part_ref.at[:, pl.ds(0, rows), :],
                to_ref.at[:, owner, :, to],
                semaphores.at[2 * k + i],
            )
            copy.start()
            copies.append(copy)
    return copies


def device_place():
    return jnp.stack([lax.axis_index("c"), lax.axis_index("z")]).astype(jnp.int32)


def shaped(shape, dtype):
    return jax.ShapeDtypeStruct(shape, dtype)


def inverse_rms(values):
    return lax.rsqrt(jnp.mean(values * values, axis=-1, keepdims=True) + EPSILON)


def norm_back(values, gain_row, upstream):
    factor = inverse_rms(values)
    grad_normed = upstream * gain_row
    grad_gain = upstream * values * factor
    cubed = factor * factor * factor
    grad_input = factor * grad_normed - values * cubed * jnp.mean(
        grad_normed * values, axis=-1, keepdims=True
    )
    return grad_input, grad_gain


def gain_tile(grad_gain, lower):
    rows = grad_gain.shape[0]
    lane = lax.broadcasted_iota(jnp.int32, (rows, 128), 1)
    return transposed_times(grad_gain, ((lane < 64) == lower).astype(f32))


def rotary_tables(position):
    half = HEAD_SIZE // 2
    frequency = ROPE_BASE ** (-jnp.arange(half, dtype=f32) / half)
    angle = position.astype(f32)[:, None] * frequency[None, :]
    cosine, sine = jnp.cos(angle), jnp.sin(angle)
    return jnp.concatenate([cosine, cosine], 1), jnp.concatenate([-sine, sine], 1)


def rotate(values, cosine, sine):
    return values * cosine + pltpu.roll(values, HEAD_SIZE // 2, 1) * sine


def project_qkv(tokens, gain, weights, cosine, sine, earlier):
    rows, width = tokens.shape
    kv_width = KEY_VALUE_HEADS * HEAD_SIZE
    turned = QUERY_HEADS + KEY_VALUE_HEADS
    total = width + 2 * kv_width

    def kernel(
        token_ref, gain_ref, all_ref, cos_ref, sin_ref, normed_ref, query_ref, keyval_ref, w_ref, sem
    ):
        copies = fetch(all_ref, w_ref, sem, 1)
        wide = token_ref[...].astype(f32)
        normed = (wide * inverse_rms(wide) * gain_ref[...]).astype(bf16)
        normed_ref[...] = normed
        cos, sin = cos_ref[...], sin_ref[...]
        for block in range(total // 256):
            if block % 2 == 0:
                copies[block // 2].wait()
            both = matmul(normed, w_ref[:, block * 256 : (block + 1) * 256])
            for i in range(2):
                head = 2 * block + i
                value = both[:, i * HEAD_SIZE : (i + 1) * HEAD_SIZE]
                if head < turned:
                    value = rotate(value, cos, sin)
                value = value.astype(bf16)
                if head < QUERY_HEADS:
                    query_ref[:, head * HEAD_SIZE : (head + 1) * HEAD_SIZE] = value
                else:
                    at = (head - QUERY_HEADS) * HEAD_SIZE
                    keyval_ref[:, at : at + HEAD_SIZE] = value

    return call(
        kernel,
        [
            shaped((rows, width), bf16),
            shaped((rows, width), bf16),
            shaped((rows, 2 * kv_width), bf16),
        ],
        (tokens, gain, weights, cosine, sine),
        earlier,
        specs=[WHOLE, WHOLE, UNUSED, WHOLE, WHOLE],
        flops=2 * rows * width * total,
        scratch=[pltpu.VMEM((width, total), bf16), pltpu.SemaphoreType.DMA((total // 512,))],
    )


def allowed_keys(first_ref, rows):
    row = lax.broadcasted_iota(jnp.int32, (rows, 2 * rows), 0)
    key = lax.broadcasted_iota(jnp.int32, (rows, 2 * rows), 1) - rows
    return (key <= row) & (key >= first_ref[...])


def probabilities(query, keys, allowed):
    scores = jnp.where(allowed, times_transposed(query, keys) * SCALE, -1000000000.0)
    exp_scores = jnp.exp(scores - jnp.max(scores, axis=-1, keepdims=True))
    return exp_scores / jnp.sum(exp_scores, axis=-1, keepdims=True)


def keys_and_values(before_ref, own_ref, group):
    both = []
    for base in (group * HEAD_SIZE, (KEY_VALUE_HEADS + group) * HEAD_SIZE):
        at = slice(base, base + HEAD_SIZE)
        both.append(jnp.concatenate([before_ref[:, at], own_ref[:, at]], axis=0))
    return both


def attend(queries, before, own, first, mine, other, tokens, gain, pick, earlier):
    rows, width = tokens.shape
    wide = len(mine)
    chips = mine[0].shape[0]

    def kernel(
        query_ref, before_ref, own_ref, first_ref, token_ref, gain_ref, pick_ref, place_ref, *refs
    ):
        turned_ref, residual_ref, picked_ref, attended_ref, w_ref, sem = refs[2 * wide :]
        copies = fetch_parts(place_ref, refs[:wide], refs[wide : 2 * wide], w_ref, sem)
        allowed = allowed_keys(first_ref, rows)
        for group in range(KEY_VALUE_HEADS):
            keys, values = keys_and_values(before_ref, own_ref, group)
            for head in range(group * GROUP, (group + 1) * GROUP):
                at = slice(head * HEAD_SIZE, (head + 1) * HEAD_SIZE)
                probs = probabilities(query_ref[:, at], keys, allowed)
                mixed = matmul(probs.astype(bf16), values)
                attended_ref[:, at] = mixed.astype(bf16)
                turned_ref[at, :] = mixed.T.astype(bf16)
        attended = attended_ref[...]
        for copy in copies:
            copy.wait()
        for block in range(width // 256):
            at = slice(block * 256, (block + 1) * 256)
            weights = w_ref[:, :, :, at].reshape(width, 256)
            branch = matmul(attended, weights).astype(bf16)
            residual_ref[:, at] = token_ref[:, at].astype(f32) + branch.astype(f32)
        residual = residual_ref[...]
        normed = (residual * inverse_rms(residual) * gain_ref[...]).astype(bf16)
        for block in range(width // 512):
            at = slice(block * 512, (block + 1) * 512)
            picked_ref[:, at] = matmul(pick_ref[...], normed[:, at]).astype(bf16)

    return call(
        kernel,
        [
            shaped((width, rows), bf16),
            shaped((rows, width), f32),
            shaped((pick.shape[0], width), bf16),
        ],
        (queries, before, own, first, tokens, gain, pick, device_place(), *mine, *other),
        earlier,
        specs=[*([WHOLE] * 7), SCALAR, *([UNUSED] * (2 * wide))],
        flops=2 * rows * width * width + 8 * rows * rows * width,
        scratch=[
            pltpu.VMEM((rows, width), bf16),
            pltpu.VMEM((chips, 2, width // (2 * chips), width), bf16),
            pltpu.SemaphoreType.DMA((2 * wide,)),
        ],
    )


def expert_copies(part_ref, to_ref, base, rows, semaphores):
    ways, part = part_ref.shape[0], part_ref.shape[3]
    return [
        pltpu.make_async_copy(
            part_ref.at[i, :, pl.ds(base, rows), :],
            to_ref.at[:, i % 2, :, pl.ds(i // 2 * part, part)],
            semaphores.at[i],
        )
        for i in range(ways)
    ]


def run_experts(picked, grad_out, parts, rows_up, rows_down):
    slots, width = picked.shape
    ways, chips, _, part = parts.shape
    ff = chips * 2 * rows_down
    each = slots // chips
    near = chips // 2

    def kernel(
        picked_any, grad_any, part_ref, back_any, acted_any, pre_any,
        picked_ref, grad_ref, up_w, down_w, gate_ref, upper_ref, acted_ref, pre_ref, back_ref,
        in_sem, up_sem, down_sem, out_sem,
    ):
        rows_in = pltpu.make_async_copy(picked_any, picked_ref, in_sem.at[0])
        grads_in = pltpu.make_async_copy(grad_any, grad_ref, in_sem.at[1])
        ups = expert_copies(part_ref, up_w, 0, rows_up, up_sem)
        downs = expert_copies(part_ref, down_w, rows_up, rows_down, down_sem)
        for copy in [rows_in, *ups, grads_in, *downs]:
            copy.start()
        for copy in [rows_in, *ups]:
            copy.wait()

        @pl.loop(0, ff // 256)
        def _(j):
            at = pl.multiple_of(j * 256, 256)
            for base, ref in ((0, gate_ref), (ff, upper_ref)):
                weights = up_w[:, :, :, pl.ds(base + at, 256)].reshape(width, 256)
                ref[:, pl.ds(at, 256)] = matmul(picked_ref[...], weights)

        for copy in [grads_in, *downs]:
            copy.wait()

        @pl.loop(0, 2)
        def _(j):
            at = pl.ds(pl.multiple_of(j * (ff // 2), 128), ff // 2)
            weights = down_w[pl.ds(j * near, near)].reshape(ff // 2, width)
            grad_act = times_transposed(grad_ref[...], weights)
            gate, up = gate_ref[:, at], upper_ref[:, at]
            sigmoid = 1.0 / (1.0 + jnp.exp(-gate))
            silu = gate * sigmoid
            acted_ref[:, at] = (silu * up).astype(bf16)
            grad_gate = grad_act * up * sigmoid * (1.0 + gate * (1.0 - sigmoid))
            pre_ref[:, at] = grad_gate.astype(bf16)
            upper = pl.ds(pl.multiple_of(ff + j * (ff // 2), 128), ff // 2)
            pre_ref[:, upper] = (grad_act * silu).astype(bf16)

        outs = [
            pltpu.make_async_copy(acted_ref, acted_any, out_sem.at[0]),
            pltpu.make_async_copy(pre_ref, pre_any, out_sem.at[1]),
        ]
        for copy in outs:
            copy.start()
        columns = width // 2
        for j in range(2):
            to = slice(j * columns, (j + 1) * columns)
            weights = up_w[j * near : (j + 1) * near].reshape(columns, 2 * ff)
            back = times_transposed(pre_ref[...], weights).astype(bf16)
            back_ref[:, :, to] = back.reshape(chips, each, columns)
            copy = pltpu.make_async_copy(
                back_ref.at[:, :, to], back_any.at[:, :, to], out_sem.at[2 + j]
            )
            copy.start()
            outs.append(copy)
        for copy in outs:
            copy.wait()

    back = shaped((chips, each, width), bf16)
    return pl.pallas_call(
        kernel,
        in_specs=[UNUSED] * 3,
        out_specs=[UNUSED] * 3,
        out_shape=[back, shaped((slots, ff), bf16), shaped((slots, 2 * ff), bf16)],
        scratch_shapes=[
            pltpu.VMEM((slots, width), bf16),
            pltpu.VMEM((slots, width), bf16),
            pltpu.VMEM((chips, 2, rows_up, width), bf16),
            pltpu.VMEM((chips, 2, rows_down, width), bf16),
            pltpu.VMEM((slots, ff), f32),
            pltpu.VMEM((slots, ff), f32),
            pltpu.VMEM((slots, ff), bf16),
            pltpu.VMEM((slots, 2 * ff), bf16),
            pltpu.VMEM(back.shape, bf16),
            pltpu.SemaphoreType.DMA((2,)),
            pltpu.SemaphoreType.DMA((ways,)),
            pltpu.SemaphoreType.DMA((ways,)),
            pltpu.SemaphoreType.DMA((4,)),
        ],
        compiler_params=pltpu.CompilerParams(vmem_limit_bytes=VMEM_LIMIT),
        cost_estimate=pl.CostEstimate(
            flops=2 * slots * 5 * width * ff,
            bytes_accessed=12 * slots * width + 2 * width * 3 * ff,
            transcendentals=0,
        ),
    )(picked, grad_out, parts)


def expert_weight_grads(picked, grad_out, acted, grad_pre, parts, rows_up, rows_down, earlier):
    slots, width = picked.shape
    ways, chips, _, part = parts.shape
    wide = ways // 2
    ff = acted.shape[1]
    each = slots // chips
    half = (rows_up + rows_down) // 2
    near = chips // 2
    columns = width // 2

    def kernel(picked_any, grad_any, acted_any, pre_any, part_ref, *refs):
        expert_any, piece_any = refs[len(earlier) : len(earlier) + 2]
        (
            picked_ref, grad_ref, acted_ref, pre_ref, down_w, expert_ref, keep_ref, piece_ref,
            in_sem, down_sem, out_sem,
        ) = refs[len(earlier) + 2 :]
        ins = [
            pltpu.make_async_copy(source, to, in_sem.at[i])
            for i, (source, to) in enumerate(
                (
                    (picked_any, picked_ref),
                    (pre_any, pre_ref),
                    (acted_any, acted_ref),
                    (grad_any, grad_ref),
                )
            )
        ]
        downs = expert_copies(part_ref, down_w, rows_up, rows_down, down_sem)
        for copy in ins + downs:
            copy.start()
        for copy in ins:
            copy.wait()

        @pl.loop(0, 2)
        def _(s):
            for n in range(2):
                at = slice(n * columns, (n + 1) * columns)
                for m in range(near // 2):
                    base = pl.multiple_of(s * near * 2 * rows_up + m * 4 * rows_up, 128)
                    block = picked_ref[:, pl.ds(base, 4 * rows_up)]
                    up = transposed_times(block, pre_ref[:, at])
                    for i in range(4):
                        rows = up[i * rows_up : (i + 1) * rows_up]
                        k, c = 2 * m + i // 2, i % 2
                        keep_ref[k, c] = rows[half:]
                        low = rows[:half].astype(bf16)
                        for j in range(columns // part):
                            z = n * (columns // part) + j
                            piece_ref[z, c, s * near + k, 0] = low[:, j * part : (j + 1) * part]
                base = pl.multiple_of(s * near * 2 * rows_down, 128)
                block = acted_ref[:, pl.ds(base, near * 2 * rows_down)]
                down = transposed_times(block, grad_ref[:, at])
                for k in range(near):
                    for c in range(2):
                        low = (2 * k + c) * rows_down
                        rest = jnp.concatenate([keep_ref[k, c], down[low : low + rows_down]], axis=0)
                        rest = rest.astype(bf16)
                        for j in range(columns // part):
                            z = n * (columns // part) + j
                            piece_ref[z, c, s * near + k, 1] = rest[:, j * part : (j + 1) * part]
            chip = pl.ds(s * near, near)
            pltpu.make_async_copy(
                piece_ref.at[:, :, chip], piece_any.at[:, :, chip], out_sem.at[s]
            ).start()

        for copy in downs:
            copy.wait()
        for j in range(2):
            to = slice(j * columns, (j + 1) * columns)
            weights = down_w[:, :, :, to].reshape(ff, columns)
            forward = matmul(acted_ref[...], weights).astype(bf16)
            expert_ref[:, :, to] = forward.reshape(chips, each, columns)
        expert_out = pltpu.make_async_copy(expert_ref, expert_any, out_sem.at[2])
        expert_out.start()
        for s in range(2):
            chip = pl.ds(s * near, near)
            pltpu.make_async_copy(
                piece_ref.at[:, :, chip], piece_any.at[:, :, chip], out_sem.at[s]
            ).wait()
        expert_out.wait()

    expert = shaped((chips, each, width), bf16)
    pieces = shaped((wide, 2, chips, 2, half, part), bf16)
    return pl.pallas_call(
        kernel,
        in_specs=[UNUSED] * (5 + len(earlier)),
        out_specs=[UNUSED] * 2,
        out_shape=[expert, pieces],
        scratch_shapes=[
            pltpu.VMEM((slots, width), bf16),
            pltpu.VMEM((slots, width), bf16),
            pltpu.VMEM((slots, ff), bf16),
            pltpu.VMEM((slots, 2 * ff), bf16),
            pltpu.VMEM((chips, 2, rows_down, width), bf16),
            pltpu.VMEM(expert.shape, bf16),
            pltpu.VMEM((near, 2, rows_up - half, columns), f32),
            pltpu.VMEM(pieces.shape, bf16),
            pltpu.SemaphoreType.DMA((4,)),
            pltpu.SemaphoreType.DMA((ways,)),
            pltpu.SemaphoreType.DMA((3,)),
        ],
        compiler_params=pltpu.CompilerParams(vmem_limit_bytes=VMEM_LIMIT),
        cost_estimate=pl.CostEstimate(
            flops=2 * slots * 4 * width * ff,
            bytes_accessed=10 * slots * width + 8 * width * 3 * ff,
            transcendentals=0,
        ),
    )(picked, grad_out, acted, grad_pre, parts, *earlier)


def residual_grad(pick, returned, residual, gain, cotangent, earlier):
    rows, width = residual.shape
    slots = pick.shape[0]

    def kernel(pick_ref, back_ref, residual_ref, gain_ref, cot_ref, grad_ref, branch_ref, gain_grad_ref):
        for block in range(width // 512):
            at = slice(block * 512, (block + 1) * 512)
            back = back_ref[:, :, at].reshape(slots, 512)
            grad_ref[:, at] = transposed_times(pick_ref[...], back)
        grad, grad_gain = norm_back(residual_ref[...], gain_ref[...], grad_ref[...])
        grad = grad + cot_ref[...].astype(f32)
        grad_ref[...] = grad
        branch_ref[...] = grad.astype(bf16)
        gain_grad_ref[...] = gain_tile(grad_gain, False)

    return call(
        kernel,
        [shaped((rows, width), f32), shaped((rows, width), bf16), shaped((width, 128), f32)],
        (pick, returned, residual, gain, cotangent),
        earlier,
        flops=2 * slots * width * rows,
    )


def add_expert_rows(pick, weight, returned, residual, earlier):
    rows, width = residual.shape
    slots = pick.shape[0]

    def kernel(pick_ref, weight_ref, back_ref, residual_ref, out_ref):
        back = jnp.where(pick_ref[...] > 0, weight_ref[...], 0.0)
        high = back.astype(bf16)
        low = (back - high.astype(f32)).astype(bf16)
        for block in range(width // 512):
            at = slice(block * 512, (block + 1) * 512)
            expert = back_ref[:, :, at].reshape(slots, 512)
            mixture = transposed_times(high, expert) + transposed_times(low, expert)
            out_ref[:, at] = (residual_ref[:, at] + mixture).astype(bf16)

    return call(
        kernel,
        [shaped((rows, width), bf16)],
        (pick, weight, returned, residual),
        earlier,
        flops=4 * slots * width * rows,
    )[0]


def attend_back(grad_branch, mine, other, queries, before, own, first, cosine, sine, earlier):
    rows, width = grad_branch.shape
    kv_width = KEY_VALUE_HEADS * HEAD_SIZE
    wide = len(mine)
    chips = mine[0].shape[0]

    def kernel(
        grad_ref, query_ref, before_ref, own_ref, first_ref, cos_ref, sin_ref, place_ref, *refs
    ):
        out_ref, prev_ref, self_ref, attended_ref, prob_ref, w_ref, sem = refs[2 * wide :]
        copies = fetch_parts(place_ref, refs[:wide], refs[wide : 2 * wide], w_ref, sem)
        allowed = allowed_keys(first_ref, rows)
        for head in range(QUERY_HEADS):
            at = slice(head * HEAD_SIZE, (head + 1) * HEAD_SIZE)
            keys, _ = keys_and_values(before_ref, own_ref, head // GROUP)
            prob_ref[head] = probabilities(query_ref[:, at], keys, allowed)
        for copy in copies:
            copy.wait()
        for half in range(2):
            at = slice(half * (width // 2), (half + 1) * (width // 2))
            weights = w_ref[half * (chips // 2) : (half + 1) * (chips // 2)]
            weights = weights.reshape(width // 2, width)
            attended_ref[:, at] = times_transposed(grad_ref[...], weights).astype(bf16)
        cos, sin = cos_ref[...], sin_ref[...]
        for group in range(KEY_VALUE_HEADS):
            keys, values = keys_and_values(before_ref, own_ref, group)
            raws, lows, uppers, asked = [], [], [], []
            for head in range(group * GROUP, (group + 1) * GROUP):
                at = slice(head * HEAD_SIZE, (head + 1) * HEAD_SIZE)
                query, upper = query_ref[:, at], attended_ref[:, at]
                probs = prob_ref[head]
                grad_probs = times_transposed(upper, values)
                inner = jnp.sum(probs * grad_probs, axis=-1, keepdims=True)
                raw = (probs * (grad_probs - inner) * SCALE).astype(bf16)
                out_ref[head] = rotate(matmul(raw, keys), cos, -sin).astype(bf16)
                raws.append(raw)
                lows.append(probs.astype(bf16))
                uppers.append(upper)
                asked.append(query)
            for base, lefts, rights in (
                (group * HEAD_SIZE, raws, asked),
                (kv_width + group * HEAD_SIZE, lows, uppers),
            ):
                grad = transposed_times(
                    jnp.concatenate(lefts, axis=0), jnp.concatenate(rights, axis=0)
                )
                prev_ref[:, base : base + HEAD_SIZE] = grad[:rows].astype(bf16)
                self_ref[:, base : base + HEAD_SIZE] = grad[rows:]

    return call(
        kernel,
        [
            shaped((QUERY_HEADS, rows, HEAD_SIZE), bf16),
            shaped((rows, 2 * kv_width), bf16),
            shaped((rows, 2 * kv_width), f32),
        ],
        (grad_branch, queries, before, own, first, cosine, sine, device_place(), *mine, *other),
        earlier,
        specs=[*([WHOLE] * 7), SCALAR, *([UNUSED] * (2 * wide))],
        flops=2 * rows * width * width + 20 * rows * rows * width,
        scratch=[
            pltpu.VMEM((rows, width), bf16),
            pltpu.VMEM((QUERY_HEADS, rows, 2 * rows), f32),
            pltpu.VMEM((chips, 2, width // (2 * chips), width), bf16),
            pltpu.SemaphoreType.DMA((2 * wide,)),
        ],
    )


def qkv_blocks_of(grad_queries, grad_own, from_next, cosine, sine, earlier):
    heads, rows, size = grad_queries.shape
    total = heads + 2 * KEY_VALUE_HEADS

    def kernel(query_ref, own_ref, next_ref, cos_ref, sin_ref, out_ref):
        out_ref[:heads] = query_ref[...]
        for i in range(2 * KEY_VALUE_HEADS):
            at = slice(i * size, (i + 1) * size)
            grad = own_ref[:, at] + next_ref[:, at].astype(f32)
            if i < KEY_VALUE_HEADS:
                grad = rotate(grad, cos_ref[...], -sin_ref[...])
            out_ref[heads + i] = grad.astype(bf16)

    return call(
        kernel,
        [shaped((total, rows, size), bf16)],
        (grad_queries, grad_own, from_next, cosine, sine),
        earlier,
    )[0]


def input_grad(blocks, weights, tokens, gain, grad_residual, gain_grad, earlier):
    rows, width = tokens.shape
    columns = blocks.shape[0] * HEAD_SIZE

    def kernel(
        block_ref, all_ref, token_ref, gain_ref, residual_ref, other_ref, out_ref, tile_ref, w_ref, sem
    ):
        copies = fetch(all_ref, w_ref, sem, 1)
        total = jnp.zeros((rows, width), f32)
        for i in range(blocks.shape[0] // 2):
            if i % 2 == 0:
                copies[i // 2].wait()
            pair = jnp.concatenate([block_ref[2 * i], block_ref[2 * i + 1]], axis=1)
            total = total + times_transposed(pair, w_ref[:, i * 256 : (i + 1) * 256])
        grad, grad_gain = norm_back(token_ref[...].astype(f32), gain_ref[...], total)
        out_ref[...] = (residual_ref[...] + grad).astype(bf16)
        tile_ref[...] = (other_ref[...] + gain_tile(grad_gain, True)).astype(bf16)

    return call(
        kernel,
        [shaped((rows, width), bf16), shaped((width, 128), bf16)],
        (blocks, weights, tokens, gain, grad_residual, gain_grad),
        earlier,
        specs=[WHOLE, UNUSED, WHOLE, WHOLE, WHOLE, WHOLE],
        flops=2 * rows * width * columns,
        scratch=[pltpu.VMEM((width, columns), bf16), pltpu.SemaphoreType.DMA((columns // 512,))],
    )


def gather_over_z(part):
    wide = lax.axis_size("z")
    return [part] + [
        lax.ppermute(part, "z", [(i, i ^ k) for i in range(wide)]) for k in range(1, wide)
    ]


def expert_outputs(pieces, rows_up, rows_down):
    wide, experts, _, half, part = pieces.shape
    width = wide * part
    split = rows_up - half

    def kernel(piece_ref, up_ref, down_ref):
        for z in range(wide):
            at = slice(z * part, (z + 1) * part)
            rest = piece_ref[z, 0, 1].astype(f32)
            up_ref[0, :half, at] = piece_ref[z, 0, 0].astype(f32)
            up_ref[0, half:, at] = rest[:split]
            down_ref[0, :, at] = rest[split:]

    return pl.pallas_call(
        kernel,
        grid=(experts,),
        in_specs=[pl.BlockSpec((wide, 1, 2, half, part), lambda e: (0, e, 0, 0, 0))],
        out_specs=[
            pl.BlockSpec((1, rows_up, width), lambda e: (e, 0, 0)),
            pl.BlockSpec((1, rows_down, width), lambda e: (e, 0, 0)),
        ],
        out_shape=[
            shaped((experts, rows_up, width), f32),
            shaped((experts, rows_down, width), f32),
        ],
    )(pieces)


def part_to_square(value, across, axis):
    size = value.shape[axis] // 2
    mine = lax.dynamic_slice_in_dim(value, across * size, size, axis)
    sent = lax.dynamic_slice_in_dim(value, (1 - across) * size, size, axis)
    return jnp.stack([mine, lax.ppermute(sent, "x", SWAP)])


def part_to_core(value, core, axis):
    size = value.shape[axis] // 2
    return lax.ppermute(lax.dynamic_slice_in_dim(value, (1 - core) * size, size, axis), "c", SWAP)


def twice(value, earlier):
    size = value.shape[0]

    def kernel(in_ref, out_ref):
        out_ref[:size] = in_ref[...]
        out_ref[size:] = in_ref[...]

    return call(kernel, [shaped((2 * size, *value.shape[1:]), value.dtype)], (value,), earlier)[0]


def sum_of_halves(value, earlier):
    size = value.shape[0] // 2

    def kernel(in_ref, out_ref):
        out_ref[...] = (in_ref[:size].astype(f32) + in_ref[size:].astype(f32)).astype(bf16)

    return call(kernel, [shaped((size, *value.shape[1:]), value.dtype)], (value,), earlier)[0]


def hold(values, earlier):
    def kernel(*refs):
        del refs

    return pl.pallas_call(
        kernel,
        in_specs=[UNUSED] * (len(values) + len(earlier)),
        out_specs=[UNUSED] * len(values),
        out_shape=[shaped(one.shape, one.dtype) for one in values],
        input_output_aliases={i: i for i in range(len(values))},
    )(*values, *earlier)


def out_weight_grads(near, far, grad_near, grad_far, ways, earlier):
    _, width, rows = near.shape
    columns = grad_far.shape[2]
    core = lax.axis_index("c").astype(jnp.int32).reshape(1)

    def kernel(core_ref, near_ref, far_ref, grad_near_ref, grad_far_ref, out_ref, left_ref):
        at = pl.ds(pl.multiple_of(core_ref[0] * columns, 128), columns)
        for i in range(2):
            left_ref[:, i * rows : (i + 1) * rows] = near_ref[i]
            left_ref[:, (2 + i) * rows : (3 + i) * rows] = far_ref[i]
        right = jnp.concatenate(
            [grad_near_ref[0, :, at], grad_near_ref[1, :, at], grad_far_ref[0], grad_far_ref[1]],
            axis=0,
        )
        each = width // ways
        for i in range(ways):
            left = left_ref[i * each : (i + 1) * each, :]
            out_ref[i] = matmul(left, right).astype(bf16)

    return call(
        kernel,
        [shaped((ways, width // ways, columns), bf16)],
        (core, near, far, grad_near, grad_far),
        earlier,
        specs=[SCALAR, *([WHOLE] * 4)],
        flops=8 * width * rows * columns,
        scratch=[pltpu.VMEM((width, 4 * rows), bf16)],
    )[0]


def qkv_weight_grads(near, far, grad_near, grad_far, ways, earlier):
    _, rows, width = near.shape
    heads = grad_far.shape[1]
    columns = heads * HEAD_SIZE
    core = lax.axis_index("c").astype(jnp.int32).reshape(1)

    def kernel(core_ref, near_ref, far_ref, grad_near_ref, grad_far_ref, out_ref, left_ref, right_ref):
        for i in range(2):
            left_ref[i * rows : (i + 1) * rows, :] = near_ref[i]
            left_ref[(2 + i) * rows : (3 + i) * rows, :] = far_ref[i]
            for head in range(heads):
                at = slice(head * HEAD_SIZE, (head + 1) * HEAD_SIZE)
                mine = grad_near_ref[i, core_ref[0] * heads + head]
                right_ref[i * rows : (i + 1) * rows, at] = mine
                right_ref[(2 + i) * rows : (3 + i) * rows, at] = grad_far_ref[i, head]
        each = width // ways
        for i in range(ways):
            block = slice(i * each, (i + 1) * each)
            out_ref[i] = transposed_times(left_ref[:, block], right_ref[...]).astype(bf16)

    return call(
        kernel,
        [shaped((ways, width // ways, columns), bf16)],
        (core, near, far, grad_near, grad_far),
        earlier,
        specs=[SCALAR, *([WHOLE] * 4)],
        flops=8 * width * rows * columns,
        scratch=[pltpu.VMEM((4 * rows, width), bf16), pltpu.VMEM((4 * rows, columns), bf16)],
    )[0]


def moved_over_y(blocks):
    wide = lax.axis_size("y")
    y = lax.axis_index("y")
    moved = [lax.dynamic_index_in_dim(blocks, y, 0, keepdims=False)]
    for k in range(1, wide):
        sent = lax.dynamic_index_in_dim(blocks, y ^ k, 0, keepdims=False)
        moved.append(lax.ppermute(sent, "y", [(i, i ^ k) for i in range(wide)]))
    return moved


def tiles_of(qkv, out, gains, tiles, squares):
    terms = qkv.shape[0]
    rows = qkv.shape[1] // squares
    count = qkv.shape[2] // HEAD_SIZE

    def kernel(qkv_ref, out_ref, *refs):
        gain_refs, tile_ref = refs[:-1], refs[-1]
        for t in range(tiles):
            for p in range(squares):
                block = slice(p * rows, (p + 1) * rows)
                if t < count:
                    at = slice(t * HEAD_SIZE, (t + 1) * HEAD_SIZE)
                    values = [qkv_ref[i, block, at] for i in range(terms)]
                elif t < tiles - 1:
                    at = slice((t - count) * HEAD_SIZE, (t - count + 1) * HEAD_SIZE)
                    values = [out_ref[block, at]]
                else:
                    values = [ref[block] for ref in gain_refs]
                total = values[0].astype(f32)
                for value in values[1:]:
                    total = total + value.astype(f32)
                tile_ref[t * squares + p] = total.astype(bf16)

    return call(
        kernel, [shaped((tiles * squares, rows, HEAD_SIZE), bf16)], (qkv, out, *gains)
    )[0]


def sum_and_copy(parts, squares, copies, earlier):
    count, rows, columns = parts.shape

    def kernel(part_ref, copy_ref):
        for p in range(squares):
            total = part_ref[p].astype(f32)
            for i in range(1, count // squares):
                total = total + part_ref[i * squares + p].astype(f32)
            low = total.astype(bf16)
            for i in range(copies):
                copy_ref[i, p] = low

    return call(kernel, [shaped((copies, squares, rows, columns), bf16)], (parts,), earlier)[0]


def attention_outputs(tiles, query_width, kv_width, earlier):
    count, squares, rows, column = tiles.shape
    heads = (query_width + kv_width) // column // squares
    outs = count - 1 - heads

    def kernel(tile_ref, query_ref, keyval_ref, out_ref, gain_ref):
        gains = jnp.zeros((rows, column), f32)
        for q in range(squares):
            for t in range(heads):
                at = (q * heads + t) * column
                value = tile_ref[t, q].astype(f32)
                if at < query_width:
                    query_ref[:, at : at + column] = value
                else:
                    keyval_ref[:, at - query_width : at - query_width + column] = value
            for t in range(outs):
                at = (q * outs + t) * column
                out_ref[:, at : at + column] = tile_ref[heads + t, q].astype(f32)
            gains = gains + tile_ref[count - 1, q].astype(f32)
        gain_ref[...] = gains

    return call(
        kernel,
        [
            shaped((rows, query_width), f32),
            shaped((rows, kv_width), f32),
            shaped((rows, squares * outs * column), f32),
            shaped((rows, column), f32),
        ],
        (tiles,),
        earlier,
    )


def per_device(
    tokens,
    cotangent,
    seq_lengths,
    seq_order,
    routes,
    gate_weights,
    attn_gain,
    w_query,
    key_value_weight,
    w_out,
    ffn_gain,
    w_gateup,
    w_down,
):
    wide_z = lax.axis_size("z")
    shards = lax.axis_size("y") * lax.axis_size("x") * lax.axis_size("c")
    core = lax.axis_index("c")
    shard = (lax.axis_index("y") * lax.axis_size("x") + lax.axis_index("x")) * 2 + core
    rows, width = tokens.shape
    experts = w_gateup.shape[0]
    kv_width = KEY_VALUE_HEADS * HEAD_SIZE
    owned = width // shards

    qkv_full = lax.all_gather(
        jnp.concatenate([w_query, key_value_weight], 1), SHARD, axis=0, tiled=True
    )
    part = width // wide_z
    rows_out, rows_up, rows_down = w_out.shape[0], w_gateup.shape[1], w_down.shape[1]
    column = lax.axis_index("z") * part
    gains_own = jnp.pad(jnp.stack([attn_gain, ffn_gain]), ((0, 14), (0, part - owned)))
    out_part = jnp.concatenate(
        [lax.dynamic_slice_in_dim(w_out, column, part, 1), gains_own], axis=0
    )
    expert_part = jnp.concatenate(
        [
            lax.dynamic_slice_in_dim(w_gateup, column, part, 2),
            lax.dynamic_slice_in_dim(w_down, column, part, 2),
        ],
        axis=1,
    )
    out_part = spread(out_part, experts, CHIPS)
    expert_part = exchange(hold((expert_part,), (out_part,))[0], CHIPS)
    gains_mine = out_part[:, rows_out : rows_out + 2, :owned]
    gains = in_core_order(core, gains_mine, lax.ppermute(gains_mine, "c", SWAP))
    gains = gains.transpose(2, 0, 1, 3).reshape(2, width).astype(f32)
    gain_attn, gain_ffn = gains[:1], gains[1:]
    out_mine = gather_over_z(out_part)
    out_other = [lax.ppermute(one, "c", SWAP) for one in out_mine]
    chosen = routes[:, :, None] == jnp.arange(experts, dtype=jnp.int32)
    member = jnp.any(chosen, axis=1)
    weight = jnp.sum(jnp.where(chosen, gate_weights[:, :, None], 0.0), axis=1)
    place = jnp.cumsum(member.astype(jnp.int32), axis=0) - 1
    slot = jnp.where(member, place, -1).T
    picks = slot[:, None, :] == jnp.arange(CAP, dtype=jnp.int32)[None, :, None]
    pick = picks.astype(bf16).reshape(experts * CAP, rows)
    slot_weight = jnp.sum(jnp.where(picks, weight.T[:, None, :], 0.0), axis=2)
    grad_out = matmul(pick, cotangent) * slot_weight.reshape(-1, 1)
    grad_out_sent = hold((grad_out.astype(bf16),), (expert_part,))[0]
    grad_out = exchange(grad_out_sent, CHIPS)


    lengths = seq_lengths[0]
    starts = jnp.cumsum(lengths) - lengths
    row_at = shard * rows + jnp.arange(rows, dtype=jnp.int32)
    first_at = jnp.max(jnp.where(starts[None, :] <= row_at[:, None], starts[None, :], 0), axis=1)
    cosine, sine = rotary_tables(row_at - first_at)
    first = (first_at - shard * rows).astype(jnp.int32)[:, None]
    normed, queries, keyval = project_qkv(
        tokens, gain_attn, qkv_full, cosine, sine, (*out_mine[1:], expert_part, grad_out_sent)
    )
    expert_parts = lax.all_gather(hold((expert_part,), (queries,))[0], ("z", "c"), axis=0)
    ring = [(i, (i + 1) % shards) for i in range(shards)]
    back_ring = [((i + 1) % shards, i) for i in range(shards)]
    before = lax.ppermute(keyval, SHARD, ring)
    attended_turned, residual, picked = attend(
        queries, before, keyval, first, out_mine, out_other, tokens, gain_ffn, pick, ()
    )

    picked = exchange(hold((picked,), (grad_out,))[0], CHIPS)
    normed, attended_turned = hold((normed, attended_turned), (picked,))
    normed_moved = lax.ppermute(normed, "x", SWAP)
    attended_moved = lax.ppermute(attended_turned, "x", SWAP)
    returned, acted, grad_pre = run_experts(picked, grad_out, expert_parts, rows_up, rows_down)
    returned = hold((returned,), (normed_moved, attended_moved))[0]
    expert_rows, pieces = expert_weight_grads(
        picked, grad_out, acted, grad_pre, expert_parts, rows_up, rows_down, (returned,)
    )
    normed_near = jnp.stack([normed, normed_moved])
    attended_near = jnp.stack([attended_turned, attended_moved])
    returned, expert_rows, pieces = hold((exchange(returned, CHIPS), expert_rows, pieces), ())
    normed_far = lax.ppermute(normed_near, "c", SWAP)
    attended_far = lax.ppermute(attended_near, "c", SWAP)
    pieces = pieces.reshape(2 * wide_z, *pieces.shape[2:])
    over_z = lax.psum_scatter(pieces, ("z", "c"), scatter_dimension=0, tiled=False)

    grad_residual, grad_branch, gain_grad = residual_grad(
        pick, returned, residual, gain_ffn, cotangent, (normed_far, attended_far)
    )
    expert_rows = exchange(expert_rows, CHIPS)
    across = lax.axis_index("x")
    branch_near = part_to_square(grad_branch, across, 1)
    grad_queries, grad_before, grad_own = attend_back(
        grad_branch,
        out_mine,
        out_other,
        queries,
        before,
        keyval,
        first,
        cosine,
        sine,
        (),
    )
    from_next = lax.ppermute(grad_before, SHARD, back_ring)
    grad_blocks = qkv_blocks_of(
        grad_queries, grad_own, from_next, cosine, sine, ()
    )

    blocks_near = part_to_square(grad_blocks, across, 0)
    doubled = twice(over_z, (expert_rows, blocks_near))
    qkv_grads = qkv_weight_grads(
        normed_near,
        normed_far,
        blocks_near,
        part_to_core(blocks_near, core, 1),
        lax.axis_size("y"),
        (doubled,),
    )
    over_rep = exchange(doubled, ("h", *CHIPS))
    out_terms = out_weight_grads(
        attended_near,
        attended_far,
        branch_near,
        part_to_core(branch_near, core, 2),
        lax.axis_size("y"),
        (doubled,),
    )
    out_grads = lax.psum_scatter(out_terms, "y", scatter_dimension=0, tiled=True)
    grad_tokens, tile = input_grad(
        grad_blocks, qkv_full, tokens, gain_attn, grad_residual, gain_grad, (qkv_grads,)
    )
    over_rep = sum_of_halves(over_rep, (tile,))
    gain_terms = moved_over_y(tile.reshape(lax.axis_size("y"), -1, HEAD_SIZE))
    qkv_grads = exchange(qkv_grads, "y")
    shard_gateup, shard_down = expert_outputs(
        lax.all_gather(over_rep, "z", axis=0), rows_up, rows_down
    )
    reps = 2 * wide_z
    tiles = exchange(tiles_of(qkv_grads, out_grads.reshape(-1, part), gain_terms, reps, 4), REP + ("x", "c"))
    tiles = exchange(sum_and_copy(tiles, 4, reps, ()), REP)
    grad_query, grad_keyval, grad_out_w, gain_sums = attention_outputs(
        tiles, width, 2 * kv_width, (shard_down,)
    )

    output = add_expert_rows(
        pick, slot_weight.reshape(-1, 1), expert_rows, residual, (qkv_grads,)
    )
    return (
        output,
        grad_tokens,
        gain_sums[:, 0],
        grad_query,
        grad_keyval,
        grad_out_w,
        gain_sums[:, 64],
        shard_gateup,
        shard_down,
    )


def solution(mesh):
    reps, shards = mesh.devices.shape
    fine = Mesh(mesh.devices.reshape(2, reps // 2, shards // 4, 2, 2), ALL)
    split = ALL
    placed = (
        P(split, None),
        P(split, None),
        P(REP, None),
        P(REP, None),
        P(split, None),
        P(split, None),
        P(SHARD),
        P(SHARD, None),
        P(SHARD, None),
        P(SHARD, None),
        P(SHARD),
        P(None, SHARD, None),
        P(None, SHARD, None),
    )
    return jax.shard_map(
        per_device,
        mesh=fine,
        in_specs=placed,
        out_specs=(
            P(split, None),
            P(split, None),
            P(SHARD),
            P(SHARD, None),
            P(SHARD, None),
            P(SHARD, None),
            P(SHARD),
            P(None, SHARD, None),
            P(None, SHARD, None),
        ),
        check_vma=False,
    )
```

```python
import jax
import jax.numpy as jnp
from jax import lax
from jax.experimental import pallas as pl
from jax.experimental.pallas import tpu as pltpu
from jax.sharding import Mesh, PartitionSpec as P

QUERY_HEADS = 12
KEY_VALUE_HEADS = 2
GROUP = QUERY_HEADS // KEY_VALUE_HEADS
HEAD_SIZE = 128
CAP = 80

EPSILON = 1e-06
ROPE_BASE = 10000.0
SCALE = HEAD_SIZE ** (-0.5)
SHARD = ("y", "x", "c")
CHIPS = ("y", "x")
REP = ("h", "z")
ALL = REP + SHARD
SWAP = [(0, 1), (1, 0)]

bf16 = jnp.bfloat16
f32 = jnp.float32

VMEM_LIMIT = 63 * 1024 * 1024
WHOLE = pl.BlockSpec(memory_space=pltpu.VMEM)
UNUSED = pl.BlockSpec(memory_space=pl.ANY)
SCALAR = pl.BlockSpec(memory_space=pltpu.SMEM)


def exchange(parts, axes):
    return lax.all_to_all(parts, axes, 0, 0, tiled=True)


def spread(part, ways, axes):
    return exchange(jnp.broadcast_to(part[None], (ways, *part.shape)), axes)


def matmul(left, right):
    return jnp.dot(left, right, preferred_element_type=f32)


def dot_general(left, right, dims):
    return lax.dot_general(left, right, (dims, ((), ())), preferred_element_type=f32)


def times_transposed(left, right):
    return dot_general(left, right, ((1,), (1,)))


def transposed_times(left, right):
    return dot_general(left, right, ((0,), (0,)))


def in_core_order(core, mine, other):
    return jnp.where(core == 0, jnp.stack([mine, other], 1), jnp.stack([other, mine], 1))


def call(kernel, out_shape, operands, earlier=(), specs=None, flops=0, scratch=()):
    specs = specs or [WHOLE] * len(operands)
    count = len(operands)

    def body(*refs):
        kernel(*refs[:count], *refs[count + len(earlier) :])

    size = sum(one.size * one.dtype.itemsize for one in (*operands, *out_shape))
    return pl.pallas_call(
        body,
        in_specs=[*specs, *([UNUSED] * len(earlier))],
        out_specs=[WHOLE] * len(out_shape),
        out_shape=out_shape,
        scratch_shapes=scratch,
        compiler_params=pltpu.CompilerParams(vmem_limit_bytes=VMEM_LIMIT),
        cost_estimate=pl.CostEstimate(flops=flops, bytes_accessed=size, transcendentals=0),
    )(*operands, *earlier)


def fetch(source_ref, to_ref, semaphores, along, base=0):
    rows, columns = to_ref.shape
    copies = []
    for i in range(to_ref.shape[along] // 512):
        chunk = pl.ds(i * 512, 512)
        if along:
            source = source_ref.at[:, pl.ds(base + i * 512, 512)]
            copy = pltpu.make_async_copy(source, to_ref.at[:, chunk], semaphores.at[i])
        else:
            source = source_ref.at[chunk, pl.ds(base, columns)]
            copy = pltpu.make_async_copy(source, to_ref.at[chunk, :], semaphores.at[i])
        copy.start()
        copies.append(copy)
    return copies


def fetch_parts(place_ref, mine_refs, other_refs, to_ref, semaphores):
    rows = to_ref.shape[2]
    part = to_ref.shape[3] // len(mine_refs)
    copies = []
    for k in range(len(mine_refs)):
        to = pl.ds(pl.multiple_of((place_ref[1] ^ k) * part, 128), part)
        owners = ((place_ref[0], mine_refs[k]), (1 - place_ref[0], other_refs[k]))
        for i, (owner, part_ref) in enumerate(owners):
            copy = pltpu.make_async_copy(
                part_ref.at[:, pl.ds(0, rows), :],
                to_ref.at[:, owner, :, to],
                semaphores.at[2 * k + i],
            )
            copy.start()
            copies.append(copy)
    return copies


def device_place():
    return jnp.stack([lax.axis_index("c"), lax.axis_index("z")]).astype(jnp.int32)


def shaped(shape, dtype):
    return jax.ShapeDtypeStruct(shape, dtype)


def inverse_rms(values):
    return lax.rsqrt(jnp.mean(values * values, axis=-1, keepdims=True) + EPSILON)


def norm_back(values, gain_row, upstream):
    factor = inverse_rms(values)
    grad_normed = upstream * gain_row
    grad_gain = upstream * values * factor
    cubed = factor * factor * factor
    grad_input = factor * grad_normed - values * cubed * jnp.mean(
        grad_normed * values, axis=-1, keepdims=True
    )
    return grad_input, grad_gain


def gain_tile(grad_gain, lower):
    rows = grad_gain.shape[0]
    lane = lax.broadcasted_iota(jnp.int32, (rows, 128), 1)
    return transposed_times(grad_gain, ((lane < 64) == lower).astype(f32))


def rotary_tables(position):
    half = HEAD_SIZE // 2
    frequency = ROPE_BASE ** (-jnp.arange(half, dtype=f32) / half)
    angle = position.astype(f32)[:, None] * frequency[None, :]
    cosine, sine = jnp.cos(angle), jnp.sin(angle)
    return jnp.concatenate([cosine, cosine], 1), jnp.concatenate([-sine, sine], 1)


def rotate(values, cosine, sine):
    return values * cosine + pltpu.roll(values, HEAD_SIZE // 2, 1) * sine


def project_qkv(tokens, gain, weights, cosine, sine, earlier):
    rows, width = tokens.shape
    kv_width = KEY_VALUE_HEADS * HEAD_SIZE
    turned = QUERY_HEADS + KEY_VALUE_HEADS
    total = width + 2 * kv_width

    def kernel(
        token_ref, gain_ref, all_ref, cos_ref, sin_ref, normed_ref, query_ref, keyval_ref, w_ref, sem
    ):
        copies = fetch(all_ref, w_ref, sem, 1)
        wide = token_ref[...].astype(f32)
        normed = (wide * inverse_rms(wide) * gain_ref[...]).astype(bf16)
        normed_ref[...] = normed
        cos, sin = cos_ref[...], sin_ref[...]
        for block in range(total // 256):
            if block % 2 == 0:
                copies[block // 2].wait()
            both = matmul(normed, w_ref[:, block * 256 : (block + 1) * 256])
            for i in range(2):
                head = 2 * block + i
                value = both[:, i * HEAD_SIZE : (i + 1) * HEAD_SIZE]
                if head < turned:
                    value = rotate(value, cos, sin)
                value = value.astype(bf16)
                if head < QUERY_HEADS:
                    query_ref[:, head * HEAD_SIZE : (head + 1) * HEAD_SIZE] = value
                else:
                    at = (head - QUERY_HEADS) * HEAD_SIZE
                    keyval_ref[:, at : at + HEAD_SIZE] = value

    return call(
        kernel,
        [
            shaped((rows, width), bf16),
            shaped((rows, width), bf16),
            shaped((rows, 2 * kv_width), bf16),
        ],
        (tokens, gain, weights, cosine, sine),
        earlier,
        specs=[WHOLE, WHOLE, UNUSED, WHOLE, WHOLE],
        flops=2 * rows * width * total,
        scratch=[pltpu.VMEM((width, total), bf16), pltpu.SemaphoreType.DMA((total // 512,))],
    )


def allowed_keys(first_ref, rows):
    row = lax.broadcasted_iota(jnp.int32, (rows, 2 * rows), 0)
    key = lax.broadcasted_iota(jnp.int32, (rows, 2 * rows), 1) - rows
    return (key <= row) & (key >= first_ref[...])


def probabilities(query, keys, allowed):
    scores = jnp.where(allowed, times_transposed(query, keys) * SCALE, -1000000000.0)
    exp_scores = jnp.exp(scores - jnp.max(scores, axis=-1, keepdims=True))
    return exp_scores / jnp.sum(exp_scores, axis=-1, keepdims=True)


def keys_and_values(before_ref, own_ref, group):
    both = []
    for base in (group * HEAD_SIZE, (KEY_VALUE_HEADS + group) * HEAD_SIZE):
        at = slice(base, base + HEAD_SIZE)
        both.append(jnp.concatenate([before_ref[:, at], own_ref[:, at]], axis=0))
    return both


def attend(queries, before, own, first, mine, other, tokens, gain, pick, earlier):
    rows, width = tokens.shape
    wide = len(mine)
    chips = mine[0].shape[0]

    def kernel(
        query_ref, before_ref, own_ref, first_ref, token_ref, gain_ref, pick_ref, place_ref, *refs
    ):
        turned_ref, residual_ref, picked_ref, attended_ref, w_ref, sem = refs[2 * wide :]
        copies = fetch_parts(place_ref, refs[:wide], refs[wide : 2 * wide], w_ref, sem)
        allowed = allowed_keys(first_ref, rows)
        for group in range(KEY_VALUE_HEADS):
            keys, values = keys_and_values(before_ref, own_ref, group)
            for head in range(group * GROUP, (group + 1) * GROUP):
                at = slice(head * HEAD_SIZE, (head + 1) * HEAD_SIZE)
                probs = probabilities(query_ref[:, at], keys, allowed)
                mixed = matmul(probs.astype(bf16), values)
                attended_ref[:, at] = mixed.astype(bf16)
                turned_ref[at, :] = mixed.T.astype(bf16)
        attended = attended_ref[...]
        for copy in copies:
            copy.wait()
        for block in range(width // 256):
            at = slice(block * 256, (block + 1) * 256)
            weights = w_ref[:, :, :, at].reshape(width, 256)
            branch = matmul(attended, weights).astype(bf16)
            residual_ref[:, at] = token_ref[:, at].astype(f32) + branch.astype(f32)
        residual = residual_ref[...]
        normed = (residual * inverse_rms(residual) * gain_ref[...]).astype(bf16)
        for block in range(width // 512):
            at = slice(block * 512, (block + 1) * 512)
            picked_ref[:, at] = matmul(pick_ref[...], normed[:, at]).astype(bf16)

    return call(
        kernel,
        [
            shaped((width, rows), bf16),
            shaped((rows, width), f32),
            shaped((pick.shape[0], width), bf16),
        ],
        (queries, before, own, first, tokens, gain, pick, device_place(), *mine, *other),
        earlier,
        specs=[*([WHOLE] * 7), SCALAR, *([UNUSED] * (2 * wide))],
        flops=2 * rows * width * width + 8 * rows * rows * width,
        scratch=[
            pltpu.VMEM((rows, width), bf16),
            pltpu.VMEM((chips, 2, width // (2 * chips), width), bf16),
            pltpu.SemaphoreType.DMA((2 * wide,)),
        ],
    )


def expert_copies(part_ref, to_ref, base, rows, semaphores):
    ways, part = part_ref.shape[0], part_ref.shape[3]
    return [
        pltpu.make_async_copy(
            part_ref.at[i, :, pl.ds(base, rows), :],
            to_ref.at[:, i % 2, :, pl.ds(i // 2 * part, part)],
            semaphores.at[i],
        )
        for i in range(ways)
    ]


def run_experts(picked, grad_out, parts, rows_up, rows_down):
    slots, width = picked.shape
    ways, chips, _, part = parts.shape
    ff = chips * 2 * rows_down
    each = slots // chips
    near = chips // 2

    def kernel(
        picked_any, grad_any, part_ref, back_any, acted_any, pre_any,
        picked_ref, grad_ref, up_w, down_w, gate_ref, upper_ref, acted_ref, pre_ref, back_ref,
        in_sem, up_sem, down_sem, out_sem,
    ):
        rows_in = pltpu.make_async_copy(picked_any, picked_ref, in_sem.at[0])
        grads_in = pltpu.make_async_copy(grad_any, grad_ref, in_sem.at[1])
        ups = expert_copies(part_ref, up_w, 0, rows_up, up_sem)
        downs = expert_copies(part_ref, down_w, rows_up, rows_down, down_sem)
        for copy in [rows_in, *ups, grads_in, *downs]:
            copy.start()
        for copy in [rows_in, *ups]:
            copy.wait()

        @pl.loop(0, ff // 256)
        def _(j):
            at = pl.multiple_of(j * 256, 256)
            for base, ref in ((0, gate_ref), (ff, upper_ref)):
                weights = up_w[:, :, :, pl.ds(base + at, 256)].reshape(width, 256)
                ref[:, pl.ds(at, 256)] = matmul(picked_ref[...], weights)

        for copy in [grads_in, *downs]:
            copy.wait()

        @pl.loop(0, 2)
        def _(j):
            at = pl.ds(pl.multiple_of(j * (ff // 2), 128), ff // 2)
            weights = down_w[pl.ds(j * near, near)].reshape(ff // 2, width)
            grad_act = times_transposed(grad_ref[...], weights)
            gate, up = gate_ref[:, at], upper_ref[:, at]
            sigmoid = 1.0 / (1.0 + jnp.exp(-gate))
            silu = gate * sigmoid
            acted_ref[:, at] = (silu * up).astype(bf16)
            grad_gate = grad_act * up * sigmoid * (1.0 + gate * (1.0 - sigmoid))
            pre_ref[:, at] = grad_gate.astype(bf16)
            upper = pl.ds(pl.multiple_of(ff + j * (ff // 2), 128), ff // 2)
            pre_ref[:, upper] = (grad_act * silu).astype(bf16)

        outs = [
            pltpu.make_async_copy(acted_ref, acted_any, out_sem.at[0]),
            pltpu.make_async_copy(pre_ref, pre_any, out_sem.at[1]),
        ]
        for copy in outs:
            copy.start()
        columns = width // 2
        for j in range(2):
            to = slice(j * columns, (j + 1) * columns)
            weights = up_w[j * near : (j + 1) * near].reshape(columns, 2 * ff)
            back = times_transposed(pre_ref[...], weights).astype(bf16)
            back_ref[:, :, to] = back.reshape(chips, each, columns)
            copy = pltpu.make_async_copy(
                back_ref.at[:, :, to], back_any.at[:, :, to], out_sem.at[2 + j]
            )
            copy.start()
            outs.append(copy)
        for copy in outs:
            copy.wait()

    back = shaped((chips, each, width), bf16)
    return pl.pallas_call(
        kernel,
        in_specs=[UNUSED] * 3,
        out_specs=[UNUSED] * 3,
        out_shape=[back, shaped((slots, ff), bf16), shaped((slots, 2 * ff), bf16)],
        scratch_shapes=[
            pltpu.VMEM((slots, width), bf16),
            pltpu.VMEM((slots, width), bf16),
            pltpu.VMEM((chips, 2, rows_up, width), bf16),
            pltpu.VMEM((chips, 2, rows_down, width), bf16),
            pltpu.VMEM((slots, ff), f32),
            pltpu.VMEM((slots, ff), f32),
            pltpu.VMEM((slots, ff), bf16),
            pltpu.VMEM((slots, 2 * ff), bf16),
            pltpu.VMEM(back.shape, bf16),
            pltpu.SemaphoreType.DMA((2,)),
            pltpu.SemaphoreType.DMA((ways,)),
            pltpu.SemaphoreType.DMA((ways,)),
            pltpu.SemaphoreType.DMA((4,)),
        ],
        compiler_params=pltpu.CompilerParams(vmem_limit_bytes=VMEM_LIMIT),
        cost_estimate=pl.CostEstimate(
            flops=2 * slots * 5 * width * ff,
            bytes_accessed=12 * slots * width + 2 * width * 3 * ff,
            transcendentals=0,
        ),
    )(picked, grad_out, parts)


def expert_weight_grads(picked, grad_out, acted, grad_pre, parts, rows_up, rows_down, earlier):
    slots, width = picked.shape
    ways, chips, _, part = parts.shape
    wide = ways // 2
    ff = acted.shape[1]
    each = slots // chips
    half = (rows_up + rows_down) // 2
    near = chips // 2
    columns = width // 2

    def kernel(picked_any, grad_any, acted_any, pre_any, part_ref, *refs):
        expert_any, piece_any = refs[len(earlier) : len(earlier) + 2]
        (
            picked_ref, grad_ref, acted_ref, pre_ref, down_w, expert_ref, keep_ref, piece_ref,
            in_sem, down_sem, out_sem,
        ) = refs[len(earlier) + 2 :]
        ins = [
            pltpu.make_async_copy(source, to, in_sem.at[i])
            for i, (source, to) in enumerate(
                (
                    (picked_any, picked_ref),
                    (pre_any, pre_ref),
                    (acted_any, acted_ref),
                    (grad_any, grad_ref),
                )
            )
        ]
        downs = expert_copies(part_ref, down_w, rows_up, rows_down, down_sem)
        for copy in ins + downs:
            copy.start()
        for copy in ins:
            copy.wait()

        @pl.loop(0, 2)
        def _(s):
            for n in range(2):
                at = slice(n * columns, (n + 1) * columns)
                for m in range(near // 2):
                    base = pl.multiple_of(s * near * 2 * rows_up + m * 4 * rows_up, 128)
                    block = picked_ref[:, pl.ds(base, 4 * rows_up)]
                    up = transposed_times(block, pre_ref[:, at])
                    for i in range(4):
                        rows = up[i * rows_up : (i + 1) * rows_up]
                        k, c = 2 * m + i // 2, i % 2
                        keep_ref[k, c] = rows[half:]
                        low = rows[:half].astype(bf16)
                        for j in range(columns // part):
                            z = n * (columns // part) + j
                            piece_ref[z, c, s * near + k, 0] = low[:, j * part : (j + 1) * part]
                base = pl.multiple_of(s * near * 2 * rows_down, 128)
                block = acted_ref[:, pl.ds(base, near * 2 * rows_down)]
                down = transposed_times(block, grad_ref[:, at])
                for k in range(near):
                    for c in range(2):
                        low = (2 * k + c) * rows_down
                        rest = jnp.concatenate([keep_ref[k, c], down[low : low + rows_down]], axis=0)
                        rest = rest.astype(bf16)
                        for j in range(columns // part):
                            z = n * (columns // part) + j
                            piece_ref[z, c, s * near + k, 1] = rest[:, j * part : (j + 1) * part]
            chip = pl.ds(s * near, near)
            pltpu.make_async_copy(
                piece_ref.at[:, :, chip], piece_any.at[:, :, chip], out_sem.at[s]
            ).start()

        for copy in downs:
            copy.wait()
        for j in range(2):
            to = slice(j * columns, (j + 1) * columns)
            weights = down_w[:, :, :, to].reshape(ff, columns)
            forward = matmul(acted_ref[...], weights).astype(bf16)
            expert_ref[:, :, to] = forward.reshape(chips, each, columns)
        expert_out = pltpu.make_async_copy(expert_ref, expert_any, out_sem.at[2])
        expert_out.start()
        for s in range(2):
            chip = pl.ds(s * near, near)
            pltpu.make_async_copy(
                piece_ref.at[:, :, chip], piece_any.at[:, :, chip], out_sem.at[s]
            ).wait()
        expert_out.wait()

    expert = shaped((chips, each, width), bf16)
    pieces = shaped((wide, 2, chips, 2, half, part), bf16)
    return pl.pallas_call(
        kernel,
        in_specs=[UNUSED] * (5 + len(earlier)),
        out_specs=[UNUSED] * 2,
        out_shape=[expert, pieces],
        scratch_shapes=[
            pltpu.VMEM((slots, width), bf16),
            pltpu.VMEM((slots, width), bf16),
            pltpu.VMEM((slots, ff), bf16),
            pltpu.VMEM((slots, 2 * ff), bf16),
            pltpu.VMEM((chips, 2, rows_down, width), bf16),
            pltpu.VMEM(expert.shape, bf16),
            pltpu.VMEM((near, 2, rows_up - half, columns), f32),
            pltpu.VMEM(pieces.shape, bf16),
            pltpu.SemaphoreType.DMA((4,)),
            pltpu.SemaphoreType.DMA((ways,)),
            pltpu.SemaphoreType.DMA((3,)),
        ],
        compiler_params=pltpu.CompilerParams(vmem_limit_bytes=VMEM_LIMIT),
        cost_estimate=pl.CostEstimate(
            flops=2 * slots * 4 * width * ff,
            bytes_accessed=10 * slots * width + 8 * width * 3 * ff,
            transcendentals=0,
        ),
    )(picked, grad_out, acted, grad_pre, parts, *earlier)


def residual_grad(pick, returned, residual, gain, cotangent, earlier):
    rows, width = residual.shape
    slots = pick.shape[0]

    def kernel(
        pick_ref, back_any, residual_ref, gain_ref, cot_ref, grad_ref, branch_ref, product_ref,
        back_ref, sem,
    ):
        blocks = [slice(i * 512, (i + 1) * 512) for i in range(width // 512)]
        copies = [
            pltpu.make_async_copy(back_any.at[:, :, at], back_ref.at[:, :, at], sem.at[i])
            for i, at in enumerate(blocks)
        ]
        for copy in copies:
            copy.start()
        for copy, at in zip(copies, blocks):
            copy.wait()
            back = back_ref[:, :, at].reshape(slots, 512)
            grad_ref[:, at] = transposed_times(pick_ref[...], back)
        grad, products = norm_back(residual_ref[...], gain_ref[...], grad_ref[...])
        grad = grad + cot_ref[...].astype(f32)
        grad_ref[...] = grad
        branch_ref[...] = grad.astype(bf16)
        product_ref[...] = products.astype(bf16)

    return call(
        kernel,
        [shaped((rows, width), f32), shaped((rows, width), bf16), shaped((rows, width), bf16)],
        (pick, returned, residual, gain, cotangent),
        earlier,
        specs=[WHOLE, UNUSED, WHOLE, WHOLE, WHOLE],
        flops=2 * slots * width * rows,
        scratch=[
            pltpu.VMEM(returned.shape, bf16),
            pltpu.SemaphoreType.DMA((width // 512,)),
        ],
    )


def add_expert_rows(pick, weight, returned, residual, earlier):
    rows, width = residual.shape
    slots = pick.shape[0]

    def kernel(pick_ref, weight_ref, back_ref, residual_ref, out_ref):
        back = jnp.where(pick_ref[...] > 0, weight_ref[...], 0.0)
        high = back.astype(bf16)
        low = (back - high.astype(f32)).astype(bf16)
        for block in range(width // 512):
            at = slice(block * 512, (block + 1) * 512)
            expert = back_ref[:, :, at].reshape(slots, 512)
            mixture = transposed_times(high, expert) + transposed_times(low, expert)
            out_ref[:, at] = (residual_ref[:, at] + mixture).astype(bf16)

    return call(
        kernel,
        [shaped((rows, width), bf16)],
        (pick, weight, returned, residual),
        earlier,
        flops=4 * slots * width * rows,
    )[0]


def attend_back(grad_branch, mine, other, queries, before, own, first, cosine, sine, earlier):
    rows, width = grad_branch.shape
    kv_width = KEY_VALUE_HEADS * HEAD_SIZE
    wide = len(mine)
    chips = mine[0].shape[0]

    def kernel(
        grad_ref, query_ref, before_ref, own_ref, first_ref, cos_ref, sin_ref, place_ref, *refs
    ):
        out_ref, prev_ref, self_ref, attended_ref, prob_ref, w_ref, sem = refs[2 * wide :]
        copies = fetch_parts(place_ref, refs[:wide], refs[wide : 2 * wide], w_ref, sem)
        allowed = allowed_keys(first_ref, rows)
        for head in range(QUERY_HEADS):
            at = slice(head * HEAD_SIZE, (head + 1) * HEAD_SIZE)
            keys, _ = keys_and_values(before_ref, own_ref, head // GROUP)
            prob_ref[head] = probabilities(query_ref[:, at], keys, allowed)
        for copy in copies:
            copy.wait()
        for half in range(2):
            at = slice(half * (width // 2), (half + 1) * (width // 2))
            weights = w_ref[half * (chips // 2) : (half + 1) * (chips // 2)]
            weights = weights.reshape(width // 2, width)
            attended_ref[:, at] = times_transposed(grad_ref[...], weights).astype(bf16)
        cos, sin = cos_ref[...], sin_ref[...]
        for group in range(KEY_VALUE_HEADS):
            keys, values = keys_and_values(before_ref, own_ref, group)
            raws, lows, uppers, asked = [], [], [], []
            for head in range(group * GROUP, (group + 1) * GROUP):
                at = slice(head * HEAD_SIZE, (head + 1) * HEAD_SIZE)
                query, upper = query_ref[:, at], attended_ref[:, at]
                probs = prob_ref[head]
                grad_probs = times_transposed(upper, values)
                inner = jnp.sum(probs * grad_probs, axis=-1, keepdims=True)
                raw = (probs * (grad_probs - inner) * SCALE).astype(bf16)
                out_ref[head] = rotate(matmul(raw, keys), cos, -sin).astype(bf16)
                raws.append(raw)
                lows.append(probs.astype(bf16))
                uppers.append(upper)
                asked.append(query)
            for base, lefts, rights in (
                (group * HEAD_SIZE, raws, asked),
                (kv_width + group * HEAD_SIZE, lows, uppers),
            ):
                grad = transposed_times(
                    jnp.concatenate(lefts, axis=0), jnp.concatenate(rights, axis=0)
                )
                prev_ref[:, base : base + HEAD_SIZE] = grad[:rows].astype(bf16)
                self_ref[:, base : base + HEAD_SIZE] = grad[rows:]

    return call(
        kernel,
        [
            shaped((QUERY_HEADS, rows, HEAD_SIZE), bf16),
            shaped((rows, 2 * kv_width), bf16),
            shaped((rows, 2 * kv_width), f32),
        ],
        (grad_branch, queries, before, own, first, cosine, sine, device_place(), *mine, *other),
        earlier,
        specs=[*([WHOLE] * 7), SCALAR, *([UNUSED] * (2 * wide))],
        flops=2 * rows * width * width + 20 * rows * rows * width,
        scratch=[
            pltpu.VMEM((rows, width), bf16),
            pltpu.VMEM((QUERY_HEADS, rows, 2 * rows), f32),
            pltpu.VMEM((chips, 2, width // (2 * chips), width), bf16),
            pltpu.SemaphoreType.DMA((2 * wide,)),
        ],
    )


def qkv_blocks_of(grad_queries, grad_own, from_next, cosine, sine, earlier):
    heads, rows, size = grad_queries.shape
    total = heads + 2 * KEY_VALUE_HEADS

    def kernel(query_ref, own_ref, next_ref, cos_ref, sin_ref, out_ref):
        out_ref[:heads] = query_ref[...]
        for i in range(2 * KEY_VALUE_HEADS):
            at = slice(i * size, (i + 1) * size)
            grad = own_ref[:, at] + next_ref[:, at].astype(f32)
            if i < KEY_VALUE_HEADS:
                grad = rotate(grad, cos_ref[...], -sin_ref[...])
            out_ref[heads + i] = grad.astype(bf16)

    return call(
        kernel,
        [shaped((total, rows, size), bf16)],
        (grad_queries, grad_own, from_next, cosine, sine),
        earlier,
    )[0]


def input_grad(blocks, weights, tokens, gain, grad_residual, gain_grad, earlier):
    rows, width = tokens.shape
    columns = blocks.shape[0] * HEAD_SIZE

    def kernel(
        block_ref, all_ref, token_ref, gain_ref, residual_ref, other_ref, out_ref, tile_ref, w_ref, sem
    ):
        copies = fetch(all_ref, w_ref, sem, 1)
        total = jnp.zeros((rows, width), f32)
        for i in range(blocks.shape[0] // 2):
            if i % 2 == 0:
                copies[i // 2].wait()
            pair = jnp.concatenate([block_ref[2 * i], block_ref[2 * i + 1]], axis=1)
            total = total + times_transposed(pair, w_ref[:, i * 256 : (i + 1) * 256])
        grad, grad_gain = norm_back(token_ref[...].astype(f32), gain_ref[...], total)
        out_ref[...] = (residual_ref[...] + grad).astype(bf16)
        other = gain_tile(other_ref[...].astype(f32), False)
        tile_ref[...] = (other + gain_tile(grad_gain, True)).astype(bf16)

    return call(
        kernel,
        [shaped((rows, width), bf16), shaped((width, 128), bf16)],
        (blocks, weights, tokens, gain, grad_residual, gain_grad),
        earlier,
        specs=[WHOLE, UNUSED, WHOLE, WHOLE, WHOLE, WHOLE],
        flops=2 * rows * width * columns,
        scratch=[pltpu.VMEM((width, columns), bf16), pltpu.SemaphoreType.DMA((columns // 512,))],
    )


def gather_over_z(part):
    wide = lax.axis_size("z")
    return [part] + [
        lax.ppermute(part, "z", [(i, i ^ k) for i in range(wide)]) for k in range(1, wide)
    ]


def expert_outputs(pieces, rows_up, rows_down):
    wide, experts, _, half, part = pieces.shape
    width = wide * part
    split = rows_up - half

    def kernel(piece_ref, up_ref, down_ref):
        for z in range(wide):
            at = slice(z * part, (z + 1) * part)
            rest = piece_ref[z, 0, 1].astype(f32)
            up_ref[0, :half, at] = piece_ref[z, 0, 0].astype(f32)
            up_ref[0, half:, at] = rest[:split]
            down_ref[0, :, at] = rest[split:]

    return pl.pallas_call(
        kernel,
        grid=(experts,),
        in_specs=[pl.BlockSpec((wide, 1, 2, half, part), lambda e: (0, e, 0, 0, 0))],
        out_specs=[
            pl.BlockSpec((1, rows_up, width), lambda e: (e, 0, 0)),
            pl.BlockSpec((1, rows_down, width), lambda e: (e, 0, 0)),
        ],
        out_shape=[
            shaped((experts, rows_up, width), f32),
            shaped((experts, rows_down, width), f32),
        ],
    )(pieces)


def part_to_square(value, across, axis):
    size = value.shape[axis] // 2
    mine = lax.dynamic_slice_in_dim(value, across * size, size, axis)
    sent = lax.dynamic_slice_in_dim(value, (1 - across) * size, size, axis)
    return jnp.stack([mine, lax.ppermute(sent, "x", SWAP)])


def part_to_core(value, core, axis):
    size = value.shape[axis] // 2
    return lax.ppermute(lax.dynamic_slice_in_dim(value, (1 - core) * size, size, axis), "c", SWAP)


def twice(value, earlier):
    size = value.shape[0]
    near = size // 2

    def kernel(in_any, *refs):
        out_any, value_ref, in_sem, out_sem = refs[len(earlier) :]
        blocks = [pl.ds(i * near, near) for i in range(2)]
        ins = [
            pltpu.make_async_copy(in_any.at[at], value_ref.at[at], in_sem.at[i])
            for i, at in enumerate(blocks)
        ]
        for copy in ins:
            copy.start()
        outs = []
        for i, at in enumerate(blocks):
            ins[i].wait()
            for j in range(2):
                to = pl.ds(j * size + i * near, near)
                copy = pltpu.make_async_copy(value_ref.at[at], out_any.at[to], out_sem.at[2 * i + j])
                copy.start()
                outs.append(copy)
        for copy in outs:
            copy.wait()

    return pl.pallas_call(
        kernel,
        in_specs=[UNUSED] * (1 + len(earlier)),
        out_specs=UNUSED,
        out_shape=shaped((2 * size, *value.shape[1:]), value.dtype),
        scratch_shapes=[
            pltpu.VMEM(value.shape, value.dtype),
            pltpu.SemaphoreType.DMA((2,)),
            pltpu.SemaphoreType.DMA((4,)),
        ],
        compiler_params=pltpu.CompilerParams(vmem_limit_bytes=VMEM_LIMIT),
    )(value, *earlier)


def sum_of_halves(value, earlier):
    size = value.shape[0] // 2
    out = shaped((size, *value.shape[1:]), value.dtype)

    def kernel(in_any, *refs):
        out_any, in_ref, out_ref, in_sem, out_sem = refs[len(earlier) :]
        near = size // 2
        copies = [
            pltpu.make_async_copy(
                in_any.at[pl.ds(i * near, near)], in_ref.at[pl.ds(i * near, near)], in_sem.at[i]
            )
            for i in range(4)
        ]
        for i in (0, 2, 1, 3):
            copies[i].start()
        outs = []
        for i in range(2):
            copies[i].wait()
            copies[2 + i].wait()
            at = slice(i * near, (i + 1) * near)
            low = in_ref[at].astype(f32)
            out_ref[at] = (low + in_ref[size + i * near : size + (i + 1) * near].astype(f32)).astype(bf16)
            block = pl.ds(i * near, near)
            copy = pltpu.make_async_copy(out_ref.at[block], out_any.at[block], out_sem.at[i])
            copy.start()
            outs.append(copy)
        for copy in outs:
            copy.wait()

    return pl.pallas_call(
        kernel,
        in_specs=[UNUSED] * (1 + len(earlier)),
        out_specs=UNUSED,
        out_shape=out,
        scratch_shapes=[
            pltpu.VMEM(value.shape, value.dtype),
            pltpu.VMEM(out.shape, value.dtype),
            pltpu.SemaphoreType.DMA((4,)),
            pltpu.SemaphoreType.DMA((2,)),
        ],
        compiler_params=pltpu.CompilerParams(vmem_limit_bytes=VMEM_LIMIT),
    )(value, *earlier)


def hold(values, earlier):
    def kernel(*refs):
        del refs

    return pl.pallas_call(
        kernel,
        in_specs=[UNUSED] * (len(values) + len(earlier)),
        out_specs=[UNUSED] * len(values),
        out_shape=[shaped(one.shape, one.dtype) for one in values],
        input_output_aliases={i: i for i in range(len(values))},
    )(*values, *earlier)


def out_weight_grads(near, far, grad_near, grad_far, ways, earlier):
    _, width, rows = near.shape
    columns = grad_far.shape[2]
    core = lax.axis_index("c").astype(jnp.int32).reshape(1)

    def kernel(core_ref, near_ref, far_ref, grad_near_ref, grad_far_ref, out_ref, left_ref):
        at = pl.ds(pl.multiple_of(core_ref[0] * columns, 128), columns)
        for i in range(2):
            left_ref[:, i * rows : (i + 1) * rows] = near_ref[i]
            left_ref[:, (2 + i) * rows : (3 + i) * rows] = far_ref[i]
        right = jnp.concatenate(
            [grad_near_ref[0, :, at], grad_near_ref[1, :, at], grad_far_ref[0], grad_far_ref[1]],
            axis=0,
        )
        each = width // ways
        for i in range(ways):
            left = left_ref[i * each : (i + 1) * each, :]
            out_ref[i] = matmul(left, right).astype(bf16)

    return call(
        kernel,
        [shaped((ways, width // ways, columns), bf16)],
        (core, near, far, grad_near, grad_far),
        earlier,
        specs=[SCALAR, *([WHOLE] * 4)],
        flops=8 * width * rows * columns,
        scratch=[pltpu.VMEM((width, 4 * rows), bf16)],
    )[0]


def qkv_weight_grads(near, far, grad_near, grad_far, ways, earlier):
    _, rows, width = near.shape
    heads = grad_far.shape[1]
    columns = heads * HEAD_SIZE
    core = lax.axis_index("c").astype(jnp.int32).reshape(1)

    def kernel(core_ref, near_ref, far_ref, grad_near_ref, grad_far_ref, out_ref, left_ref, right_ref):
        for i in range(2):
            left_ref[i * rows : (i + 1) * rows, :] = near_ref[i]
            left_ref[(2 + i) * rows : (3 + i) * rows, :] = far_ref[i]
            for head in range(heads):
                at = slice(head * HEAD_SIZE, (head + 1) * HEAD_SIZE)
                mine = grad_near_ref[i, core_ref[0] * heads + head]
                right_ref[i * rows : (i + 1) * rows, at] = mine
                right_ref[(2 + i) * rows : (3 + i) * rows, at] = grad_far_ref[i, head]
        each = width // ways
        for i in range(ways):
            block = slice(i * each, (i + 1) * each)
            out_ref[i] = transposed_times(left_ref[:, block], right_ref[...]).astype(bf16)

    return call(
        kernel,
        [shaped((ways, width // ways, columns), bf16)],
        (core, near, far, grad_near, grad_far),
        earlier,
        specs=[SCALAR, *([WHOLE] * 4)],
        flops=8 * width * rows * columns,
        scratch=[pltpu.VMEM((4 * rows, width), bf16), pltpu.VMEM((4 * rows, columns), bf16)],
    )[0]


def moved_over_y(blocks):
    wide = lax.axis_size("y")
    y = lax.axis_index("y")
    moved = [lax.dynamic_index_in_dim(blocks, y, 0, keepdims=False)]
    for k in range(1, wide):
        sent = lax.dynamic_index_in_dim(blocks, y ^ k, 0, keepdims=False)
        moved.append(lax.ppermute(sent, "y", [(i, i ^ k) for i in range(wide)]))
    return moved


def tiles_of(qkv, out, gains, tiles, squares):
    terms = qkv.shape[0]
    rows = qkv.shape[1] // squares
    count = qkv.shape[2] // HEAD_SIZE

    def kernel(qkv_ref, out_ref, *refs):
        gain_refs, tile_ref = refs[:-1], refs[-1]
        for t in range(tiles):
            for p in range(squares):
                block = slice(p * rows, (p + 1) * rows)
                if t < count:
                    at = slice(t * HEAD_SIZE, (t + 1) * HEAD_SIZE)
                    values = [qkv_ref[i, block, at] for i in range(terms)]
                elif t < tiles - 1:
                    at = slice((t - count) * HEAD_SIZE, (t - count + 1) * HEAD_SIZE)
                    values = [out_ref[block, at]]
                else:
                    values = [ref[block] for ref in gain_refs]
                total = values[0].astype(f32)
                for value in values[1:]:
                    total = total + value.astype(f32)
                tile_ref[t * squares + p] = total.astype(bf16)

    return call(
        kernel, [shaped((tiles * squares, rows, HEAD_SIZE), bf16)], (qkv, out, *gains)
    )[0]


def sum_and_copy(parts, squares, copies, earlier):
    count, rows, columns = parts.shape

    def kernel(part_ref, copy_ref):
        for p in range(squares):
            total = part_ref[p].astype(f32)
            for i in range(1, count // squares):
                total = total + part_ref[i * squares + p].astype(f32)
            low = total.astype(bf16)
            for i in range(copies):
                copy_ref[i, p] = low

    return call(kernel, [shaped((copies, squares, rows, columns), bf16)], (parts,), earlier)[0]


def attention_outputs(tiles, query_width, kv_width, earlier):
    count, squares, rows, column = tiles.shape
    heads = (query_width + kv_width) // column // squares
    outs = count - 1 - heads

    def kernel(tile_ref, query_ref, keyval_ref, out_ref, gain_ref):
        gains = jnp.zeros((rows, column), f32)
        for q in range(squares):
            for t in range(heads):
                at = (q * heads + t) * column
                value = tile_ref[t, q].astype(f32)
                if at < query_width:
                    query_ref[:, at : at + column] = value
                else:
                    keyval_ref[:, at - query_width : at - query_width + column] = value
            for t in range(outs):
                at = (q * outs + t) * column
                out_ref[:, at : at + column] = tile_ref[heads + t, q].astype(f32)
            gains = gains + tile_ref[count - 1, q].astype(f32)
        gain_ref[...] = gains

    return call(
        kernel,
        [
            shaped((rows, query_width), f32),
            shaped((rows, kv_width), f32),
            shaped((rows, squares * outs * column), f32),
            shaped((rows, column), f32),
        ],
        (tiles,),
        earlier,
    )


def per_device(
    tokens,
    cotangent,
    seq_lengths,
    seq_order,
    routes,
    gate_weights,
    attn_gain,
    w_query,
    key_value_weight,
    w_out,
    ffn_gain,
    w_gateup,
    w_down,
):
    wide_z = lax.axis_size("z")
    shards = lax.axis_size("y") * lax.axis_size("x") * lax.axis_size("c")
    core = lax.axis_index("c")
    shard = (lax.axis_index("y") * lax.axis_size("x") + lax.axis_index("x")) * 2 + core
    rows, width = tokens.shape
    experts = w_gateup.shape[0]
    kv_width = KEY_VALUE_HEADS * HEAD_SIZE
    owned = width // shards

    qkv_full = lax.all_gather(
        jnp.concatenate([w_query, key_value_weight], 1), SHARD, axis=0, tiled=True
    )
    part = width // wide_z
    rows_out, rows_up, rows_down = w_out.shape[0], w_gateup.shape[1], w_down.shape[1]
    column = lax.axis_index("z") * part
    gains_own = jnp.pad(jnp.stack([attn_gain, ffn_gain]), ((0, 14), (0, part - owned)))
    out_part = jnp.concatenate(
        [lax.dynamic_slice_in_dim(w_out, column, part, 1), gains_own], axis=0
    )
    expert_part = jnp.concatenate(
        [
            lax.dynamic_slice_in_dim(w_gateup, column, part, 2),
            lax.dynamic_slice_in_dim(w_down, column, part, 2),
        ],
        axis=1,
    )
    out_part = spread(out_part, experts, CHIPS)
    expert_part = exchange(hold((expert_part,), (out_part,))[0], CHIPS)
    gains_mine = out_part[:, rows_out : rows_out + 2, :owned]
    gains = in_core_order(core, gains_mine, lax.ppermute(gains_mine, "c", SWAP))
    gains = gains.transpose(2, 0, 1, 3).reshape(2, width).astype(f32)
    gain_attn, gain_ffn = gains[:1], gains[1:]
    out_mine = gather_over_z(out_part)
    out_other = [lax.ppermute(one, "c", SWAP) for one in out_mine]
    chosen = routes[:, :, None] == jnp.arange(experts, dtype=jnp.int32)
    member = jnp.any(chosen, axis=1)
    weight = jnp.sum(jnp.where(chosen, gate_weights[:, :, None], 0.0), axis=1)
    place = jnp.cumsum(member.astype(jnp.int32), axis=0) - 1
    slot = jnp.where(member, place, -1).T
    picks = slot[:, None, :] == jnp.arange(CAP, dtype=jnp.int32)[None, :, None]
    pick = picks.astype(bf16).reshape(experts * CAP, rows)
    slot_weight = jnp.sum(jnp.where(picks, weight.T[:, None, :], 0.0), axis=2)
    grad_out = matmul(pick, cotangent) * slot_weight.reshape(-1, 1)
    grad_out_sent = hold((grad_out.astype(bf16),), (expert_part,))[0]
    grad_out = exchange(grad_out_sent, CHIPS)


    lengths = seq_lengths[0]
    starts = jnp.cumsum(lengths) - lengths
    row_at = shard * rows + jnp.arange(rows, dtype=jnp.int32)
    first_at = jnp.max(jnp.where(starts[None, :] <= row_at[:, None], starts[None, :], 0), axis=1)
    cosine, sine = rotary_tables(row_at - first_at)
    first = (first_at - shard * rows).astype(jnp.int32)[:, None]
    normed, queries, keyval = project_qkv(
        tokens, gain_attn, qkv_full, cosine, sine, (*out_mine[1:], expert_part, grad_out_sent)
    )
    expert_parts = lax.all_gather(hold((expert_part,), (queries,))[0], ("z", "c"), axis=0)
    ring = [(i, (i + 1) % shards) for i in range(shards)]
    back_ring = [((i + 1) % shards, i) for i in range(shards)]
    before = lax.ppermute(keyval, SHARD, ring)
    attended_turned, residual, picked = attend(
        queries, before, keyval, first, out_mine, out_other, tokens, gain_ffn, pick, ()
    )

    picked = exchange(hold((picked,), (grad_out,))[0], CHIPS)
    normed, attended_turned = hold((normed, attended_turned), (picked,))
    normed_moved = lax.ppermute(normed, "x", SWAP)
    attended_moved = lax.ppermute(attended_turned, "x", SWAP)
    returned, acted, grad_pre = run_experts(picked, grad_out, expert_parts, rows_up, rows_down)
    returned = hold((returned,), (normed_moved, attended_moved))[0]
    expert_rows, pieces = expert_weight_grads(
        picked, grad_out, acted, grad_pre, expert_parts, rows_up, rows_down, (returned,)
    )
    normed_near = jnp.stack([normed, normed_moved])
    attended_near = jnp.stack([attended_turned, attended_moved])
    returned, expert_rows, pieces = hold((exchange(returned, CHIPS), expert_rows, pieces), ())
    normed_far = lax.ppermute(normed_near, "c", SWAP)
    attended_far = lax.ppermute(attended_near, "c", SWAP)
    pieces = pieces.reshape(2 * wide_z, *pieces.shape[2:])
    over_z = lax.psum_scatter(pieces, ("z", "c"), scatter_dimension=0, tiled=False)

    grad_residual, grad_branch, gain_grad = residual_grad(
        pick, returned, residual, gain_ffn, cotangent, (normed_far, attended_far)
    )
    expert_rows = exchange(expert_rows, CHIPS)
    across = lax.axis_index("x")
    branch_near = part_to_square(grad_branch, across, 1)
    grad_queries, grad_before, grad_own = attend_back(
        grad_branch,
        out_mine,
        out_other,
        queries,
        before,
        keyval,
        first,
        cosine,
        sine,
        (),
    )
    from_next = lax.ppermute(grad_before, SHARD, back_ring)
    grad_blocks = qkv_blocks_of(
        grad_queries, grad_own, from_next, cosine, sine, ()
    )

    blocks_near = part_to_square(grad_blocks, across, 0)
    doubled = twice(over_z, (expert_rows, blocks_near))
    qkv_grads = qkv_weight_grads(
        normed_near,
        normed_far,
        blocks_near,
        part_to_core(blocks_near, core, 1),
        lax.axis_size("y"),
        (doubled,),
    )
    over_rep = exchange(doubled, ("h", *CHIPS))
    out_terms = out_weight_grads(
        attended_near,
        attended_far,
        branch_near,
        part_to_core(branch_near, core, 2),
        lax.axis_size("y"),
        (doubled,),
    )
    out_grads = lax.psum_scatter(out_terms, "y", scatter_dimension=0, tiled=True)
    grad_tokens, tile = input_grad(
        grad_blocks, qkv_full, tokens, gain_attn, grad_residual, gain_grad, (qkv_grads,)
    )
    over_rep = sum_of_halves(over_rep, (tile,))
    gain_terms = moved_over_y(tile.reshape(lax.axis_size("y"), -1, HEAD_SIZE))
    qkv_grads = exchange(qkv_grads, "y")
    shard_gateup, shard_down = expert_outputs(
        lax.all_gather(over_rep, "z", axis=0), rows_up, rows_down
    )
    reps = 2 * wide_z
    tiles = exchange(tiles_of(qkv_grads, out_grads.reshape(-1, part), gain_terms, reps, 4), REP + ("x", "c"))
    tiles = exchange(sum_and_copy(tiles, 4, reps, ()), REP)
    grad_query, grad_keyval, grad_out_w, gain_sums = attention_outputs(
        tiles, width, 2 * kv_width, (shard_down,)
    )

    output = add_expert_rows(
        pick, slot_weight.reshape(-1, 1), expert_rows, residual, (qkv_grads,)
    )
    return (
        output,
        grad_tokens,
        gain_sums[:, 0],
        grad_query,
        grad_keyval,
        grad_out_w,
        gain_sums[:, 64],
        shard_gateup,
        shard_down,
    )


def solution(mesh):
    reps, shards = mesh.devices.shape
    fine = Mesh(mesh.devices.reshape(2, reps // 2, shards // 4, 2, 2), ALL)
    split = ALL
    placed = (
        P(split, None),
        P(split, None),
        P(REP, None),
        P(REP, None),
        P(split, None),
        P(split, None),
        P(SHARD),
        P(SHARD, None),
        P(SHARD, None),
        P(SHARD, None),
        P(SHARD),
        P(None, SHARD, None),
        P(None, SHARD, None),
    )
    return jax.shard_map(
        per_device,
        mesh=fine,
        in_specs=placed,
        out_specs=(
            P(split, None),
            P(split, None),
            P(SHARD),
            P(SHARD, None),
            P(SHARD, None),
            P(SHARD, None),
            P(SHARD),
            P(None, SHARD, None),
            P(None, SHARD, None),
        ),
        check_vma=False,
    )
```

```python
import jax
import jax.numpy as jnp
from jax import lax
from jax.experimental import pallas as pl
from jax.experimental.pallas import tpu as pltpu
from jax.sharding import Mesh, PartitionSpec as P

QUERY_HEADS = 12
KEY_VALUE_HEADS = 2
GROUP = QUERY_HEADS // KEY_VALUE_HEADS
HEAD_SIZE = 128
CAP = 80

EPSILON = 1e-06
ROPE_BASE = 10000.0
SCALE = HEAD_SIZE ** (-0.5)
SHARD = ("y", "x", "c")
CHIPS = ("y", "x")
REP = ("h", "z")
ALL = REP + SHARD
SWAP = [(0, 1), (1, 0)]

bf16 = jnp.bfloat16
f32 = jnp.float32

VMEM_LIMIT = 63 * 1024 * 1024
WHOLE = pl.BlockSpec(memory_space=pltpu.VMEM)
UNUSED = pl.BlockSpec(memory_space=pl.ANY)
SCALAR = pl.BlockSpec(memory_space=pltpu.SMEM)


def exchange(parts, axes):
    return lax.all_to_all(parts, axes, 0, 0, tiled=True)


def spread(part, ways, axes):
    return exchange(jnp.broadcast_to(part[None], (ways, *part.shape)), axes)


def matmul(left, right):
    return jnp.dot(left, right, preferred_element_type=f32)


def dot_general(left, right, dims):
    return lax.dot_general(left, right, (dims, ((), ())), preferred_element_type=f32)


def times_transposed(left, right):
    return dot_general(left, right, ((1,), (1,)))


def transposed_times(left, right):
    return dot_general(left, right, ((0,), (0,)))


def in_core_order(core, mine, other):
    return jnp.where(core == 0, jnp.stack([mine, other], 1), jnp.stack([other, mine], 1))


def call(kernel, out_shape, operands, earlier=(), specs=None, flops=0, scratch=()):
    specs = specs or [WHOLE] * len(operands)
    count = len(operands)

    def body(*refs):
        kernel(*refs[:count], *refs[count + len(earlier) :])

    size = sum(one.size * one.dtype.itemsize for one in (*operands, *out_shape))
    return pl.pallas_call(
        body,
        in_specs=[*specs, *([UNUSED] * len(earlier))],
        out_specs=[WHOLE] * len(out_shape),
        out_shape=out_shape,
        scratch_shapes=scratch,
        compiler_params=pltpu.CompilerParams(vmem_limit_bytes=VMEM_LIMIT),
        cost_estimate=pl.CostEstimate(flops=flops, bytes_accessed=size, transcendentals=0),
    )(*operands, *earlier)


def fetch(source_ref, to_ref, semaphores, along, base=0):
    rows, columns = to_ref.shape
    copies = []
    for i in range(to_ref.shape[along] // 512):
        chunk = pl.ds(i * 512, 512)
        if along:
            source = source_ref.at[:, pl.ds(base + i * 512, 512)]
            copy = pltpu.make_async_copy(source, to_ref.at[:, chunk], semaphores.at[i])
        else:
            source = source_ref.at[chunk, pl.ds(base, columns)]
            copy = pltpu.make_async_copy(source, to_ref.at[chunk, :], semaphores.at[i])
        copy.start()
        copies.append(copy)
    return copies


def fetch_parts(place_ref, mine_refs, other_refs, to_ref, semaphores):
    rows = to_ref.shape[2]
    part = to_ref.shape[3] // len(mine_refs)
    copies = []
    for k in range(len(mine_refs)):
        to = pl.ds(pl.multiple_of((place_ref[1] ^ k) * part, 128), part)
        owners = ((place_ref[0], mine_refs[k]), (1 - place_ref[0], other_refs[k]))
        for i, (owner, part_ref) in enumerate(owners):
            copy = pltpu.make_async_copy(
                part_ref.at[:, pl.ds(0, rows), :],
                to_ref.at[:, owner, :, to],
                semaphores.at[2 * k + i],
            )
            copy.start()
            copies.append(copy)
    return copies


def device_place():
    return jnp.stack([lax.axis_index("c"), lax.axis_index("z")]).astype(jnp.int32)


def shaped(shape, dtype):
    return jax.ShapeDtypeStruct(shape, dtype)


def inverse_rms(values):
    return lax.rsqrt(jnp.mean(values * values, axis=-1, keepdims=True) + EPSILON)


def norm_back(values, gain_row, upstream):
    factor = inverse_rms(values)
    grad_normed = upstream * gain_row
    grad_gain = upstream * values * factor
    cubed = factor * factor * factor
    grad_input = factor * grad_normed - values * cubed * jnp.mean(
        grad_normed * values, axis=-1, keepdims=True
    )
    return grad_input, grad_gain


def gain_tile(grad_gain, lower):
    rows = grad_gain.shape[0]
    lane = lax.broadcasted_iota(jnp.int32, (rows, 128), 1)
    return transposed_times(grad_gain, ((lane < 64) == lower).astype(f32))


def rotary_tables(position):
    half = HEAD_SIZE // 2
    frequency = ROPE_BASE ** (-jnp.arange(half, dtype=f32) / half)
    angle = position.astype(f32)[:, None] * frequency[None, :]
    cosine, sine = jnp.cos(angle), jnp.sin(angle)
    return jnp.concatenate([cosine, cosine], 1), jnp.concatenate([-sine, sine], 1)


def rotate(values, cosine, sine):
    return values * cosine + pltpu.roll(values, HEAD_SIZE // 2, 1) * sine


def project_qkv(tokens, gain, weights, cosine, sine, earlier):
    rows, width = tokens.shape
    kv_width = KEY_VALUE_HEADS * HEAD_SIZE
    turned = QUERY_HEADS + KEY_VALUE_HEADS
    total = width + 2 * kv_width

    def kernel(
        token_ref, gain_ref, all_ref, cos_ref, sin_ref, normed_ref, query_ref, keyval_ref, w_ref, sem
    ):
        copies = fetch(all_ref, w_ref, sem, 1)
        wide = token_ref[...].astype(f32)
        normed = (wide * inverse_rms(wide) * gain_ref[...]).astype(bf16)
        normed_ref[...] = normed
        cos, sin = cos_ref[...], sin_ref[...]
        for block in range(total // 256):
            if block % 2 == 0:
                copies[block // 2].wait()
            both = matmul(normed, w_ref[:, block * 256 : (block + 1) * 256])
            for i in range(2):
                head = 2 * block + i
                value = both[:, i * HEAD_SIZE : (i + 1) * HEAD_SIZE]
                if head < turned:
                    value = rotate(value, cos, sin)
                value = value.astype(bf16)
                if head < QUERY_HEADS:
                    query_ref[:, head * HEAD_SIZE : (head + 1) * HEAD_SIZE] = value
                else:
                    at = (head - QUERY_HEADS) * HEAD_SIZE
                    keyval_ref[:, at : at + HEAD_SIZE] = value

    return call(
        kernel,
        [
            shaped((rows, width), bf16),
            shaped((rows, width), bf16),
            shaped((rows, 2 * kv_width), bf16),
        ],
        (tokens, gain, weights, cosine, sine),
        earlier,
        specs=[WHOLE, WHOLE, UNUSED, WHOLE, WHOLE],
        flops=2 * rows * width * total,
        scratch=[pltpu.VMEM((width, total), bf16), pltpu.SemaphoreType.DMA((total // 512,))],
    )


def allowed_keys(first_ref, rows):
    row = lax.broadcasted_iota(jnp.int32, (rows, 2 * rows), 0)
    key = lax.broadcasted_iota(jnp.int32, (rows, 2 * rows), 1) - rows
    return (key <= row) & (key >= first_ref[...])


def probabilities(query, keys, allowed):
    scores = jnp.where(allowed, times_transposed(query, keys) * SCALE, -1000000000.0)
    exp_scores = jnp.exp(scores - jnp.max(scores, axis=-1, keepdims=True))
    return exp_scores / jnp.sum(exp_scores, axis=-1, keepdims=True)


def keys_and_values(before_ref, own_ref, group):
    both = []
    for base in (group * HEAD_SIZE, (KEY_VALUE_HEADS + group) * HEAD_SIZE):
        at = slice(base, base + HEAD_SIZE)
        both.append(jnp.concatenate([before_ref[:, at], own_ref[:, at]], axis=0))
    return both


def attend(queries, before, own, first, mine, other, tokens, gain, pick, earlier):
    rows, width = tokens.shape
    wide = len(mine)
    chips = mine[0].shape[0]

    def kernel(
        query_ref, before_ref, own_ref, first_ref, token_ref, gain_ref, pick_ref, place_ref, *refs
    ):
        turned_ref, residual_ref, picked_ref, attended_ref, w_ref, sem = refs[2 * wide :]
        copies = fetch_parts(place_ref, refs[:wide], refs[wide : 2 * wide], w_ref, sem)
        allowed = allowed_keys(first_ref, rows)
        for group in range(KEY_VALUE_HEADS):
            keys, values = keys_and_values(before_ref, own_ref, group)
            for head in range(group * GROUP, (group + 1) * GROUP):
                at = slice(head * HEAD_SIZE, (head + 1) * HEAD_SIZE)
                probs = probabilities(query_ref[:, at], keys, allowed)
                mixed = matmul(probs.astype(bf16), values)
                attended_ref[:, at] = mixed.astype(bf16)
                turned_ref[at, :] = mixed.T.astype(bf16)
        attended = attended_ref[...]
        for copy in copies:
            copy.wait()
        for block in range(width // 256):
            at = slice(block * 256, (block + 1) * 256)
            weights = w_ref[:, :, :, at].reshape(width, 256)
            branch = matmul(attended, weights).astype(bf16)
            residual_ref[:, at] = token_ref[:, at].astype(f32) + branch.astype(f32)
        residual = residual_ref[...]
        normed = (residual * inverse_rms(residual) * gain_ref[...]).astype(bf16)
        for block in range(width // 512):
            at = slice(block * 512, (block + 1) * 512)
            picked_ref[:, at] = matmul(pick_ref[...], normed[:, at]).astype(bf16)

    return call(
        kernel,
        [
            shaped((width, rows), bf16),
            shaped((rows, width), f32),
            shaped((pick.shape[0], width), bf16),
        ],
        (queries, before, own, first, tokens, gain, pick, device_place(), *mine, *other),
        earlier,
        specs=[*([WHOLE] * 7), SCALAR, *([UNUSED] * (2 * wide))],
        flops=2 * rows * width * width + 8 * rows * rows * width,
        scratch=[
            pltpu.VMEM((rows, width), bf16),
            pltpu.VMEM((chips, 2, width // (2 * chips), width), bf16),
            pltpu.SemaphoreType.DMA((2 * wide,)),
        ],
    )


def expert_copies(part_ref, to_ref, base, rows, semaphores):
    ways, part = part_ref.shape[0], part_ref.shape[3]
    return [
        pltpu.make_async_copy(
            part_ref.at[i, :, pl.ds(base, rows), :],
            to_ref.at[:, i % 2, :, pl.ds(i // 2 * part, part)],
            semaphores.at[i],
        )
        for i in range(ways)
    ]


def run_experts(picked, grad_out, parts, rows_up, rows_down):
    slots, width = picked.shape
    ways, chips, _, part = parts.shape
    ff = chips * 2 * rows_down
    each = slots // chips
    near = chips // 2

    def kernel(
        picked_any, grad_any, part_ref, back_any, acted_any, pre_any,
        picked_ref, grad_ref, up_w, down_w, gate_ref, upper_ref, acted_ref, pre_ref, back_ref,
        in_sem, up_sem, down_sem, out_sem,
    ):
        rows_in = pltpu.make_async_copy(picked_any, picked_ref, in_sem.at[0])
        grads_in = pltpu.make_async_copy(grad_any, grad_ref, in_sem.at[1])
        ups = expert_copies(part_ref, up_w, 0, rows_up, up_sem)
        downs = expert_copies(part_ref, down_w, rows_up, rows_down, down_sem)
        for copy in [rows_in, *ups, grads_in, *downs]:
            copy.start()
        for copy in [rows_in, *ups]:
            copy.wait()

        @pl.loop(0, ff // 256)
        def _(j):
            at = pl.multiple_of(j * 256, 256)
            for base, ref in ((0, gate_ref), (ff, upper_ref)):
                weights = up_w[:, :, :, pl.ds(base + at, 256)].reshape(width, 256)
                ref[:, pl.ds(at, 256)] = matmul(picked_ref[...], weights)

        for copy in [grads_in, *downs]:
            copy.wait()

        @pl.loop(0, 2)
        def _(j):
            at = pl.ds(pl.multiple_of(j * (ff // 2), 128), ff // 2)
            weights = down_w[pl.ds(j * near, near)].reshape(ff // 2, width)
            grad_act = times_transposed(grad_ref[...], weights)
            gate, up = gate_ref[:, at], upper_ref[:, at]
            sigmoid = 1.0 / (1.0 + jnp.exp(-gate))
            silu = gate * sigmoid
            acted_ref[:, at] = (silu * up).astype(bf16)
            grad_gate = grad_act * up * sigmoid * (1.0 + gate * (1.0 - sigmoid))
            pre_ref[:, at] = grad_gate.astype(bf16)
            upper = pl.ds(pl.multiple_of(ff + j * (ff // 2), 128), ff // 2)
            pre_ref[:, upper] = (grad_act * silu).astype(bf16)

        outs = [
            pltpu.make_async_copy(acted_ref, acted_any, out_sem.at[0]),
            pltpu.make_async_copy(pre_ref, pre_any, out_sem.at[1]),
        ]
        for copy in outs:
            copy.start()
        columns = width // 2
        for j in range(2):
            to = slice(j * columns, (j + 1) * columns)
            weights = up_w[j * near : (j + 1) * near].reshape(columns, 2 * ff)
            back = times_transposed(pre_ref[...], weights).astype(bf16)
            back_ref[:, :, to] = back.reshape(chips, each, columns)
            copy = pltpu.make_async_copy(
                back_ref.at[:, :, to], back_any.at[:, :, to], out_sem.at[2 + j]
            )
            copy.start()
            outs.append(copy)
        for copy in outs:
            copy.wait()

    back = shaped((chips, each, width), bf16)
    return pl.pallas_call(
        kernel,
        in_specs=[UNUSED] * 3,
        out_specs=[UNUSED] * 3,
        out_shape=[back, shaped((slots, ff), bf16), shaped((slots, 2 * ff), bf16)],
        scratch_shapes=[
            pltpu.VMEM((slots, width), bf16),
            pltpu.VMEM((slots, width), bf16),
            pltpu.VMEM((chips, 2, rows_up, width), bf16),
            pltpu.VMEM((chips, 2, rows_down, width), bf16),
            pltpu.VMEM((slots, ff), f32),
            pltpu.VMEM((slots, ff), f32),
            pltpu.VMEM((slots, ff), bf16),
            pltpu.VMEM((slots, 2 * ff), bf16),
            pltpu.VMEM(back.shape, bf16),
            pltpu.SemaphoreType.DMA((2,)),
            pltpu.SemaphoreType.DMA((ways,)),
            pltpu.SemaphoreType.DMA((ways,)),
            pltpu.SemaphoreType.DMA((4,)),
        ],
        compiler_params=pltpu.CompilerParams(vmem_limit_bytes=VMEM_LIMIT),
        cost_estimate=pl.CostEstimate(
            flops=2 * slots * 5 * width * ff,
            bytes_accessed=12 * slots * width + 2 * width * 3 * ff,
            transcendentals=0,
        ),
    )(picked, grad_out, parts)


def expert_weight_grads(picked, grad_out, acted, grad_pre, parts, rows_up, rows_down, earlier):
    slots, width = picked.shape
    ways, chips, _, part = parts.shape
    wide = ways // 2
    ff = acted.shape[1]
    each = slots // chips
    half = (rows_up + rows_down) // 2
    near = chips // 2
    columns = width // 2

    def kernel(picked_any, grad_any, acted_any, pre_any, part_ref, *refs):
        expert_any, piece_any = refs[len(earlier) : len(earlier) + 2]
        (
            picked_ref, grad_ref, acted_ref, pre_ref, down_w, expert_ref, keep_ref, piece_ref,
            in_sem, down_sem, out_sem,
        ) = refs[len(earlier) + 2 :]
        ins = [
            pltpu.make_async_copy(source, to, in_sem.at[i])
            for i, (source, to) in enumerate(
                (
                    (picked_any, picked_ref),
                    (pre_any, pre_ref),
                    (acted_any, acted_ref),
                    (grad_any, grad_ref),
                )
            )
        ]
        downs = expert_copies(part_ref, down_w, rows_up, rows_down, down_sem)
        for copy in ins + downs:
            copy.start()
        for copy in ins:
            copy.wait()

        @pl.loop(0, 2)
        def _(s):
            for n in range(2):
                at = slice(n * columns, (n + 1) * columns)
                for m in range(near // 2):
                    base = pl.multiple_of(s * near * 2 * rows_up + m * 4 * rows_up, 128)
                    block = picked_ref[:, pl.ds(base, 4 * rows_up)]
                    up = transposed_times(block, pre_ref[:, at])
                    for i in range(4):
                        rows = up[i * rows_up : (i + 1) * rows_up]
                        k, c = 2 * m + i // 2, i % 2
                        keep_ref[k, c] = rows[half:]
                        low = rows[:half].astype(bf16)
                        for j in range(columns // part):
                            z = n * (columns // part) + j
                            piece_ref[z, c, s * near + k, 0] = low[:, j * part : (j + 1) * part]
                base = pl.multiple_of(s * near * 2 * rows_down, 128)
                block = acted_ref[:, pl.ds(base, near * 2 * rows_down)]
                down = transposed_times(block, grad_ref[:, at])
                for k in range(near):
                    for c in range(2):
                        low = (2 * k + c) * rows_down
                        rest = jnp.concatenate([keep_ref[k, c], down[low : low + rows_down]], axis=0)
                        rest = rest.astype(bf16)
                        for j in range(columns // part):
                            z = n * (columns // part) + j
                            piece_ref[z, c, s * near + k, 1] = rest[:, j * part : (j + 1) * part]
            chip = pl.ds(s * near, near)
            pltpu.make_async_copy(
                piece_ref.at[:, :, chip], piece_any.at[:, :, chip], out_sem.at[s]
            ).start()

        for copy in downs:
            copy.wait()
        for j in range(2):
            to = slice(j * columns, (j + 1) * columns)
            weights = down_w[:, :, :, to].reshape(ff, columns)
            forward = matmul(acted_ref[...], weights).astype(bf16)
            expert_ref[:, :, to] = forward.reshape(chips, each, columns)
        expert_out = pltpu.make_async_copy(expert_ref, expert_any, out_sem.at[2])
        expert_out.start()
        for s in range(2):
            chip = pl.ds(s * near, near)
            pltpu.make_async_copy(
                piece_ref.at[:, :, chip], piece_any.at[:, :, chip], out_sem.at[s]
            ).wait()
        expert_out.wait()

    expert = shaped((chips, each, width), bf16)
    pieces = shaped((wide, 2, chips, 2, half, part), bf16)
    return pl.pallas_call(
        kernel,
        in_specs=[UNUSED] * (5 + len(earlier)),
        out_specs=[UNUSED] * 2,
        out_shape=[expert, pieces],
        scratch_shapes=[
            pltpu.VMEM((slots, width), bf16),
            pltpu.VMEM((slots, width), bf16),
            pltpu.VMEM((slots, ff), bf16),
            pltpu.VMEM((slots, 2 * ff), bf16),
            pltpu.VMEM((chips, 2, rows_down, width), bf16),
            pltpu.VMEM(expert.shape, bf16),
            pltpu.VMEM((near, 2, rows_up - half, columns), f32),
            pltpu.VMEM(pieces.shape, bf16),
            pltpu.SemaphoreType.DMA((4,)),
            pltpu.SemaphoreType.DMA((ways,)),
            pltpu.SemaphoreType.DMA((3,)),
        ],
        compiler_params=pltpu.CompilerParams(vmem_limit_bytes=VMEM_LIMIT),
        cost_estimate=pl.CostEstimate(
            flops=2 * slots * 4 * width * ff,
            bytes_accessed=10 * slots * width + 8 * width * 3 * ff,
            transcendentals=0,
        ),
    )(picked, grad_out, acted, grad_pre, parts, *earlier)


def residual_grad(pick, returned, residual, gain, cotangent, earlier):
    rows, width = residual.shape
    slots = pick.shape[0]

    def kernel(
        pick_ref, back_any, residual_ref, gain_ref, cot_ref, grad_ref, branch_ref, product_ref,
        back_ref, sem,
    ):
        blocks = [slice(i * 512, (i + 1) * 512) for i in range(width // 512)]
        copies = [
            pltpu.make_async_copy(back_any.at[:, :, at], back_ref.at[:, :, at], sem.at[i])
            for i, at in enumerate(blocks)
        ]
        for copy in copies:
            copy.start()
        for copy, at in zip(copies, blocks):
            copy.wait()
            back = back_ref[:, :, at].reshape(slots, 512)
            grad_ref[:, at] = transposed_times(pick_ref[...], back)
        grad, products = norm_back(residual_ref[...], gain_ref[...], grad_ref[...])
        grad = grad + cot_ref[...].astype(f32)
        grad_ref[...] = grad
        branch_ref[...] = grad.astype(bf16)
        product_ref[...] = products.astype(bf16)

    return call(
        kernel,
        [shaped((rows, width), f32), shaped((rows, width), bf16), shaped((rows, width), bf16)],
        (pick, returned, residual, gain, cotangent),
        earlier,
        specs=[WHOLE, UNUSED, WHOLE, WHOLE, WHOLE],
        flops=2 * slots * width * rows,
        scratch=[
            pltpu.VMEM(returned.shape, bf16),
            pltpu.SemaphoreType.DMA((width // 512,)),
        ],
    )


def add_expert_rows(pick, weight, returned, residual, earlier):
    rows, width = residual.shape
    slots = pick.shape[0]

    def kernel(pick_ref, weight_ref, back_ref, residual_ref, out_ref):
        back = jnp.where(pick_ref[...] > 0, weight_ref[...], 0.0)
        high = back.astype(bf16)
        low = (back - high.astype(f32)).astype(bf16)
        for block in range(width // 512):
            at = slice(block * 512, (block + 1) * 512)
            expert = back_ref[:, :, at].reshape(slots, 512)
            mixture = transposed_times(high, expert) + transposed_times(low, expert)
            out_ref[:, at] = (residual_ref[:, at] + mixture).astype(bf16)

    return call(
        kernel,
        [shaped((rows, width), bf16)],
        (pick, weight, returned, residual),
        earlier,
        flops=4 * slots * width * rows,
    )[0]


def attend_back(grad_branch, mine, other, queries, before, own, first, cosine, sine, earlier):
    rows, width = grad_branch.shape
    kv_width = KEY_VALUE_HEADS * HEAD_SIZE
    wide = len(mine)
    chips = mine[0].shape[0]

    def kernel(
        grad_ref, query_ref, before_ref, own_ref, first_ref, cos_ref, sin_ref, place_ref, *refs
    ):
        out_ref, prev_ref, self_ref, attended_ref, prob_ref, w_ref, sem = refs[2 * wide :]
        copies = fetch_parts(place_ref, refs[:wide], refs[wide : 2 * wide], w_ref, sem)
        allowed = allowed_keys(first_ref, rows)
        for head in range(QUERY_HEADS):
            at = slice(head * HEAD_SIZE, (head + 1) * HEAD_SIZE)
            keys, _ = keys_and_values(before_ref, own_ref, head // GROUP)
            prob_ref[head] = probabilities(query_ref[:, at], keys, allowed)
        for copy in copies:
            copy.wait()
        for half in range(2):
            at = slice(half * (width // 2), (half + 1) * (width // 2))
            weights = w_ref[half * (chips // 2) : (half + 1) * (chips // 2)]
            weights = weights.reshape(width // 2, width)
            attended_ref[:, at] = times_transposed(grad_ref[...], weights).astype(bf16)
        cos, sin = cos_ref[...], sin_ref[...]
        for group in range(KEY_VALUE_HEADS):
            keys, values = keys_and_values(before_ref, own_ref, group)
            raws, lows, uppers, asked = [], [], [], []
            for head in range(group * GROUP, (group + 1) * GROUP):
                at = slice(head * HEAD_SIZE, (head + 1) * HEAD_SIZE)
                query, upper = query_ref[:, at], attended_ref[:, at]
                probs = prob_ref[head]
                grad_probs = times_transposed(upper, values)
                inner = jnp.sum(probs * grad_probs, axis=-1, keepdims=True)
                raw = (probs * (grad_probs - inner) * SCALE).astype(bf16)
                out_ref[head] = rotate(matmul(raw, keys), cos, -sin).astype(bf16)
                raws.append(raw)
                lows.append(probs.astype(bf16))
                uppers.append(upper)
                asked.append(query)
            for base, lefts, rights in (
                (group * HEAD_SIZE, raws, asked),
                (kv_width + group * HEAD_SIZE, lows, uppers),
            ):
                grad = transposed_times(
                    jnp.concatenate(lefts, axis=0), jnp.concatenate(rights, axis=0)
                )
                prev_ref[:, base : base + HEAD_SIZE] = grad[:rows].astype(bf16)
                self_ref[:, base : base + HEAD_SIZE] = grad[rows:]

    return call(
        kernel,
        [
            shaped((QUERY_HEADS, rows, HEAD_SIZE), bf16),
            shaped((rows, 2 * kv_width), bf16),
            shaped((rows, 2 * kv_width), f32),
        ],
        (grad_branch, queries, before, own, first, cosine, sine, device_place(), *mine, *other),
        earlier,
        specs=[*([WHOLE] * 7), SCALAR, *([UNUSED] * (2 * wide))],
        flops=2 * rows * width * width + 20 * rows * rows * width,
        scratch=[
            pltpu.VMEM((rows, width), bf16),
            pltpu.VMEM((QUERY_HEADS, rows, 2 * rows), f32),
            pltpu.VMEM((chips, 2, width // (2 * chips), width), bf16),
            pltpu.SemaphoreType.DMA((2 * wide,)),
        ],
    )


def qkv_blocks_of(grad_queries, grad_own, from_next, cosine, sine, earlier):
    heads, rows, size = grad_queries.shape
    total = heads + 2 * KEY_VALUE_HEADS

    def kernel(query_ref, own_ref, next_ref, cos_ref, sin_ref, out_ref):
        out_ref[:heads] = query_ref[...]
        for i in range(2 * KEY_VALUE_HEADS):
            at = slice(i * size, (i + 1) * size)
            grad = own_ref[:, at] + next_ref[:, at].astype(f32)
            if i < KEY_VALUE_HEADS:
                grad = rotate(grad, cos_ref[...], -sin_ref[...])
            out_ref[heads + i] = grad.astype(bf16)

    return call(
        kernel,
        [shaped((total, rows, size), bf16)],
        (grad_queries, grad_own, from_next, cosine, sine),
        earlier,
    )[0]


def input_grad(blocks, weights, tokens, gain, grad_residual, gain_grad, earlier):
    rows, width = tokens.shape
    columns = blocks.shape[0] * HEAD_SIZE

    def kernel(
        block_ref, all_ref, token_ref, gain_ref, residual_ref, other_ref, out_ref, tile_ref, w_ref, sem
    ):
        copies = fetch(all_ref, w_ref, sem, 1)
        total = jnp.zeros((rows, width), f32)
        for i in range(blocks.shape[0] // 2):
            if i % 2 == 0:
                copies[i // 2].wait()
            pair = jnp.concatenate([block_ref[2 * i], block_ref[2 * i + 1]], axis=1)
            total = total + times_transposed(pair, w_ref[:, i * 256 : (i + 1) * 256])
        grad, grad_gain = norm_back(token_ref[...].astype(f32), gain_ref[...], total)
        out_ref[...] = (residual_ref[...] + grad).astype(bf16)
        other = gain_tile(other_ref[...].astype(f32), False)
        tile_ref[...] = (other + gain_tile(grad_gain, True)).astype(bf16)

    return call(
        kernel,
        [shaped((rows, width), bf16), shaped((width, 128), bf16)],
        (blocks, weights, tokens, gain, grad_residual, gain_grad),
        earlier,
        specs=[WHOLE, UNUSED, WHOLE, WHOLE, WHOLE, WHOLE],
        flops=2 * rows * width * columns,
        scratch=[pltpu.VMEM((width, columns), bf16), pltpu.SemaphoreType.DMA((columns // 512,))],
    )


def gather_over_z(part):
    wide = lax.axis_size("z")
    return [part] + [
        lax.ppermute(part, "z", [(i, i ^ k) for i in range(wide)]) for k in range(1, wide)
    ]


def expert_outputs(pieces, rows_up, rows_down):
    wide, experts, _, half, part = pieces.shape
    width = wide * part
    split = rows_up - half

    def kernel(piece_ref, up_ref, down_ref):
        for z in range(wide):
            at = slice(z * part, (z + 1) * part)
            rest = piece_ref[z, 0, 1].astype(f32)
            up_ref[0, :half, at] = piece_ref[z, 0, 0].astype(f32)
            up_ref[0, half:, at] = rest[:split]
            down_ref[0, :, at] = rest[split:]

    return pl.pallas_call(
        kernel,
        grid=(experts,),
        in_specs=[pl.BlockSpec((wide, 1, 2, half, part), lambda e: (0, e, 0, 0, 0))],
        out_specs=[
            pl.BlockSpec((1, rows_up, width), lambda e: (e, 0, 0)),
            pl.BlockSpec((1, rows_down, width), lambda e: (e, 0, 0)),
        ],
        out_shape=[
            shaped((experts, rows_up, width), f32),
            shaped((experts, rows_down, width), f32),
        ],
    )(pieces)


def part_to_square(value, across, axis):
    size = value.shape[axis] // 2
    mine = lax.dynamic_slice_in_dim(value, across * size, size, axis)
    sent = lax.dynamic_slice_in_dim(value, (1 - across) * size, size, axis)
    return jnp.stack([mine, lax.ppermute(sent, "x", SWAP)])


def part_to_core(value, core, axis):
    size = value.shape[axis] // 2
    return lax.ppermute(lax.dynamic_slice_in_dim(value, (1 - core) * size, size, axis), "c", SWAP)


def twice(value, earlier):
    size = value.shape[0]
    near = size // 2

    def kernel(in_any, *refs):
        out_any, value_ref, in_sem, out_sem = refs[len(earlier) :]
        blocks = [pl.ds(i * near, near) for i in range(2)]
        ins = [
            pltpu.make_async_copy(in_any.at[at], value_ref.at[at], in_sem.at[i])
            for i, at in enumerate(blocks)
        ]
        for copy in ins:
            copy.start()
        outs = []
        for i, at in enumerate(blocks):
            ins[i].wait()
            for j in range(2):
                to = pl.ds(j * size + i * near, near)
                copy = pltpu.make_async_copy(value_ref.at[at], out_any.at[to], out_sem.at[2 * i + j])
                copy.start()
                outs.append(copy)
        for copy in outs:
            copy.wait()

    return pl.pallas_call(
        kernel,
        in_specs=[UNUSED] * (1 + len(earlier)),
        out_specs=UNUSED,
        out_shape=shaped((2 * size, *value.shape[1:]), value.dtype),
        scratch_shapes=[
            pltpu.VMEM(value.shape, value.dtype),
            pltpu.SemaphoreType.DMA((2,)),
            pltpu.SemaphoreType.DMA((4,)),
        ],
        compiler_params=pltpu.CompilerParams(vmem_limit_bytes=VMEM_LIMIT),
    )(value, *earlier)


def sum_of_halves(value, earlier):
    size = value.shape[0] // 2
    out = shaped((size, *value.shape[1:]), value.dtype)

    def kernel(in_any, *refs):
        out_any, in_ref, out_ref, in_sem, out_sem = refs[len(earlier) :]
        near = size // 2
        copies = [
            pltpu.make_async_copy(
                in_any.at[pl.ds(i * near, near)], in_ref.at[pl.ds(i * near, near)], in_sem.at[i]
            )
            for i in range(4)
        ]
        for i in (0, 2, 1, 3):
            copies[i].start()
        outs = []
        for i in range(2):
            copies[i].wait()
            copies[2 + i].wait()
            at = slice(i * near, (i + 1) * near)
            low = in_ref[at].astype(f32)
            out_ref[at] = (low + in_ref[size + i * near : size + (i + 1) * near].astype(f32)).astype(bf16)
            block = pl.ds(i * near, near)
            copy = pltpu.make_async_copy(out_ref.at[block], out_any.at[block], out_sem.at[i])
            copy.start()
            outs.append(copy)
        for copy in outs:
            copy.wait()

    return pl.pallas_call(
        kernel,
        in_specs=[UNUSED] * (1 + len(earlier)),
        out_specs=UNUSED,
        out_shape=out,
        scratch_shapes=[
            pltpu.VMEM(value.shape, value.dtype),
            pltpu.VMEM(out.shape, value.dtype),
            pltpu.SemaphoreType.DMA((4,)),
            pltpu.SemaphoreType.DMA((2,)),
        ],
        compiler_params=pltpu.CompilerParams(vmem_limit_bytes=VMEM_LIMIT),
    )(value, *earlier)


def hold(values, earlier):
    def kernel(*refs):
        del refs

    return pl.pallas_call(
        kernel,
        in_specs=[UNUSED] * (len(values) + len(earlier)),
        out_specs=[UNUSED] * len(values),
        out_shape=[shaped(one.shape, one.dtype) for one in values],
        input_output_aliases={i: i for i in range(len(values))},
    )(*values, *earlier)


def out_weight_grads(near, far, grad_near, grad_far, ways, earlier):
    _, width, rows = near.shape
    columns = grad_far.shape[2]
    core = lax.axis_index("c").astype(jnp.int32).reshape(1)

    def kernel(core_ref, near_ref, far_ref, grad_near_ref, grad_far_ref, out_ref, left_ref):
        at = pl.ds(pl.multiple_of(core_ref[0] * columns, 128), columns)
        for i in range(2):
            left_ref[:, i * rows : (i + 1) * rows] = near_ref[i]
            left_ref[:, (2 + i) * rows : (3 + i) * rows] = far_ref[i]
        right = jnp.concatenate(
            [grad_near_ref[0, :, at], grad_near_ref[1, :, at], grad_far_ref[0], grad_far_ref[1]],
            axis=0,
        )
        each = width // ways
        for i in range(ways):
            left = left_ref[i * each : (i + 1) * each, :]
            out_ref[i] = matmul(left, right).astype(bf16)

    return call(
        kernel,
        [shaped((ways, width // ways, columns), bf16)],
        (core, near, far, grad_near, grad_far),
        earlier,
        specs=[SCALAR, *([WHOLE] * 4)],
        flops=8 * width * rows * columns,
        scratch=[pltpu.VMEM((width, 4 * rows), bf16)],
    )[0]


def qkv_weight_grads(near, far, grad_near, grad_far, ways, earlier):
    _, rows, width = near.shape
    heads = grad_far.shape[1]
    columns = heads * HEAD_SIZE
    core = lax.axis_index("c").astype(jnp.int32).reshape(1)

    def kernel(core_ref, near_ref, far_ref, grad_near_ref, grad_far_ref, out_ref, left_ref, right_ref):
        for i in range(2):
            left_ref[i * rows : (i + 1) * rows, :] = near_ref[i]
            left_ref[(2 + i) * rows : (3 + i) * rows, :] = far_ref[i]
            for head in range(heads):
                at = slice(head * HEAD_SIZE, (head + 1) * HEAD_SIZE)
                mine = grad_near_ref[i, core_ref[0] * heads + head]
                right_ref[i * rows : (i + 1) * rows, at] = mine
                right_ref[(2 + i) * rows : (3 + i) * rows, at] = grad_far_ref[i, head]
        each = width // ways
        for i in range(ways):
            block = slice(i * each, (i + 1) * each)
            out_ref[i] = transposed_times(left_ref[:, block], right_ref[...]).astype(bf16)

    return call(
        kernel,
        [shaped((ways, width // ways, columns), bf16)],
        (core, near, far, grad_near, grad_far),
        earlier,
        specs=[SCALAR, *([WHOLE] * 4)],
        flops=8 * width * rows * columns,
        scratch=[pltpu.VMEM((4 * rows, width), bf16), pltpu.VMEM((4 * rows, columns), bf16)],
    )[0]


def moved_over_y(blocks):
    wide = lax.axis_size("y")
    y = lax.axis_index("y")
    moved = [lax.dynamic_index_in_dim(blocks, y, 0, keepdims=False)]
    for k in range(1, wide):
        sent = lax.dynamic_index_in_dim(blocks, y ^ k, 0, keepdims=False)
        moved.append(lax.ppermute(sent, "y", [(i, i ^ k) for i in range(wide)]))
    return moved


def tiles_of(qkv, out, gains, tiles, squares):
    terms = qkv.shape[0]
    rows = qkv.shape[1] // squares
    count = qkv.shape[2] // HEAD_SIZE

    def kernel(qkv_ref, out_ref, *refs):
        gain_refs, tile_ref = refs[:-1], refs[-1]
        for t in range(tiles):
            for p in range(squares):
                block = slice(p * rows, (p + 1) * rows)
                if t < count:
                    at = slice(t * HEAD_SIZE, (t + 1) * HEAD_SIZE)
                    values = [qkv_ref[i, block, at] for i in range(terms)]
                elif t < tiles - 1:
                    at = slice((t - count) * HEAD_SIZE, (t - count + 1) * HEAD_SIZE)
                    values = [out_ref[block, at]]
                else:
                    values = [ref[block] for ref in gain_refs]
                total = values[0].astype(f32)
                for value in values[1:]:
                    total = total + value.astype(f32)
                tile_ref[t * squares + p] = total.astype(bf16)

    return call(
        kernel, [shaped((tiles * squares, rows, HEAD_SIZE), bf16)], (qkv, out, *gains)
    )[0]


def sum_and_copy(parts, squares, copies, earlier):
    count, rows, columns = parts.shape

    def kernel(part_ref, copy_ref):
        for p in range(squares):
            total = part_ref[p].astype(f32)
            for i in range(1, count // squares):
                total = total + part_ref[i * squares + p].astype(f32)
            low = total.astype(bf16)
            for i in range(copies):
                copy_ref[i, p] = low

    return call(kernel, [shaped((copies, squares, rows, columns), bf16)], (parts,), earlier)[0]


def attention_outputs(tiles, query_width, kv_width, earlier):
    count, squares, rows, column = tiles.shape
    heads = (query_width + kv_width) // column // squares
    outs = count - 1 - heads

    def kernel(tile_ref, query_ref, keyval_ref, out_ref, gain_ref):
        gains = jnp.zeros((rows, column), f32)
        for q in range(squares):
            for t in range(heads):
                at = (q * heads + t) * column
                value = tile_ref[t, q].astype(f32)
                if at < query_width:
                    query_ref[:, at : at + column] = value
                else:
                    keyval_ref[:, at - query_width : at - query_width + column] = value
            for t in range(outs):
                at = (q * outs + t) * column
                out_ref[:, at : at + column] = tile_ref[heads + t, q].astype(f32)
            gains = gains + tile_ref[count - 1, q].astype(f32)
        gain_ref[...] = gains

    return call(
        kernel,
        [
            shaped((rows, query_width), f32),
            shaped((rows, kv_width), f32),
            shaped((rows, squares * outs * column), f32),
            shaped((rows, column), f32),
        ],
        (tiles,),
        earlier,
    )


def per_device(
    tokens,
    cotangent,
    seq_lengths,
    seq_order,
    routes,
    gate_weights,
    attn_gain,
    w_query,
    key_value_weight,
    w_out,
    ffn_gain,
    w_gateup,
    w_down,
):
    wide_z = lax.axis_size("z")
    shards = lax.axis_size("y") * lax.axis_size("x") * lax.axis_size("c")
    core = lax.axis_index("c")
    shard = (lax.axis_index("y") * lax.axis_size("x") + lax.axis_index("x")) * 2 + core
    rows, width = tokens.shape
    experts = w_gateup.shape[0]
    kv_width = KEY_VALUE_HEADS * HEAD_SIZE
    owned = width // shards

    qkv_full = lax.all_gather(
        jnp.concatenate([w_query, key_value_weight], 1), SHARD, axis=0, tiled=True
    )
    part = width // wide_z
    rows_out, rows_up, rows_down = w_out.shape[0], w_gateup.shape[1], w_down.shape[1]
    column = lax.axis_index("z") * part
    gains_own = jnp.pad(jnp.stack([attn_gain, ffn_gain]), ((0, 14), (0, part - owned)))
    out_part = jnp.concatenate(
        [lax.dynamic_slice_in_dim(w_out, column, part, 1), gains_own], axis=0
    )
    expert_part = jnp.concatenate(
        [
            lax.dynamic_slice_in_dim(w_gateup, column, part, 2),
            lax.dynamic_slice_in_dim(w_down, column, part, 2),
        ],
        axis=1,
    )
    out_part = spread(out_part, experts, CHIPS)
    expert_part = exchange(hold((expert_part,), (out_part,))[0], CHIPS)
    gains_mine = out_part[:, rows_out : rows_out + 2, :owned]
    gains = in_core_order(core, gains_mine, lax.ppermute(gains_mine, "c", SWAP))
    gains = gains.transpose(2, 0, 1, 3).reshape(2, width).astype(f32)
    gain_attn, gain_ffn = gains[:1], gains[1:]
    out_mine = gather_over_z(out_part[:, :rows_out])
    out_other = [lax.ppermute(one, "c", SWAP) for one in out_mine]
    chosen = routes[:, :, None] == jnp.arange(experts, dtype=jnp.int32)
    member = jnp.any(chosen, axis=1)
    weight = jnp.sum(jnp.where(chosen, gate_weights[:, :, None], 0.0), axis=1)
    place = jnp.cumsum(member.astype(jnp.int32), axis=0) - 1
    slot = jnp.where(member, place, -1).T
    picks = slot[:, None, :] == jnp.arange(CAP, dtype=jnp.int32)[None, :, None]
    pick = picks.astype(bf16).reshape(experts * CAP, rows)
    slot_weight = jnp.sum(jnp.where(picks, weight.T[:, None, :], 0.0), axis=2)
    grad_out = matmul(pick, cotangent) * slot_weight.reshape(-1, 1)
    grad_out_sent = hold((grad_out.astype(bf16),), (expert_part,))[0]
    grad_out = exchange(grad_out_sent, CHIPS)


    lengths = seq_lengths[0]
    starts = jnp.cumsum(lengths) - lengths
    row_at = shard * rows + jnp.arange(rows, dtype=jnp.int32)
    first_at = jnp.max(jnp.where(starts[None, :] <= row_at[:, None], starts[None, :], 0), axis=1)
    cosine, sine = rotary_tables(row_at - first_at)
    first = (first_at - shard * rows).astype(jnp.int32)[:, None]
    normed, queries, keyval = project_qkv(
        tokens, gain_attn, qkv_full, cosine, sine, (*out_mine[1:], expert_part, grad_out_sent)
    )
    expert_parts = lax.all_gather(hold((expert_part,), (queries,))[0], ("z", "c"), axis=0)
    ring = [(i, (i + 1) % shards) for i in range(shards)]
    back_ring = [((i + 1) % shards, i) for i in range(shards)]
    before = lax.ppermute(keyval, SHARD, ring)
    attended_turned, residual, picked = attend(
        queries, before, keyval, first, out_mine, out_other, tokens, gain_ffn, pick, ()
    )

    picked = exchange(hold((picked,), (grad_out,))[0], CHIPS)
    normed, attended_turned = hold((normed, attended_turned), (picked,))
    normed_moved = lax.ppermute(normed, "x", SWAP)
    attended_moved = lax.ppermute(attended_turned, "x", SWAP)
    returned, acted, grad_pre = run_experts(picked, grad_out, expert_parts, rows_up, rows_down)
    returned = hold((returned,), (normed_moved, attended_moved))[0]
    expert_rows, pieces = expert_weight_grads(
        picked, grad_out, acted, grad_pre, expert_parts, rows_up, rows_down, (returned,)
    )
    normed_near = jnp.stack([normed, normed_moved])
    attended_near = jnp.stack([attended_turned, attended_moved])
    returned, expert_rows, pieces = hold((exchange(returned, CHIPS), expert_rows, pieces), ())
    normed_far = lax.ppermute(normed_near, "c", SWAP)
    attended_far = lax.ppermute(attended_near, "c", SWAP)
    pieces = pieces.reshape(2 * wide_z, *pieces.shape[2:])
    over_z = lax.psum_scatter(pieces, ("z", "c"), scatter_dimension=0, tiled=False)

    grad_residual, grad_branch, gain_grad = residual_grad(
        pick, returned, residual, gain_ffn, cotangent, (normed_far, attended_far)
    )
    expert_rows = exchange(expert_rows, CHIPS)
    across = lax.axis_index("x")
    branch_near = part_to_square(grad_branch, across, 1)
    grad_queries, grad_before, grad_own = attend_back(
        grad_branch,
        out_mine,
        out_other,
        queries,
        before,
        keyval,
        first,
        cosine,
        sine,
        (),
    )
    from_next = lax.ppermute(grad_before, SHARD, back_ring)
    grad_blocks = qkv_blocks_of(
        grad_queries, grad_own, from_next, cosine, sine, ()
    )

    blocks_near = part_to_square(grad_blocks, across, 0)
    doubled = twice(over_z, (expert_rows, blocks_near))
    qkv_grads = qkv_weight_grads(
        normed_near,
        normed_far,
        blocks_near,
        part_to_core(blocks_near, core, 1),
        lax.axis_size("y"),
        (doubled,),
    )
    over_rep = exchange(doubled, ("h", *CHIPS))
    out_terms = out_weight_grads(
        attended_near,
        attended_far,
        branch_near,
        part_to_core(branch_near, core, 2),
        lax.axis_size("y"),
        (doubled,),
    )
    out_grads = lax.psum_scatter(out_terms, "y", scatter_dimension=0, tiled=True)
    grad_tokens, tile = input_grad(
        grad_blocks, qkv_full, tokens, gain_attn, grad_residual, gain_grad, (qkv_grads,)
    )
    over_rep = sum_of_halves(over_rep, (tile,))
    gain_terms = moved_over_y(tile.reshape(lax.axis_size("y"), -1, HEAD_SIZE))
    qkv_grads = exchange(qkv_grads, "y")
    shard_gateup, shard_down = expert_outputs(
        lax.all_gather(over_rep, "z", axis=0), rows_up, rows_down
    )
    reps = 2 * wide_z
    tiles = exchange(tiles_of(qkv_grads, out_grads.reshape(-1, part), gain_terms, reps, 4), REP + ("x", "c"))
    tiles = exchange(sum_and_copy(tiles, 4, reps, ()), REP)
    grad_query, grad_keyval, grad_out_w, gain_sums = attention_outputs(
        tiles, width, 2 * kv_width, (shard_down,)
    )

    output = add_expert_rows(
        pick, slot_weight.reshape(-1, 1), expert_rows, residual, (qkv_grads,)
    )
    return (
        output,
        grad_tokens,
        gain_sums[:, 0],
        grad_query,
        grad_keyval,
        grad_out_w,
        gain_sums[:, 64],
        shard_gateup,
        shard_down,
    )


def solution(mesh):
    reps, shards = mesh.devices.shape
    fine = Mesh(mesh.devices.reshape(2, reps // 2, shards // 4, 2, 2), ALL)
    split = ALL
    placed = (
        P(split, None),
        P(split, None),
        P(REP, None),
        P(REP, None),
        P(split, None),
        P(split, None),
        P(SHARD),
        P(SHARD, None),
        P(SHARD, None),
        P(SHARD, None),
        P(SHARD),
        P(None, SHARD, None),
        P(None, SHARD, None),
    )
    return jax.shard_map(
        per_device,
        mesh=fine,
        in_specs=placed,
        out_specs=(
            P(split, None),
            P(split, None),
            P(SHARD),
            P(SHARD, None),
            P(SHARD, None),
            P(SHARD, None),
            P(SHARD),
            P(None, SHARD, None),
            P(None, SHARD, None),
        ),
        check_vma=False,
    )
```
